32 devices in a mesh: seq: 16 (over z, y, core), img: 2 (over x).
Axes of the slice: x: 2, y: 2, z: 4, core: 2. Of those that a mesh axis runs over, the one named last changes fastest.
Arguments:
- pixels: int32 [16, 24, 128], P('img', None, 'seq'), may hold values from 0 to 255
- loss_mask: int32 [16, 24, 128], P('img', None, 'seq'), may hold values from 0 to 1, as said below
- tok_table: float32 [256, 256], P(None, 'seq'), may hold values from -1.2 to 1.2
- pos_table: float32 [67, 256], P(None, 'seq'), may hold values from -0.9 to 0.9
- attn_in: float32 [3, 256, 768], P(None, 'seq'), may hold values from -0.375 to 0.375
- attn_out: float32 [3, 256, 256], P(None, 'seq'), may hold values from -1.5 to 1.5
- ffn_in: float32 [3, 256, 512], P(None, 'seq'), may hold values from -0.375 to 0.375
- ffn_out: float32 [3, 512, 256], P(None, None, 'seq'), may hold values from -0.25 to 0.25
- head_table: float32 [256, 256], P('seq'), may hold values from -0.75 to 0.75
- norms: float32 [7, 2, 256], P(None, None, 'seq')
- tok_first: float32 [256, 256], P(None, 'seq')
- pos_first: float32 [67, 256], P(None, 'seq')
- in_first: float32 [3, 256, 768], P(None, 'seq')
- out_first: float32 [3, 256, 256], P(None, 'seq')
- up_first: float32 [3, 256, 512], P(None, 'seq')
- down_first: float32 [3, 512, 256], P(None, None, 'seq')
- head_first: float32 [256, 256], P('seq')
- norm_first: float32 [7, 2, 256], P(None, None, 'seq')
- tok_second: float32 [256, 256], P(None, 'seq')
- pos_second: float32 [67, 256], P(None, 'seq')
- in_second: float32 [3, 256, 768], P(None, 'seq')
- out_second: float32 [3, 256, 256], P(None, 'seq')
- up_second: float32 [3, 256, 512], P(None, 'seq')
- down_second: float32 [3, 512, 256], P(None, None, 'seq')
- head_second: float32 [256, 256], P('seq')
- norm_second: float32 [7, 2, 256], P(None, None, 'seq')
Outputs:
- loss_sum: float32 [], replicated
- loss_count: float32 [], replicated
- grad_norm: float32 [], replicated
- new_tok: float32 [256, 256], P(None, 'seq')
- new_pos: float32 [67, 256], P(None, 'seq')
- new_in: float32 [3, 256, 768], P(None, 'seq')
- new_out: float32 [3, 256, 256], P(None, 'seq')
- new_up: float32 [3, 256, 512], P(None, 'seq')
- new_down: float32 [3, 512, 256], P(None, None, 'seq')
- new_head: float32 [256, 256], P('seq')
- new_norms: float32 [7, 2, 256], P(None, None, 'seq')
- tok_first_new: float32 [256, 256], P(None, 'seq')
- pos_first_new: float32 [67, 256], P(None, 'seq')
- in_first_new: float32 [3, 256, 768], P(None, 'seq')
- out_first_new: float32 [3, 256, 256], P(None, 'seq')
- up_first_new: float32 [3, 256, 512], P(None, 'seq')
- down_first_new: float32 [3, 512, 256], P(None, None, 'seq')
- head_first_new: float32 [256, 256], P('seq')
- norm_first_new: float32 [7, 2, 256], P(None, None, 'seq')
- tok_second_new: float32 [256, 256], P(None, 'seq')
- pos_second_new: float32 [67, 256], P(None, 'seq')
- in_second_new: float32 [3, 256, 768], P(None, 'seq')
- out_second_new: float32 [3, 256, 256], P(None, 'seq')
- up_second_new: float32 [3, 256, 512], P(None, 'seq')
- down_second_new: float32 [3, 512, 256], P(None, None, 'seq')
- head_second_new: float32 [256, 256], P('seq')
- norm_second_new: float32 [7, 2, 256], P(None, None, 'seq')
The draws below stay inside these ranges and needn't reach their ends.
Inputs may be any that keep to these rules, and one draw needn't show every extreme that they name: `loss_mask`: 0 or 1; position 0 of every image is supervised.
All inputs are finite; a program needn't handle non-finite values.
Results may differ from the reference program's by a relative error of at most 0.012.
Values may be sent and summed in bfloat16 or wider, within the bound.
A program may use at most 320 MiB of HBM per device.

```python
import math
import jax
import jax.numpy as jnp
from jax import lax

D = 256
HEAD = 128
FF = 512
V = 256
STRIDE = 128
BLK = 24
LAYERS = 3
STEP = 10
SIDE = 32
IMAGES = 16
NPARAM = 1724672


def entry_scale(boost):
    return boost * 0.05 / math.sqrt(NPARAM)


def first_draw(key, salt, shape, boost):
    key = jax.random.fold_in(key, salt)
    return 0.11 * entry_scale(boost) * jax.random.normal(key, shape, jnp.float32)


def second_draw(key, salt, shape, boost):
    key = jax.random.fold_in(key, salt)
    factor = jnp.exp(jax.random.uniform(key, shape, jnp.float32, math.log(0.5), math.log(8.0)))
    return 0.0526 * entry_scale(boost) ** 2 * factor


def draw_loss_mask(key, part):
    key = jax.random.fold_in(key, 7)
    first_key, second_key = jax.random.split(key)
    rolls = jax.random.randint(first_key, (IMAGES, BLK, STRIDE), 0, 1000)
    offset = jax.random.randint(second_key, (IMAGES, 1, 1), -100, 101)
    level = 250 + 500 * jnp.arange(STRIDE, dtype=jnp.int32) // max(STRIDE - 1, 1) + offset
    mask_values = (rolls < level).astype(jnp.int32)
    return mask_values.at[:, 0, 0].set(1)


def draw_norms(key, part):
    key = jax.random.fold_in(key, 11)
    first_key, second_key = jax.random.split(key)
    ramp = 0.5 + jnp.arange(D, dtype=jnp.float32) / (D - 1)
    gains = ramp * jax.random.uniform(first_key, (2 * LAYERS + 1, D), jnp.float32, 0.9, 1.1) - 1.0
    shifts = 0.1 * jax.random.normal(second_key, (2 * LAYERS + 1, D), jnp.float32)
    return jnp.stack([gains, shifts], 1)


def draw_tok_first(key, part):
    return first_draw(key, 21, (V, D), 1.0 / math.sqrt(V))


def draw_pos_first(key, part):
    return first_draw(key, 22, (2 * SIDE + 3, D), 1.0)


def draw_in_first(key, part):
    return first_draw(key, 23, (LAYERS, D, 3 * D), 1.0)


def draw_out_first(key, part):
    return first_draw(key, 24, (LAYERS, D, D), 1.0)


def draw_up_first(key, part):
    return first_draw(key, 25, (LAYERS, D, FF), 1.0)


def draw_down_first(key, part):
    return first_draw(key, 26, (LAYERS, FF, D), 1.0)


def draw_head_first(key, part):
    return first_draw(key, 27, (D, V), 1.0)


def draw_norm_first(key, part):
    return first_draw(key, 28, (2 * LAYERS + 1, 2, D), 5.0)


def draw_tok_second(key, part):
    return second_draw(key, 31, (V, D), 1.0 / math.sqrt(V))


def draw_pos_second(key, part):
    return second_draw(key, 32, (2 * SIDE + 3, D), 1.0)


def draw_in_second(key, part):
    return second_draw(key, 33, (LAYERS, D, 3 * D), 1.0)


def draw_out_second(key, part):
    return second_draw(key, 34, (LAYERS, D, D), 1.0)


def draw_up_second(key, part):
    return second_draw(key, 35, (LAYERS, D, FF), 1.0)


def draw_down_second(key, part):
    return second_draw(key, 36, (LAYERS, FF, D), 1.0)


def draw_head_second(key, part):
    return second_draw(key, 37, (D, V), 1.0)


def draw_norm_second(key, part):
    return second_draw(key, 38, (2 * LAYERS + 1, 2, D), 5.0)


def set_ends(array, stream_key, least, high):
    longest = array.shape.index(max(array.shape))
    spots = []
    for shift in (0, 1):
        where = [jax.random.randint(jax.random.fold_in(stream_key, axis), (), 0, length) for axis, length in enumerate(array.shape)]
        where[longest] = (where[longest] + shift) % array.shape[longest]
        spots.append(tuple(where))
    return array.at[spots[0]].set(least).at[spots[1]].set(high)


def levels(key, shape, shards, least, largest):
    gain, own = 1.0, jax.random.fold_in(key, 6)
    for position, blocks in shards:
        draws = jnp.exp(jax.random.uniform(jax.random.fold_in(own, position), (blocks,), jnp.float32, least / len(shards), largest / len(shards)))
        gain = gain * jnp.repeat(draws, shape[position] // blocks).reshape([-1 if axis == position else 1 for axis in range(len(shape))])
    return gain


def gaussian(key, extent, scale, bound, shards=(), kind=jnp.bfloat16):
    drawn = scale * jax.random.normal(key, extent, jnp.float32)
    if shards:
        drawn = drawn * levels(key, extent, shards, -0.22, 0.18)
    return jnp.clip(drawn, -bound, bound).astype(kind)


def setup_inputs(seed: int = 0) -> dict:
    key_of = jax.random.split(jax.random.key(seed), 27)
    return {
        "pixels": set_ends(jax.random.randint(key_of[0], (IMAGES, BLK, STRIDE), 0, V), jax.random.fold_in(key_of[0], 1), 0, V - 1).astype(jnp.int32),
        "loss_mask": draw_loss_mask(jax.random.fold_in(key_of[26], 71), 0),
        "tok_table": gaussian(key_of[2], (V, D), 0.2, 1.2, ((1, 16),), jnp.float32),
        "pos_table": gaussian(key_of[3], (2 * SIDE + 3, D), 0.15, 0.9, ((1, 16),), jnp.float32),
        "attn_in": gaussian(key_of[4], (LAYERS, D, 3 * D), D ** -0.5, 0.375, ((1, 16),), jnp.float32),
        "attn_out": gaussian(key_of[5], (LAYERS, D, D), (D // 16) ** -0.5, 1.5, ((1, 16),), jnp.float32),
        "ffn_in": gaussian(key_of[6], (LAYERS, D, FF), D ** -0.5, 0.375, ((1, 16),), jnp.float32),
        "ffn_out": gaussian(key_of[7], (LAYERS, FF, D), FF ** -0.5, 0.25, ((2, 16),), jnp.float32),
        "head_table": gaussian(key_of[8], (D, V), (D // 4) ** -0.5, 0.75, ((0, 16),), jnp.float32),
        "norms": draw_norms(jax.random.fold_in(key_of[26], 71), 0),
        "tok_first": draw_tok_first(jax.random.fold_in(key_of[26], 71), 0),
        "pos_first": draw_pos_first(jax.random.fold_in(key_of[26], 71), 0),
        "in_first": draw_in_first(jax.random.fold_in(key_of[26], 71), 0),
        "out_first": draw_out_first(jax.random.fold_in(key_of[26], 71), 0),
        "up_first": draw_up_first(jax.random.fold_in(key_of[26], 71), 0),
        "down_first": draw_down_first(jax.random.fold_in(key_of[26], 71), 0),
        "head_first": draw_head_first(jax.random.fold_in(key_of[26], 71), 0),
        "norm_first": draw_norm_first(jax.random.fold_in(key_of[26], 71), 0),
        "tok_second": draw_tok_second(jax.random.fold_in(key_of[26], 71), 0),
        "pos_second": draw_pos_second(jax.random.fold_in(key_of[26], 71), 0),
        "in_second": draw_in_second(jax.random.fold_in(key_of[26], 71), 0),
        "out_second": draw_out_second(jax.random.fold_in(key_of[26], 71), 0),
        "up_second": draw_up_second(jax.random.fold_in(key_of[26], 71), 0),
        "down_second": draw_down_second(jax.random.fold_in(key_of[26], 71), 0),
        "head_second": draw_head_second(jax.random.fold_in(key_of[26], 71), 0),
        "norm_second": draw_norm_second(jax.random.fold_in(key_of[26], 71), 0),
    }


@jax.custom_vjp
def low(v):
    return lax.optimization_barrier(v.astype(jnp.bfloat16)).astype(jnp.float32)

@jax.custom_vjp
def low_back(v):
    return v

def low_keep(v):
    return (low(v), None)

def low_pass(kept, grad):
    return (grad,)

def back_keep(v):
    return (v, None)

def back_low(kept, grad):
    return (low(grad),)
low.defvjp(low_keep, low_pass)
low_back.defvjp(back_keep, back_low)
HIGHEST = lax.Precision.HIGHEST
CLIP_NORM = 0.05
BETA_ONE = 0.9
BETA_TWO = 0.95
LEARN_RATE = 0.1
WEIGHT_DECAY = 0.1
ADAM_EPS = 1e-08
SMOOTHING = 0.1
NORM_EPS = 1e-05
WINDOW_FORMS = ('...brh,...bjh->...brj', '...brj,...bjh->...brh', '...brj,...brh->...bjh')
STRIDE_FORMS = ('...brh,...crh->...brc', '...brc,...crh->...brh', '...brc,...brh->...crh')

def layer_norm(values, gain_pair):
    centre = values - lax.optimization_barrier(jnp.mean(values, -1, keepdims=True))
    spread = lax.optimization_barrier(jnp.mean(centre * centre, -1, keepdims=True))
    return centre * lax.rsqrt(spread + NORM_EPS) * (1.0 + gain_pair[0]) + gain_pair[1]

def matmul(left, right):
    return jnp.matmul(left, right, precision=HIGHEST)

def window_keys(joined):
    earlier = jnp.concatenate([jnp.zeros_like(joined[:1]), joined[:-1]], 0)
    return jnp.concatenate([earlier, joined], 1)

def window_allowed(blocks, residues):
    key_index = jnp.arange(2 * STRIDE, dtype=jnp.int32)
    distance = STRIDE + residues[:, None] - key_index[None, :]
    nearby = (distance >= 0) & (distance < STRIDE)
    started = (jnp.arange(blocks, dtype=jnp.int32)[:, None, None] > 0) | (key_index[None, None, :] >= STRIDE)
    return nearby[None] & started

def stride_allowed(blocks):
    block_index = jnp.arange(blocks, dtype=jnp.int32)
    return (block_index[:, None] >= block_index[None, :])[:, None, :]

def attend(query, key_rows, value_rows, allowed, forms):
    raw = low_back(jnp.einsum(forms[0], query, key_rows, precision=HIGHEST))
    scores = jnp.where(allowed, raw * HEAD ** (-0.5), -1e+30)
    weights = low(jax.nn.softmax(scores, axis=-1))
    return jnp.einsum(forms[1], weights, value_rows, precision=HIGHEST)

def block_forward(state, w_in, w_out, w_up, w_down, pair_one, pair_two, window, strided):
    hidden = low(layer_norm(state, pair_one))
    mixed = low(low_back(matmul(hidden, w_in)))
    query0, query1, key0, key1, value0, value1 = jnp.split(mixed, 6, axis=-1)
    joined = window_keys(jnp.concatenate([key0, value0], -1))
    out0 = attend(query0, joined[..., :HEAD], joined[..., HEAD:], window, WINDOW_FORMS)
    out1 = attend(query1, key1, value1, strided, STRIDE_FORMS)
    heads = low(low_back(jnp.concatenate([out0, out1], -1)))
    middle = state + low_back(matmul(heads, w_out))
    hidden_two = low(layer_norm(middle, pair_two))
    upper = low_back(matmul(hidden_two, w_up))
    active = low(jax.nn.gelu(upper))
    return middle + low_back(matmul(active, w_down))

def forward_image(weights, input_ids, targets, mask):
    tok_w, pos_w, in_w, out_w, up_w, down_w, head_w, norm_w = weights
    blocks = input_ids.shape[0]
    place = jnp.arange(blocks, dtype=jnp.int32)[:, None] * STRIDE + jnp.arange(STRIDE, dtype=jnp.int32)[None, :]
    present = (input_ids >= 0).astype(jnp.float32)[..., None]
    state = tok_w[jnp.maximum(input_ids, 0)] * present
    state = state + pos_w[place // (3 * SIDE)] + pos_w[SIDE + place // 3 % SIDE] + pos_w[2 * SIDE + place % 3]
    window = window_allowed(blocks, jnp.arange(STRIDE, dtype=jnp.int32))
    strided = stride_allowed(blocks)
    for layer_at in range(LAYERS):
        state = block_forward(state, in_w[layer_at], out_w[layer_at], up_w[layer_at], down_w[layer_at], norm_w[2 * layer_at], norm_w[2 * layer_at + 1], window, strided)
    hidden = low(layer_norm(state, norm_w[2 * LAYERS]))
    logits = low_back(matmul(hidden, head_w))
    log_probs = jax.nn.log_softmax(logits, -1)
    picked = jnp.take_along_axis(log_probs, targets[..., None], -1)[..., 0]
    per_token = -((1.0 - SMOOTHING) * picked + SMOOTHING * lax.optimization_barrier(jnp.mean(log_probs, -1)))
    return jnp.sum(mask.astype(jnp.float32) * per_token)

def adam_step(master, gradient, first, second, factor):
    gradient = gradient * factor
    first = BETA_ONE * first + (1.0 - BETA_ONE) * gradient
    second = BETA_TWO * second + (1.0 - BETA_TWO) * gradient * gradient
    moved = first / (1.0 - BETA_ONE ** STEP) / (jnp.sqrt(second / (1.0 - BETA_TWO ** STEP)) + ADAM_EPS)
    return (master - LEARN_RATE * (moved + WEIGHT_DECAY * master), first, second)

def reference(pixels, loss_mask, tok_table, pos_table, attn_in, attn_out, ffn_in, ffn_out, head_table, norms, tok_first, pos_first, in_first, out_first, up_first, down_first, head_first, norm_first, tok_second, pos_second, in_second, out_second, up_second, down_second, head_second, norm_second):
    masters = (tok_table, pos_table, attn_in, attn_out, ffn_in, ffn_out, head_table, norms)
    firsts = (tok_first, pos_first, in_first, out_first, up_first, down_first, head_first, norm_first)
    seconds = (tok_second, pos_second, in_second, out_second, up_second, down_second, head_second, norm_second)
    flat = pixels.reshape(pixels.shape[0], -1)
    start = jnp.full((flat.shape[0], 1), -1, jnp.int32)
    input_ids = jnp.concatenate([start, flat[:, :-1]], 1).reshape(pixels.shape)
    count = jnp.sum(loss_mask).astype(jnp.float32)

    def total(params):
        weights = tuple((low(item) for item in params))

        def one_image(carry, item):
            return (carry + jax.checkpoint(forward_image)(weights, item[0], item[1], item[2]), None)
        summed, _ = lax.scan(one_image, jnp.zeros((), jnp.float32), (input_ids, pixels, loss_mask))
        return (summed / count, summed)
    _, pull, loss_sum = jax.vjp(total, masters, has_aux=True)
    grads = pull(jnp.ones((), jnp.float32))[0]
    squares = sum((jnp.sum(item * item) for item in grads))
    norm = jnp.sqrt(squares)
    factor = jnp.minimum(1.0, CLIP_NORM / norm)
    updated = [adam_step(masters[index], grads[index], firsts[index], seconds[index], factor) for index in range(8)]
    return (loss_sum, count, norm, updated[0][0], updated[1][0], updated[2][0], updated[3][0], updated[4][0], updated[5][0], updated[6][0], updated[7][0], updated[0][1], updated[1][1], updated[2][1], updated[3][1], updated[4][1], updated[5][1], updated[6][1], updated[7][1], updated[0][2], updated[1][2], updated[2][2], updated[3][2], updated[4][2], updated[5][2], updated[6][2], updated[7][2])
```

```python
import functools
import math

import jax
import jax.numpy as jnp
from jax import lax
from jax.experimental import pallas as pl
from jax.experimental.pallas import tpu as pltpu
from jax.sharding import PartitionSpec as P

D = 256
HEAD = 128
FF = 512
V = 256
STRIDE = 128
LAYERS = 3
NORMS = 2 * LAYERS + 1
STEP = 10
SIDE = 32
POS = 2 * SIDE + 3
CLIP_NORM = 0.05
BETA_ONE = 0.9
BETA_TWO = 0.95
LEARN_RATE = 0.1
WEIGHT_DECAY = 0.1
ADAM_EPS = 1e-08
SMOOTHING = 0.1
NORM_EPS = 1e-05
SCALE = HEAD ** (-0.5)

C_IN, C_OUT, C_UP, C_DOWN = (0, 768), (768, 1024), (1024, 1536), (1536, 2048)
C_LAYER = 2048
C_TOK, C_POS, C_HEAD, C_NORM = (0, 256), (256, 384), (384, 640), (640, 768)
C_REST = 768

BF = jnp.bfloat16
F32 = jnp.float32
VMEM_LIMIT = 64 * 1024 * 1024


def dot(a, b):
    return lax.dot_general(a, b, (((1,), (0,)), ((), ())), preferred_element_type=F32)


def dot_nt(a, b):
    return lax.dot_general(a, b, (((1,), (1,)), ((), ())), preferred_element_type=F32)


def dot_tn(a, b):
    return lax.dot_general(a, b, (((0,), (0,)), ((), ())), preferred_element_type=F32)


class Geometry:
    def __init__(self, n, m, images, blocks):
        self.n, self.m, self.images, self.blocks = n, m, images, blocks
        self.depth = n // 4
        self.rows = D // n
        self.group = n // images
        self.res = STRIDE // self.group
        self.own = STRIDE // n

    def place(self):
        me = lax.axis_index("seq")
        return me // 4, me // 2 % 2, me % 2


def seq_id(z, y, core):
    return {"seq": z * 4 + y * 2 + core}


def greet(devices):
    barrier = pltpu.get_barrier_semaphore()
    for device in devices:
        pl.semaphore_signal(barrier, inc=1, device_id=device, device_id_type=pl.DeviceIdType.MESH)
    pl.semaphore_wait(barrier, len(devices))


def push(src, dst, send_sem, recv_sem, device):
    return pltpu.make_async_remote_copy(
        src_ref=src,
        dst_ref=dst,
        send_sem=send_sem,
        recv_sem=recv_sem,
        device_id=device,
        device_id_type=pl.DeviceIdType.MESH,
    )


def gather_kernel(
    geo, pixels, mask, tok, pos, w_in, w_out, w_up, w_down, head, norms, px, rest, layers, send, recv
):
    z, y, core = geo.place()
    depth = geo.depth
    px[z, y, core, : geo.images] = pixels[...]
    px[z, y, core, geo.images :] = mask[...]
    rest[z, y, core, :, C_TOK[0] : C_TOK[1]] = tok[...].astype(BF)
    rest[z, y, core, :, C_POS[0] : C_POS[1]] = pos[...].astype(BF)
    rest[z, y, core, :, C_HEAD[0] : C_HEAD[1]] = head[...].astype(BF)
    rest[z, y, core, :, C_NORM[0] : C_NORM[1]] = norms[...].astype(BF)
    for l in range(LAYERS):
        layers[l, z, y, core, :, C_IN[0] : C_IN[1]] = w_in[l].astype(BF)
        layers[l, z, y, core, :, C_OUT[0] : C_OUT[1]] = w_out[l].astype(BF)
        layers[l, z, y, core, :, C_UP[0] : C_UP[1]] = w_up[l].astype(BF)
        layers[l, z, y, core, :, C_DOWN[0] : C_DOWN[1]] = w_down[l].astype(BF)
    peers = [seq_id(lax.rem(z + k, depth), y, core) for k in range(1, depth)]
    beside, sibling = seq_id(z, 1 - y, core), seq_id(z, y, 1 - core)
    greet(peers + [beside, sibling])
    arrays = [px, rest] + [layers.at[l] for l in range(LAYERS)]
    first, second, third = [], [], []
    for a, array in enumerate(arrays):
        mine = array.at[z, y, core]
        copies = [push(mine, mine, send.at[a, k], recv.at[a, k], peers[k]) for k in range(depth - 1)]
        for copy in copies:
            copy.start()
        first.append(copies)
    for a, array in enumerate(arrays):
        for copy in first[a]:
            copy.wait_recv()
        column = array.at[pl.ds(0, depth), y, core]
        copy = push(column, column, send.at[a, depth - 1], recv.at[a, depth - 1], beside)
        copy.start()
        second.append(copy)
    for a, array in enumerate(arrays):
        second[a].wait_recv()
        half = array.at[pl.ds(0, depth), pl.ds(0, 2), core]
        copy = push(half, half, send.at[a, depth], recv.at[a, depth], sibling)
        copy.start()
        third.append(copy)
    for a in range(len(arrays)):
        third[a].wait()
        second[a].wait_send()
        for copy in first[a]:
            copy.wait_send()


def normalise(x):
    centre = x - jnp.mean(x, -1, keepdims=True)
    spread = jnp.mean(centre * centre, -1, keepdims=True)
    rstd = lax.rsqrt(spread + NORM_EPS)
    return centre * rstd, rstd


def fold(x):
    return jnp.sum(x.reshape(x.shape[0] // 8, 8, x.shape[1]), 0)


def normalise_back(dy, unit, rstd, gain):
    dxh = dy * (1.0 + gain)
    mean_one = jnp.mean(dxh, -1, keepdims=True)
    mean_two = jnp.mean(dxh * unit, -1, keepdims=True)
    return rstd * (dxh - mean_one - unit * mean_two), fold(dy * unit), fold(dy)


def gelu_both(u):
    c = math.sqrt(2.0 / math.pi)
    square = u * u
    t = jnp.tanh(c * u * (1.0 + 0.044715 * square))
    half = 0.5 * (1.0 + t)
    slope = half + 0.5 * u * (1.0 - t * t) * (c * (1.0 + 3.0 * 0.044715 * square))
    return u * half, slope


def softmax(scores):
    e = jnp.exp(scores - jnp.max(scores, -1, keepdims=True))
    return e * (1.0 / jnp.sum(e, -1, keepdims=True))


def step_kernel(
    geo, chunk, px, rest, layers, g_rest, g_layers, stats,
    x_s, x1_s, q0_s, kv_s, qkv1_s, p0_s, p1_s, o_s, a_s, slope_s, stage, o1_s, do0_s, dq0_s, acc, back,
    dx_s, ids_s, tgt_s, msk_s, prev_s, bias0, bias1, norm_s, gnorm, wide, send, recv,
):
    z, y, core = geo.place()
    me = lax.axis_index("seq")
    depth, group, res, blocks, own = geo.depth, geo.group, geo.res, geo.blocks, geo.own
    image, part = me // group, me % group
    siblings = [{"seq": image * group + lax.rem(part + k, group)} for k in range(1, group)]
    greet(siblings)
    rows = chunk * res
    chunks = blocks // chunk
    n_groups = res // 8

    def table(ref, cols):
        piece = ref[..., cols[0] : cols[1]]
        width = cols[1] - cols[0]
        if geo.rows % 16:
            return piece.astype(F32).reshape(D, width).astype(BF)
        return piece.reshape(D, width)

    def layer_table(l, cols):
        return table(layers.at[l], cols)

    def add_to(ref, cols, value):
        shape = (depth, 2, 2, geo.rows, cols[1] - cols[0])
        ref[..., cols[0] : cols[1]] += value.reshape(shape)

    for ref in (ids_s, tgt_s, msk_s, prev_s, wide):
        ref[...] = jnp.zeros_like(ref)
    span = depth // group
    for j in range(geo.images):
        slot = (part * span + j // 4, j // 2 % 2, j % 2)
        tgt_s[j * own : (j + 1) * own, :blocks] = px[(*slot, image)].astype(F32)
        msk_s[j * own : (j + 1) * own, :blocks] = px[(*slot, geo.images + image)].astype(F32)
    before = px[lax.rem(part * span + depth - 1, depth), 1, 1, image].astype(F32)
    prev_s[:own, :blocks] = before
    prev = prev_s[...]
    lane = lax.broadcasted_iota(jnp.int32, prev.shape, 1)
    moved = jnp.where(lane == 0, -1.0, pltpu.roll(prev, 1, 1))
    prev = jnp.where(part == 0, moved, prev)
    ids_s[0:1, :] = prev[own - 1 : own, :]
    ids_s[1:res, :] = tgt_s[0 : res - 1, :]

    norm_s[...] = jnp.transpose(table(rest, C_NORM).astype(F32))[:16].reshape(16, 1, D)

    qi = part * res + lax.broadcasted_iota(jnp.int32, (res, 2 * STRIDE), 0)
    kj = lax.broadcasted_iota(jnp.int32, (res, 2 * STRIDE), 1)
    seen = (kj > qi) & (kj <= qi + STRIDE)
    bias0[0] = jnp.where(seen & (kj >= STRIDE), 0.0, -1e30)
    bias0[1] = jnp.where(seen, 0.0, -1e30)
    side = 8 * blocks
    ri = lax.broadcasted_iota(jnp.int32, (side, side), 0)
    ci = lax.broadcasted_iota(jnp.int32, (side, side), 1)
    bias1[...] = jnp.where(((ri & 7) == (ci & 7)) & (ri >= ci), 0.0, -1e30)

    g_rest[...] = jnp.zeros_like(g_rest)
    g_layers[...] = jnp.zeros_like(g_layers)
    gnorm[...] = jnp.zeros_like(gnorm)

    def spread(ref, b0):
        values = ref[...].astype(BF)
        at = lax.broadcasted_iota(jnp.int32, (128, 128), 0)
        return jnp.concatenate(
            [dot(values, (at == b0 + j).astype(F32).astype(BF)) for j in range(chunk)], 0
        )

    def one_hot(ref, b0):
        value = spread(ref, b0)
        lane = lax.broadcasted_iota(jnp.int32, (rows, 128), 1).astype(F32)
        return jnp.concatenate([(value == lane).astype(F32), (value == lane + 128.0).astype(F32)], 1)

    def place_hot(b0):
        r = lax.broadcasted_iota(jnp.int32, (rows, 128), 0)
        lane = lax.broadcasted_iota(jnp.int32, (rows, 128), 1).astype(F32)
        p = ((b0 + r // res) * STRIDE + part * res + r % res).astype(F32)
        third = jnp.floor((p + 0.5) * (1.0 / 3.0))
        line = jnp.floor((third + 0.5) * (1.0 / SIDE))
        hits = (lane == line) | (lane == SIDE + third - SIDE * line)
        return (hits | (lane == 2 * SIDE + p - 3.0 * third)).astype(F32)

    def loop(count, body):
        lax.fori_loop(0, count, lambda i, carry: (body(i), carry)[1], 0)

    def embed(i):
        b0 = i * chunk
        hot = jnp.concatenate([one_hot(ids_s, b0), place_hot(b0)], 1).astype(BF)
        x = dot_nt(hot, table(rest, (C_TOK[0], C_POS[1])))
        x_s[0, pl.ds(b0, chunk)] = x.reshape(chunk, res, D)

    loop(chunks, embed)

    def exchange(l, k):
        mine = kv_s.at[l, pl.ds(1, blocks), part]
        return push(mine, mine, send.at[k], recv.at[l, k], siblings[k])

    def forward(l):
        def mix(i):
            b0 = i * chunk
            unit, _ = normalise(x_s[l, pl.ds(b0, chunk)].reshape(rows, D))
            h = (unit * (1.0 + norm_s[4 * l]) + norm_s[4 * l + 1]).astype(BF)
            qkv = dot(h, layer_table(l, C_IN)).reshape(chunk, res, 6 * HEAD)
            q0_s[l, pl.ds(b0, chunk)] = qkv[..., :HEAD].astype(BF)
            kv_s[l, pl.ds(b0 + 1, chunk), part, :, :HEAD] = qkv[..., 2 * HEAD : 3 * HEAD].astype(BF)
            kv_s[l, pl.ds(b0 + 1, chunk), part, :, HEAD:] = qkv[..., 4 * HEAD : 5 * HEAD].astype(BF)
            stage[pl.ds(b0, chunk), :, :HEAD] = qkv[..., HEAD : 2 * HEAD]
            stage[pl.ds(b0, chunk), :, HEAD : 2 * HEAD] = qkv[..., 3 * HEAD : 4 * HEAD]
            stage[pl.ds(b0, chunk), :, 2 * HEAD :] = qkv[..., 5 * HEAD :]

        kv_s[l, 0] = jnp.zeros((group, res, 2 * HEAD), BF)
        loop(chunks, mix)
        copies = [exchange(l, k) for k in range(group - 1)]
        for copy in copies:
            copy.start()

        def strided(g):
            at = pl.ds(pl.multiple_of(8 * g, 8), 8)
            qkv = stage[:, at, :].reshape(8 * blocks, 3 * HEAD).astype(BF)
            qkv1_s[l, g] = qkv
            scores = dot_nt(qkv[:, :HEAD], qkv[:, HEAD : 2 * HEAD]) * SCALE + bias1[...]
            probs = softmax(scores).astype(BF)
            p1_s[l, g] = probs
            o1_s[:, at, :] = dot(probs, qkv[:, 2 * HEAD :]).reshape(blocks, 8, HEAD)

        loop(n_groups, strided)
        for copy in copies:
            copy.wait()

        def window(b):
            kv = kv_s[l, pl.ds(b, 2)].reshape(2 * STRIDE, 2 * HEAD)
            scores = dot_nt(q0_s[l, b], kv[:, :HEAD]) * SCALE + bias0[jnp.minimum(b, 1)]
            probs = softmax(scores).astype(BF)
            p0_s[l, b] = probs
            o_s[l, b, :, :HEAD] = dot(probs, kv[:, HEAD:]).astype(BF)

        loop(blocks, window)

        def feed(i):
            b0 = i * chunk
            at = pl.ds(b0, chunk)
            o_s[l, at, :, HEAD:] = o1_s[at].astype(BF)
            x1 = x_s[l, at].reshape(rows, D) + dot(o_s[l, at].reshape(rows, D), layer_table(l, C_OUT))
            x1_s[l, at] = x1.reshape(chunk, res, D)
            unit, _ = normalise(x1)
            h = (unit * (1.0 + norm_s[4 * l + 2]) + norm_s[4 * l + 3]).astype(BF)
            a, slope = gelu_both(dot(h, layer_table(l, C_UP)))
            a = a.astype(BF)
            a_s[l, at] = a.reshape(chunk, res, FF)
            slope_s[l, at] = slope.astype(BF).reshape(chunk, res, FF)
            x2 = x1 + dot_nt(a, layer_table(l, C_DOWN))
            x_s[l + 1, at] = x2.reshape(chunk, res, D)

        loop(chunks, feed)

    loop(LAYERS, forward)

    def finish(i, loss):
        b0 = i * chunk
        at = pl.ds(b0, chunk)
        unit, rstd = normalise(x_s[LAYERS, at].reshape(rows, D))
        gain = norm_s[4 * LAYERS]
        h = (unit * (1.0 + gain) + norm_s[4 * LAYERS + 1]).astype(BF)
        head = table(rest, C_HEAD)
        logits = dot(h, head)
        hot = one_hot(tgt_s, b0)
        shift = logits - jnp.max(logits, -1, keepdims=True)
        e = jnp.exp(shift)
        total = jnp.sum(e, -1, keepdims=True)
        weight = spread(msk_s, b0)
        per = (
            jnp.log(total)
            - (1.0 - SMOOTHING) * jnp.sum(hot * shift, -1, keepdims=True)
            - SMOOTHING * jnp.mean(shift, -1, keepdims=True)
        )
        loss = loss + jnp.sum(weight[:, :1] * per, 0, keepdims=True)
        weight = jnp.concatenate([weight, weight], 1)
        d_logits = weight * (e * (1.0 / total) - (1.0 - SMOOTHING) * hot - SMOOTHING / V)
        d_logits = d_logits.astype(BF)
        add_to(g_rest, C_HEAD, dot_tn(h, d_logits))
        dx, g_gain, g_bias = normalise_back(dot_nt(d_logits, head), unit, rstd, gain)
        gnorm[4 * LAYERS] += g_gain
        gnorm[4 * LAYERS + 1] += g_bias
        dx_s[at] = dx.reshape(chunk, res, D)
        return loss

    loss = lax.fori_loop(0, chunks, finish, jnp.zeros((1, 1), F32))
    count = jnp.sum(jnp.sum(msk_s[...], 0, keepdims=True), 1, keepdims=True)
    line = lax.broadcasted_iota(jnp.int32, (8, 128), 0)
    stats[...] = jnp.where(line == 0, loss, jnp.where(line == 1, count, 0.0))

    def give(l, slot, k):
        other = lax.rem(part + k + 1, group)
        return push(
            acc.at[pl.ds(1, blocks), other], back.at[slot, k], send.at[k], recv.at[LAYERS + l, k], siblings[k]
        )

    def backward(step):
        l = LAYERS - 1 - step
        slot = step % 2

        def feed(i):
            b0 = i * chunk
            at = pl.ds(b0, chunk)
            dx2 = dx_s[at].reshape(rows, D)
            g2 = dx2.astype(BF)
            a = a_s[l, at].reshape(rows, FF)
            add_to(g_layers.at[l], C_DOWN, dot_tn(g2, a))
            du = slope_s[l, at].reshape(rows, FF).astype(F32) * dot(g2, layer_table(l, C_DOWN))
            du = du.astype(BF)
            unit, rstd = normalise(x1_s[l, at].reshape(rows, D))
            gain = norm_s[4 * l + 2]
            h = (unit * (1.0 + gain) + norm_s[4 * l + 3]).astype(BF)
            add_to(g_layers.at[l], C_UP, dot_tn(h, du))
            dh = dot_nt(du, layer_table(l, C_UP))
            dx, g_gain, g_bias = normalise_back(dh, unit, rstd, gain)
            gnorm[4 * l + 2] += g_gain
            gnorm[4 * l + 3] += g_bias
            dx = dx + dx2
            dx_s[at] = dx.reshape(chunk, res, D)
            g1 = dx.astype(BF)
            add_to(g_layers.at[l], C_OUT, dot_tn(o_s[l, at].reshape(rows, D), g1))
            do = dot_nt(g1, layer_table(l, C_OUT)).reshape(chunk, res, D)
            do0_s[at] = do[..., :HEAD].astype(BF)
            o1_s[at] = do[..., HEAD:]

        loop(chunks, feed)
        acc[...] = jnp.zeros_like(acc)

        def window(b):
            kv = kv_s[l, pl.ds(b, 2)].reshape(2 * STRIDE, 2 * HEAD)
            probs = p0_s[l, b]
            do = do0_s[b]
            dp = dot_nt(do, kv[:, HEAD:])
            wide_p = probs.astype(F32)
            ds = (wide_p * (dp - jnp.sum(wide_p * dp, -1, keepdims=True)) * SCALE).astype(BF)
            dq0_s[b] = dot(ds, kv[:, :HEAD]).astype(BF)
            dkv = jnp.concatenate([dot_tn(ds, q0_s[l, b]), dot_tn(probs, do)], 1)
            acc[pl.ds(b, 2)] += dkv.reshape(2, group, res, 2 * HEAD)

        loop(blocks, window)
        copies = [give(l, slot, k) for k in range(group - 1)]
        for copy in copies:
            copy.start()

        def strided(g):
            at = pl.ds(pl.multiple_of(8 * g, 8), 8)
            qkv = qkv1_s[l, g]
            probs = p1_s[l, g]
            do = o1_s[:, at, :].reshape(8 * blocks, HEAD).astype(BF)
            dp = dot_nt(do, qkv[:, 2 * HEAD :])
            wide_p = probs.astype(F32)
            ds = (wide_p * (dp - jnp.sum(wide_p * dp, -1, keepdims=True)) * SCALE).astype(BF)
            dq = dot(ds, qkv[:, HEAD : 2 * HEAD])
            dk = dot_tn(ds, qkv[:, :HEAD])
            dv = dot_tn(probs, do)
            stage[:, at, :] = jnp.concatenate([dq, dk, dv], 1).reshape(blocks, 8, 3 * HEAD)

        loop(n_groups, strided)
        for copy in copies:
            copy.wait()

        def mix(i):
            b0 = i * chunk
            at = pl.ds(b0, chunk)
            dkv = acc[pl.ds(b0 + 1, chunk), part]
            for k in range(group - 1):
                dkv = dkv + back[slot, k, at]
            d1 = stage[at]
            dqkv = jnp.concatenate(
                [
                    dq0_s[at],
                    d1[..., :HEAD].astype(BF),
                    dkv[..., :HEAD].astype(BF),
                    d1[..., HEAD : 2 * HEAD].astype(BF),
                    dkv[..., HEAD:].astype(BF),
                    d1[..., 2 * HEAD :].astype(BF),
                ],
                -1,
            ).reshape(rows, 6 * HEAD)
            unit, rstd = normalise(x_s[l, at].reshape(rows, D))
            gain = norm_s[4 * l]
            h = (unit * (1.0 + gain) + norm_s[4 * l + 1]).astype(BF)
            add_to(g_layers.at[l], C_IN, dot_tn(h, dqkv))
            dh = dot_nt(dqkv, layer_table(l, C_IN))
            dx, g_gain, g_bias = normalise_back(dh, unit, rstd, gain)
            gnorm[4 * l] += g_gain
            gnorm[4 * l + 1] += g_bias
            dx_s[at] += dx.reshape(chunk, res, D)

        loop(chunks, mix)

    loop(LAYERS, backward)

    def embed_back(i):
        b0 = i * chunk
        hot = jnp.concatenate([one_hot(ids_s, b0), place_hot(b0)], 1).astype(BF)
        dx = dx_s[pl.ds(b0, chunk)].reshape(rows, D)
        high = dx.astype(BF)
        low = (dx - high.astype(F32)).astype(BF)
        add_to(g_rest, (C_TOK[0], C_POS[1]), dot_tn(high, hot) + dot_tn(low, hot))

    loop(chunks, embed_back)
    for i in range(2 * NORMS):
        wide[i : i + 1, :] = jnp.sum(gnorm[i], 0, keepdims=True)
    add_to(g_rest, C_NORM, jnp.transpose(wide[...]))


def adam(master, gradient, first, second):
    first = BETA_ONE * first + (1.0 - BETA_ONE) * gradient
    second = BETA_TWO * second + (1.0 - BETA_TWO) * gradient * gradient
    moved = first / (1.0 - BETA_ONE**STEP) / (jnp.sqrt(second / (1.0 - BETA_TWO**STEP)) + ADAM_EPS)
    return master - LEARN_RATE * (moved + WEIGHT_DECAY * master), first, second


def update_kernel(geo, *refs):
    g_rest, g_layers, stats = refs[:3]
    masters, firsts, seconds = refs[3:11], refs[11:19], refs[19:27]
    totals = refs[27]
    outs = (refs[28:36], refs[36:44], refs[44:52])
    (s1_rest, s1_layers, r1_rest, r1_layers, s2_rest, s2_layers, r2_rest, r2_layers,
     s3_rest, s3_layers, r3_rest, r3_layers, r4_rest, r4_layers, sum_rest, sum_layers,
     st_img, st_core, st_y, st_z, st_send, send, recv, st_send_sem, st_recv_sem) = refs[52:]
    z, y, core = geo.place()
    x = lax.axis_index("img")
    depth, m = geo.depth, geo.m
    peers = [seq_id(lax.rem(z + k, depth), y, core) for k in range(1, depth)]
    beside, sibling = seq_id(z, 1 - y, core), seq_id(z, y, 1 - core)
    across = [{"img": lax.rem(x + k, m)} for k in range(1, m)]
    greet(peers + [beside, sibling] + across)

    def sections(a, b):
        return [a] + [b.at[l] for l in range(LAYERS)]

    grads = sections(g_rest, g_layers)
    s1, r1 = sections(s1_rest, s1_layers), sections(r1_rest, r1_layers)
    s2, r2 = sections(s2_rest, s2_layers), sections(r2_rest, r2_layers)
    s3, r3 = sections(s3_rest, s3_layers), sections(r3_rest, r3_layers)
    r4 = sections(r4_rest, r4_layers)
    sums = sections(sum_rest, sum_layers)
    order = list(range(1 + LAYERS))
    every = pl.ds(0, depth)

    st_img[x] = stats[...]
    st_copies = [
        push(st_img.at[x], st_img.at[x], st_send_sem.at[k], st_recv_sem.at[k], across[k]) for k in range(m - 1)
    ]
    for copy in st_copies:
        copy.start()
    one, two, three, four = {}, {}, {}, {}
    for a in order:
        s1[a][...] = grads[a][every, pl.ds(0, 2), 1 - core].astype(BF)
        one[a] = push(s1[a], r1[a], send.at[a, 0], recv.at[a, 0], sibling)
        one[a].start()
    for a in order:
        one[a].wait()
        s2[a][...] = (grads[a][every, 1 - y, core] + r1[a][every, 1 - y].astype(F32)).astype(BF)
        two[a] = push(s2[a], r2[a], send.at[a, 1], recv.at[a, 1], beside)
        two[a].start()
    for a in order:
        two[a].wait()
        total = grads[a][every, y, core] + r1[a][every, y].astype(F32) + r2[a][...].astype(F32)
        s3[a][...] = total.astype(BF)
        three[a] = [
            push(s3[a].at[lax.rem(z + k, depth)], r3[a].at[k - 1], send.at[a, 1 + k], recv.at[a, 1 + k], peers[k - 1])
            for k in range(1, depth)
        ]
        for copy in three[a]:
            copy.start()
    for a in order:
        for copy in three[a]:
            copy.wait()
        total = s3[a][z].astype(F32)
        for k in range(1, depth):
            total = total + r3[a][k - 1].astype(F32)
        r4[a][x] = total.astype(BF)
        four[a] = [
            push(r4[a].at[x], r4[a].at[x], send.at[a, depth + 1 + k], recv.at[a, depth + 1 + k], across[k])
            for k in range(m - 1)
        ]
        for copy in four[a]:
            copy.start()
    squares = jnp.zeros((1, 1), F32)
    for a in order:
        for copy in four[a]:
            copy.wait()
        total = r4[a][0].astype(F32)
        for k in range(1, m):
            total = total + r4[a][k].astype(F32)
        sums[a][...] = total
        squares = squares + jnp.sum(jnp.sum(total * total, 0, keepdims=True), 1, keepdims=True)
    for copy in st_copies:
        copy.wait()
    told = st_img[0]
    for k in range(1, m):
        told = told + st_img[k]
    line = lax.broadcasted_iota(jnp.int32, (8, 128), 0)
    told = jnp.where(line == 2, squares, told)
    base = m - 1

    def swap(told, buffer, index, where, device):
        buffer[where] = told
        copy = push(buffer.at[where], buffer.at[where], st_send_sem.at[base + index], st_recv_sem.at[base + index], device)
        copy.start()
        copy.wait()
        return buffer[0] + buffer[1]

    told = swap(told, st_core, 0, core, sibling)
    told = swap(told, st_y, 1, y, beside)
    st_z[z] = told
    copies = [
        push(st_z.at[z], st_z.at[z], st_send_sem.at[base + 1 + k], st_recv_sem.at[base + 1 + k], peers[k - 1])
        for k in range(1, depth)
    ]
    for copy in copies:
        copy.start()
    for copy in copies:
        copy.wait()
    told = st_z[0]
    for k in range(1, depth):
        told = told + st_z[k]
    count = told[1:2, :1]
    norm = jnp.sqrt(told[2:3, :1]) / count
    totals[...] = jnp.where(line == 2, norm, told)
    factor = jnp.minimum(1.0, CLIP_NORM / norm) / count

    def put(index, at, gradient):
        gradient = gradient * factor
        result = adam(masters[index][at], gradient, firsts[index][at], seconds[index][at])
        for k in range(3):
            outs[k][index][at] = result[k]

    put(0, ..., sum_rest[:, C_TOK[0] : C_TOK[1]])
    put(1, ..., sum_rest[:, C_POS[0] : C_POS[1]])
    put(6, ..., sum_rest[:, C_HEAD[0] : C_HEAD[1]])
    put(7, ..., sum_rest[:, C_NORM[0] : C_NORM[1]])
    for l in range(LAYERS):
        put(2, l, sum_layers[l, :, C_IN[0] : C_IN[1]])
        put(3, l, sum_layers[l, :, C_OUT[0] : C_OUT[1]])
        put(4, l, sum_layers[l, :, C_UP[0] : C_UP[1]])
        put(5, l, sum_layers[l, :, C_DOWN[0] : C_DOWN[1]])


def packed(tok, pos, w_in, w_out, w_up, w_down, head, norms):
    rows = head.shape[0]
    pos = jnp.pad(pos.T, ((0, 0), (0, 128 - POS)))
    norms = jnp.pad(norms.reshape(2 * NORMS, rows).T, ((0, 0), (0, 128 - 2 * NORMS)))
    return (tok.T, pos, w_in, w_out, w_up, jnp.swapaxes(w_down, 1, 2), head, norms)


def unpacked(tok, pos, w_in, w_out, w_up, w_down, head, norms):
    norms = norms[:, : 2 * NORMS].T.reshape(NORMS, 2, head.shape[0])
    return (tok.T, pos[:, :POS].T, w_in, w_out, w_up, jnp.swapaxes(w_down, 1, 2), head, norms)


def on_device(geo, pixels, loss_mask, *weights):
    masters, firsts, seconds = (packed(*weights[k : k + 8]) for k in (0, 8, 16))
    n_rows, depth, blocks, res, group = geo.rows, geo.depth, geo.blocks, geo.res, geo.group
    vmem = pl.BlockSpec(memory_space=pltpu.VMEM)
    px, rest, layers = pl.pallas_call(
        functools.partial(gather_kernel, geo),
        out_shape=(
            jax.ShapeDtypeStruct((depth, 2, 2, 2 * geo.images, geo.own, blocks), jnp.int32),
            jax.ShapeDtypeStruct((depth, 2, 2, n_rows, C_REST), BF),
            jax.ShapeDtypeStruct((LAYERS, depth, 2, 2, n_rows, C_LAYER), BF),
        ),
        in_specs=[vmem] * 10,
        out_specs=(vmem, vmem, vmem),
        scratch_shapes=[
            pltpu.SemaphoreType.DMA((2 + LAYERS, depth + 1)),
            pltpu.SemaphoreType.DMA((2 + LAYERS, depth + 1)),
        ],
        compiler_params=pltpu.CompilerParams(
            collective_id=0, has_side_effects=True, vmem_limit_bytes=VMEM_LIMIT
        ),
        name="gather",
    )(jnp.swapaxes(pixels, 1, 2), jnp.swapaxes(loss_mask, 1, 2), *masters)

    chunk = 4
    n_groups = res // 8
    side = 8 * blocks
    g_rest, g_layers, stats = pl.pallas_call(
        functools.partial(step_kernel, geo, chunk),
        out_shape=(
            jax.ShapeDtypeStruct((depth, 2, 2, n_rows, C_REST), F32),
            jax.ShapeDtypeStruct((LAYERS, depth, 2, 2, n_rows, C_LAYER), F32),
            jax.ShapeDtypeStruct((8, 128), F32),
        ),
        in_specs=[vmem] * 3,
        out_specs=(vmem,) * 3,
        scratch_shapes=[
            pltpu.VMEM((LAYERS + 1, blocks, res, D), F32),
            pltpu.VMEM((LAYERS, blocks, res, D), F32),
            pltpu.VMEM((LAYERS, blocks, res, HEAD), BF),
            pltpu.VMEM((LAYERS, blocks + 1, group, res, 2 * HEAD), BF),
            pltpu.VMEM((LAYERS, n_groups, side, 3 * HEAD), BF),
            pltpu.VMEM((LAYERS, blocks, res, 2 * STRIDE), BF),
            pltpu.VMEM((LAYERS, n_groups, side, side), BF),
            pltpu.VMEM((LAYERS, blocks, res, D), BF),
            pltpu.VMEM((LAYERS, blocks, res, FF), BF),
            pltpu.VMEM((LAYERS, blocks, res, FF), BF),
            pltpu.VMEM((blocks, res, 3 * HEAD), F32),
            pltpu.VMEM((blocks, res, HEAD), F32),
            pltpu.VMEM((blocks, res, HEAD), BF),
            pltpu.VMEM((blocks, res, HEAD), BF),
            pltpu.VMEM((blocks + 1, group, res, 2 * HEAD), F32),
            pltpu.VMEM((2, group - 1, blocks, res, 2 * HEAD), F32),
            pltpu.VMEM((blocks, res, D), F32),
            pltpu.VMEM((res, 128), F32),
            pltpu.VMEM((res, 128), F32),
            pltpu.VMEM((res, 128), F32),
            pltpu.VMEM((8, 128), F32),
            pltpu.VMEM((2, res, 2 * STRIDE), F32),
            pltpu.VMEM((side, side), F32),
            pltpu.VMEM((16, 1, D), F32),
            pltpu.VMEM((2 * NORMS, 8, D), F32),
            pltpu.VMEM((128, D), F32),
            pltpu.SemaphoreType.DMA((group - 1,)),
            pltpu.SemaphoreType.DMA((2 * LAYERS, group - 1)),
        ],
        compiler_params=pltpu.CompilerParams(
            collective_id=1, has_side_effects=True, vmem_limit_bytes=VMEM_LIMIT
        ),
        name="step",
    )(px, rest, layers)

    def both(lead, dtype):
        return [
            pltpu.VMEM((*lead, n_rows, C_REST), dtype),
            pltpu.VMEM((LAYERS, *lead, n_rows, C_LAYER), dtype),
        ]

    stat = jax.ShapeDtypeStruct((8, 128), F32)
    shapes = [jax.ShapeDtypeStruct(item.shape, F32) for item in masters]
    m = geo.m
    outs = pl.pallas_call(
        functools.partial(update_kernel, geo),
        out_shape=[stat] + shapes * 3,
        in_specs=[vmem] * 27,
        out_specs=[vmem] * 25,
        scratch_shapes=[
            *both((depth, 2), BF), *both((depth, 2), BF),
            *both((depth,), BF), *both((depth,), BF),
            *both((depth,), BF), *both((depth - 1,), BF),
            *both((m,), BF), *both((), F32),
            pltpu.VMEM((m, 8, 128), F32),
            pltpu.VMEM((2, 8, 128), F32),
            pltpu.VMEM((2, 8, 128), F32),
            pltpu.VMEM((depth, 8, 128), F32),
            pltpu.VMEM((8, 128), F32),
            pltpu.SemaphoreType.DMA((1 + LAYERS, depth + m)),
            pltpu.SemaphoreType.DMA((1 + LAYERS, depth + m)),
            pltpu.SemaphoreType.DMA((m + depth,)),
            pltpu.SemaphoreType.DMA((m + depth,)),
        ],
        compiler_params=pltpu.CompilerParams(
            collective_id=2, has_side_effects=True, vmem_limit_bytes=VMEM_LIMIT
        ),
        name="update",
    )(g_rest, g_layers, stats, *masters, *firsts, *seconds)
    totals = outs[0]
    return (
        totals[0, 0],
        totals[1, 0],
        totals[2, 0],
        *unpacked(*outs[1:9]),
        *unpacked(*outs[9:17]),
        *unpacked(*outs[17:25]),
    )


def solution(mesh):
    pixels = P("img", None, "seq")
    weights = (
        P(None, "seq"),
        P(None, "seq"),
        P(None, "seq", None),
        P(None, "seq", None),
        P(None, "seq", None),
        P(None, None, "seq"),
        P("seq", None),
        P(None, None, "seq"),
    )

    def body(pixels, loss_mask, *rest):
        geo = Geometry(mesh.shape["seq"], mesh.shape["img"], pixels.shape[0], pixels.shape[1])
        return on_device(geo, pixels, loss_mask, *rest)

    return jax.shard_map(
        body,
        mesh=mesh,
        in_specs=(pixels, pixels) + weights * 3,
        out_specs=(P(), P(), P()) + weights * 3,
        check_vma=False,
    )
```

```python
import functools
import math

import jax
import jax.numpy as jnp
from jax import lax
from jax.experimental import pallas as pl
from jax.experimental.pallas import tpu as pltpu
from jax.sharding import PartitionSpec as P

D = 256
HEAD = 128
FF = 512
V = 256
STRIDE = 128
LAYERS = 3
NORMS = 2 * LAYERS + 1
STEP = 10
SIDE = 32
POS = 2 * SIDE + 3
CLIP_NORM = 0.05
BETA_ONE = 0.9
BETA_TWO = 0.95
LEARN_RATE = 0.1
WEIGHT_DECAY = 0.1
ADAM_EPS = 1e-08
SMOOTHING = 0.1
NORM_EPS = 1e-05
SCALE = HEAD ** (-0.5)

C_IN, C_OUT, C_UP, C_DOWN = (0, 768), (768, 1024), (1024, 1536), (1536, 2048)
C_LAYER = 2048
C_TOK, C_POS, C_NORM, C_HEAD = (0, 256), (256, 384), (384, 512), (512, 768)
C_REST = 768
C_ALL = LAYERS * C_LAYER + C_REST

BF = jnp.bfloat16
F32 = jnp.float32
VMEM_LIMIT = 64 * 1024 * 1024


def dot(a, b):
    return lax.dot_general(a, b, (((1,), (0,)), ((), ())), preferred_element_type=F32)


def dot_nt(a, b):
    return lax.dot_general(a, b, (((1,), (1,)), ((), ())), preferred_element_type=F32)


def dot_tn(a, b):
    return lax.dot_general(a, b, (((0,), (0,)), ((), ())), preferred_element_type=F32)


class Geometry:
    def __init__(self, n, m, images, blocks):
        self.n, self.m, self.images, self.blocks = n, m, images, blocks
        self.depth = n // 4
        self.rows = D // n
        self.group = n // images
        self.res = STRIDE // self.group
        self.own = STRIDE // n
        self.wide = -(-images * blocks // 128) * 128

    def place(self):
        me = lax.axis_index("seq")
        return me // 4, me // 2 % 2, me % 2


def seq_id(z, y, core):
    return {"seq": z * 4 + y * 2 + core}


def greet(devices):
    barrier = pltpu.get_barrier_semaphore()
    for device in devices:
        pl.semaphore_signal(barrier, inc=1, device_id=device, device_id_type=pl.DeviceIdType.MESH)
    pl.semaphore_wait(barrier, len(devices))


def push(src, dst, send_sem, recv_sem, device):
    return pltpu.make_async_remote_copy(
        src_ref=src,
        dst_ref=dst,
        send_sem=send_sem,
        recv_sem=recv_sem,
        device_id=device,
        device_id_type=pl.DeviceIdType.MESH,
    )


def normalise(x):
    centre = x - jnp.mean(x, -1, keepdims=True)
    spread = jnp.mean(centre * centre, -1, keepdims=True)
    rstd = lax.rsqrt(spread + NORM_EPS)
    return centre * rstd, rstd


def fold(x):
    return jnp.sum(x.reshape(x.shape[0] // 8, 8, x.shape[1]), 0)


def normalise_back(dy, unit, rstd, gain):
    dxh = dy * (1.0 + gain)
    mean_one = jnp.mean(dxh, -1, keepdims=True)
    mean_two = jnp.mean(dxh * unit, -1, keepdims=True)
    return rstd * (dxh - mean_one - unit * mean_two), fold(dy * unit), fold(dy)


def gelu_both(u):
    c = math.sqrt(2.0 / math.pi)
    square = u * u
    t = jnp.tanh(c * u * (1.0 + 0.044715 * square))
    half = 0.5 * (1.0 + t)
    slope = half + 0.5 * u * (1.0 - t * t) * (c * (1.0 + 3.0 * 0.044715 * square))
    return u * half, slope


def softmax(scores):
    e = jnp.exp(scores - jnp.max(scores, -1, keepdims=True))
    return e * (1.0 / jnp.sum(e, -1, keepdims=True))


def step_kernel(
    geo, chunk, batch,
    pixels, mask, tok, pos, w_in, w_out, w_up, w_down, head, norms,
    sums, totals,
    px, rest, layers, g_rest, g_layers,
    x_s, x1_s, q0_s, kv_s, qkv1_s, p0_s, p1_s, o_s, a_s, slope_s, stage, o1_s, do0_s, dq0_s,
    own_s, away_s, back_s, edge_s, dx_s, ids_s, tgt_s, msk_s, prev_s, pack_s, bias0, bias1, norm_s, gnorm, wide,
    s1, r1, s2, r2, s3, r3, r4, st_img, st_core, st_y, st_z,
    g_send, g_recv, kv_send, kv_recv, rs_send, rs_recv, st_send, st_recv,
):
    z, y, core = geo.place()
    me, x_img = lax.axis_index("seq"), lax.axis_index("img")
    depth, group, res, blocks, own, m = geo.depth, geo.group, geo.res, geo.blocks, geo.own, geo.m
    image, part = me // group, me % group
    siblings = [{"seq": image * group + lax.rem(part + k, group)} for k in range(1, group)]
    peers = [seq_id(lax.rem(z + k, depth), y, core) for k in range(1, depth)]
    beside, sibling = seq_id(z, 1 - y, core), seq_id(z, y, 1 - core)
    across = [{"img": lax.rem(x_img + k, m)} for k in range(1, m)]
    rows = chunk * res
    chunks = blocks // chunk
    n_groups = res // 8
    every, pair = pl.ds(0, depth), pl.ds(0, 2)

    rest[z, y, core, :, C_TOK[0] : C_TOK[1]] = tok[...].astype(BF)
    wide[...] = jnp.zeros_like(wide)
    wide[: geo.rows, :POS] = pos[...]
    rest[z, y, core, :, C_POS[0] : C_POS[1]] = wide[: geo.rows, :128].astype(BF)
    wide[...] = jnp.zeros_like(wide)
    for i in range(NORMS):
        wide[2 * i : 2 * i + 2, : geo.rows] = norms[i]
    rest[z, y, core, :, C_NORM[0] : C_NORM[1]] = jnp.transpose(wide[:, :128])[: geo.rows].astype(BF)
    rest[z, y, core, :, C_HEAD[0] : C_HEAD[1]] = head[...].astype(BF)
    for l in range(LAYERS):
        layers[l, z, y, core, :, C_IN[0] : C_IN[1]] = w_in[l].astype(BF)
        layers[l, z, y, core, :, C_OUT[0] : C_OUT[1]] = w_out[l].astype(BF)
        layers[l, z, y, core, :, C_UP[0] : C_UP[1]] = w_up[l].astype(BF)
        layers[l, z, y, core, :, C_DOWN[0] : C_DOWN[1]] = w_down[l].astype(BF)
    pack_s[...] = jnp.zeros_like(pack_s)
    pack_s[:, :own, :blocks] = pixels[...].astype(F32)
    pack_s[:, own:, :blocks] = mask[...].astype(F32)
    at = lax.broadcasted_iota(jnp.int32, (128, geo.wide), 0)
    to = lax.broadcasted_iota(jnp.int32, (128, geo.wide), 1)
    packed = jnp.zeros((2 * own, geo.wide), F32)
    for i in range(geo.images):
        spot = ((to == at + i * blocks) & (at < blocks)).astype(F32).astype(BF)
        packed = packed + dot(pack_s[i].astype(BF), spot)
    px[z, y, core] = packed.astype(BF)

    others = peers + [beside] + across
    others = others + (siblings if group > 2 else [sibling])
    if group > 2:
        others = [d for d in others if d is not beside]
    greet(others)

    parts = [px, rest.at[..., 0 : C_NORM[1]], layers.at[0, ..., 0 : C_IN[1]], layers.at[0, ..., C_OUT[0] : C_LAYER]]
    parts += [layers.at[1], rest.at[..., C_HEAD[0] : C_HEAD[1]], layers.at[2]]

    def gather_z(a, k):
        mine = parts[a].at[z, y, core]
        return push(mine, mine, g_send.at[a, k], g_recv.at[a, k], peers[k])

    def gather_y(a):
        column = parts[a].at[every, y, core]
        return push(column, column, g_send.at[a, depth - 1], g_recv.at[a, depth - 1], beside)

    def gather_core(a):
        half = parts[a].at[every, pair, core]
        return push(half, half, g_send.at[a, depth], g_recv.at[a, depth], sibling)

    def to_y(a):
        for k in range(depth - 1):
            gather_z(a, k).wait_recv()
        gather_y(a).start()

    def to_core(a):
        gather_y(a).wait_recv()
        gather_core(a).start()

    def arrived(a):
        gather_core(a).wait_recv()

    for a in range(len(parts)):
        for k in range(depth - 1):
            gather_z(a, k).start()

    def table(ref, cols):
        piece = ref[..., cols[0] : cols[1]]
        width = cols[1] - cols[0]
        if geo.rows % 16:
            return piece.astype(F32).reshape(D, width).astype(BF)
        return piece.reshape(D, width)

    def layer_table(l, cols):
        return table(layers.at[l], cols)

    def add_to(ref, cols, value):
        shape = (depth, 2, 2, geo.rows, cols[1] - cols[0])
        ref[..., cols[0] : cols[1]] += value.reshape(shape)

    for ref in (ids_s, tgt_s, msk_s, prev_s, wide, g_rest, g_layers, gnorm):
        ref[...] = jnp.zeros_like(ref)
    for l in range(LAYERS):
        kv_s[l, 0] = jnp.zeros((group, res, 2 * HEAD), BF)

    qi = part * res + lax.broadcasted_iota(jnp.int32, (res, 2 * STRIDE), 0)
    kj = lax.broadcasted_iota(jnp.int32, (res, 2 * STRIDE), 1)
    kj = kj // STRIDE * STRIDE + (kj % STRIDE + part * res) % STRIDE
    seen = (kj > qi) & (kj <= qi + STRIDE)
    bias0[0] = jnp.where(seen & (kj >= STRIDE), 0.0, -1e30)
    bias0[1] = jnp.where(seen, 0.0, -1e30)
    side = 8 * blocks
    ri = lax.broadcasted_iota(jnp.int32, (side, side), 0)
    ci = lax.broadcasted_iota(jnp.int32, (side, side), 1)
    bias1[...] = jnp.where(((ri & 7) == (ci & 7)) & (ri >= ci), 0.0, -1e30)

    to_y(0)
    to_y(1)
    to_y(2)
    to_core(0)
    to_core(1)
    to_y(3)
    to_core(2)
    arrived(0)

    span = depth // group
    at = lax.broadcasted_iota(jnp.int32, (geo.wide, 128), 0)
    to = lax.broadcasted_iota(jnp.int32, (geo.wide, 128), 1)
    spot = ((at == to + image * blocks) & (to < blocks)).astype(F32).astype(BF)
    for j in range(geo.images):
        piece = dot(px[part * span + j // 4, j // 2 % 2, j % 2], spot)
        tgt_s[j * own : (j + 1) * own, :] = piece[:own]
        msk_s[j * own : (j + 1) * own, :] = piece[own:]
    prev = dot(px[lax.rem(part * span + depth - 1, depth), 1, 1], spot)[:own]
    lane = lax.broadcasted_iota(jnp.int32, prev.shape, 1)
    moved = jnp.where(lane == 0, -1.0, pltpu.roll(prev, 1, 1))
    prev = jnp.where(part == 0, moved, prev)
    ids_s[0:1, :] = prev[own - 1 : own, :]
    ids_s[1:res, :] = tgt_s[0 : res - 1, :]

    arrived(1)
    norm_s[...] = jnp.transpose(table(rest, C_NORM).astype(F32))[:16].reshape(16, 1, D)

    def spread(ref, b0):
        values = ref[...].astype(BF)
        at = lax.broadcasted_iota(jnp.int32, (128, 128), 0)
        return jnp.concatenate(
            [dot(values, (at == b0 + j).astype(F32).astype(BF)) for j in range(chunk)], 0
        )

    def one_hot(ref, b0):
        value = spread(ref, b0)
        lane = lax.broadcasted_iota(jnp.int32, (rows, 128), 1).astype(F32)
        return jnp.concatenate([(value == lane).astype(F32), (value == lane + 128.0).astype(F32)], 1)

    def place_hot(b0):
        r = lax.broadcasted_iota(jnp.int32, (rows, 128), 0)
        lane = lax.broadcasted_iota(jnp.int32, (rows, 128), 1).astype(F32)
        p = ((b0 + r // res) * STRIDE + part * res + r % res).astype(F32)
        third = jnp.floor((p + 0.5) * (1.0 / 3.0))
        line = jnp.floor((third + 0.5) * (1.0 / SIDE))
        hits = (lane == line) | (lane == SIDE + third - SIDE * line)
        return (hits | (lane == 2 * SIDE + p - 3.0 * third)).astype(F32)

    def loop(count, body):
        lax.fori_loop(0, count, lambda i, carry: (body(i), carry)[1], 0)

    def embed(i):
        b0 = i * chunk
        hot = jnp.concatenate([one_hot(ids_s, b0), place_hot(b0)], 1).astype(BF)
        x = dot_nt(hot, table(rest, (C_TOK[0], C_POS[1])))
        x_s[0, pl.ds(b0, chunk)] = x.reshape(chunk, res, D)

    loop(chunks, embed)

    def exchange(l, k):
        mine = kv_s.at[l, pl.ds(1, blocks), 0]
        there = kv_s.at[l, pl.ds(1, blocks), group - 1 - k]
        return push(mine, there, kv_send.at[k], kv_recv.at[l, k], siblings[k])

    def forward(l):
        def mix(i):
            b0 = i * chunk
            at = pl.ds(b0, chunk)
            unit, _ = normalise(x_s[l, at].reshape(rows, D))
            h = (unit * (1.0 + norm_s[4 * l]) + norm_s[4 * l + 1]).astype(BF)
            qkv = dot(h, layer_table(l, C_IN)).reshape(chunk, res, 6 * HEAD)
            q0_s[l, at] = qkv[..., :HEAD].astype(BF)
            kv_s[l, pl.ds(b0 + 1, chunk), 0, :, :HEAD] = qkv[..., 2 * HEAD : 3 * HEAD].astype(BF)
            kv_s[l, pl.ds(b0 + 1, chunk), 0, :, HEAD:] = qkv[..., 4 * HEAD : 5 * HEAD].astype(BF)
            stage[at, :, :HEAD] = qkv[..., HEAD : 2 * HEAD]
            stage[at, :, HEAD : 2 * HEAD] = qkv[..., 3 * HEAD : 4 * HEAD]
            stage[at, :, 2 * HEAD :] = qkv[..., 5 * HEAD :]

        def strided(g):
            at = pl.ds(pl.multiple_of(8 * g, 8), 8)
            qkv = stage[:, at, :].reshape(8 * blocks, 3 * HEAD).astype(BF)
            qkv1_s[l, g] = qkv
            scores = dot_nt(qkv[:, :HEAD], qkv[:, HEAD : 2 * HEAD]) * SCALE + bias1[...]
            probs = softmax(scores).astype(BF)
            p1_s[l, g] = probs
            o1_s[:, at, :] = dot(probs, qkv[:, 2 * HEAD :]).reshape(blocks, 8, HEAD)

        def window(i):
            b0 = i * batch
            kv = kv_s[l, pl.ds(b0, batch + 1)].reshape((batch + 1) * STRIDE, 2 * HEAD)
            raw = [
                dot_nt(q0_s[l, b0 + j], kv[j * STRIDE : (j + 2) * STRIDE, :HEAD]) * SCALE
                + bias0[jnp.minimum(b0 + j, 1)]
                for j in range(batch)
            ]
            probs = softmax(jnp.concatenate(raw, 0)).astype(BF)
            p0_s[l, pl.ds(b0, batch)] = probs.reshape(batch, res, 2 * STRIDE)
            for j in range(batch):
                value = dot(probs[j * res : (j + 1) * res], kv[j * STRIDE : (j + 2) * STRIDE, HEAD:])
                o_s[l, b0 + j, :, :HEAD] = value.astype(BF)

        def feed(i):
            b0 = i * chunk
            at = pl.ds(b0, chunk)
            o_s[l, at, :, HEAD:] = o1_s[at].astype(BF)
            x1 = x_s[l, at].reshape(rows, D) + dot(o_s[l, at].reshape(rows, D), layer_table(l, C_OUT))
            x1_s[l, at] = x1.reshape(chunk, res, D)
            unit, _ = normalise(x1)
            h = (unit * (1.0 + norm_s[4 * l + 2]) + norm_s[4 * l + 3]).astype(BF)
            a, slope = gelu_both(dot(h, layer_table(l, C_UP)))
            a = a.astype(BF)
            a_s[l, at] = a.reshape(chunk, res, FF)
            slope_s[l, at] = slope.astype(BF).reshape(chunk, res, FF)
            x2 = x1 + dot_nt(a, layer_table(l, C_DOWN))
            x_s[l + 1, at] = x2.reshape(chunk, res, D)

        arrived((2, 4, 6)[l])
        loop(chunks, mix)
        copies = [exchange(l, k) for k in range(group - 1)]
        for copy in copies:
            copy.start()
        if l == 0:
            to_core(3)
            to_y(4)
        if l == 1:
            to_core(5)
            to_core(6)
        loop(n_groups, strided)
        for copy in copies:
            copy.wait()
        loop(blocks // batch, window)
        if l == 0:
            arrived(3)
            to_y(5)
        loop(chunks, feed)
        if l == 0:
            to_core(4)
            to_y(6)

    for l in range(LAYERS):
        forward(l)
    arrived(5)

    def finish(i, loss):
        b0 = i * chunk
        at = pl.ds(b0, chunk)
        unit, rstd = normalise(x_s[LAYERS, at].reshape(rows, D))
        gain = norm_s[4 * LAYERS]
        h = (unit * (1.0 + gain) + norm_s[4 * LAYERS + 1]).astype(BF)
        table_head = table(rest, C_HEAD)
        logits = dot(h, table_head)
        hot = one_hot(tgt_s, b0)
        shift = logits - jnp.max(logits, -1, keepdims=True)
        e = jnp.exp(shift)
        total = jnp.sum(e, -1, keepdims=True)
        weight = spread(msk_s, b0)
        per = (
            jnp.log(total)
            - (1.0 - SMOOTHING) * jnp.sum(hot * shift, -1, keepdims=True)
            - SMOOTHING * jnp.mean(shift, -1, keepdims=True)
        )
        loss = loss + jnp.sum(weight[:, :1] * per, 0, keepdims=True)
        weight = jnp.concatenate([weight, weight], 1)
        d_logits = weight * (e * (1.0 / total) - (1.0 - SMOOTHING) * hot - SMOOTHING / V)
        d_logits = d_logits.astype(BF)
        add_to(g_rest, C_HEAD, dot_tn(h, d_logits))
        dx, g_gain, g_bias = normalise_back(dot_nt(d_logits, table_head), unit, rstd, gain)
        gnorm[4 * LAYERS] += g_gain
        gnorm[4 * LAYERS + 1] += g_bias
        dx_s[at] = dx.reshape(chunk, res, D)
        return loss

    loss = lax.fori_loop(0, chunks, finish, jnp.zeros((1, 1), F32))
    count = jnp.sum(jnp.sum(msk_s[...], 0, keepdims=True), 1, keepdims=True)
    line = lax.broadcasted_iota(jnp.int32, (8, 128), 0)
    st_img[x_img] = jnp.where(line == 0, loss, jnp.where(line == 1, count, 0.0))
    st_across = [
        push(st_img.at[x_img], st_img.at[x_img], st_send.at[k], st_recv.at[k], across[k]) for k in range(m - 1)
    ]
    for copy in st_across:
        copy.start()

    def give(l, k):
        return push(
            away_s.at[k, pl.ds(1, blocks)], back_s.at[l % 2, k], kv_send.at[k], kv_recv.at[LAYERS + l, k], siblings[k]
        )

    def backward(l, after_feed, after_window, after_strided):
        grads = g_layers.at[l % 2]

        def feed(i):
            b0 = i * chunk
            at = pl.ds(b0, chunk)
            dx2 = dx_s[at].reshape(rows, D)
            g2 = dx2.astype(BF)
            a = a_s[l, at].reshape(rows, FF)
            add_to(grads, C_DOWN, dot_tn(g2, a))
            du = slope_s[l, at].reshape(rows, FF).astype(F32) * dot(g2, layer_table(l, C_DOWN))
            du = du.astype(BF)
            unit, rstd = normalise(x1_s[l, at].reshape(rows, D))
            gain = norm_s[4 * l + 2]
            h = (unit * (1.0 + gain) + norm_s[4 * l + 3]).astype(BF)
            add_to(grads, C_UP, dot_tn(h, du))
            dh = dot_nt(du, layer_table(l, C_UP))
            dx, g_gain, g_bias = normalise_back(dh, unit, rstd, gain)
            gnorm[4 * l + 2] += g_gain
            gnorm[4 * l + 3] += g_bias
            dx = dx + dx2
            dx_s[at] = dx.reshape(chunk, res, D)
            g1 = dx.astype(BF)
            add_to(grads, C_OUT, dot_tn(o_s[l, at].reshape(rows, D), g1))
            do = dot_nt(g1, layer_table(l, C_OUT)).reshape(chunk, res, D)
            do0_s[at] = do[..., :HEAD].astype(BF)
            o1_s[at] = do[..., HEAD:]

        def window(i):
            b0 = i * batch
            at = pl.ds(b0, batch)
            kv = kv_s[l, pl.ds(b0, batch + 1)].reshape((batch + 1) * STRIDE, 2 * HEAD)
            probs = p0_s[l, at].reshape(batch * res, 2 * STRIDE)
            do = [do0_s[b0 + j] for j in range(batch)]
            keys = [kv[j * STRIDE : (j + 2) * STRIDE, :HEAD] for j in range(batch)]
            dp = jnp.concatenate(
                [dot_nt(do[j], kv[j * STRIDE : (j + 2) * STRIDE, HEAD:]) for j in range(batch)], 0
            )
            wide_p = probs.astype(F32)
            ds = (wide_p * (dp - jnp.sum(wide_p * dp, -1, keepdims=True)) * SCALE).astype(BF)
            carry = edge_s[...]
            for j in range(batch):
                cut = slice(j * res, (j + 1) * res)
                dq0_s[b0 + j] = dot(ds[cut], keys[j]).astype(BF)
                dkv = jnp.concatenate([dot_tn(ds[cut], q0_s[l, b0 + j]), dot_tn(probs[cut], do[j])], 1)
                done = (carry + dkv[:STRIDE]).reshape(group, res, 2 * HEAD)
                own_s[b0 + j] = done[0]
                for k in range(group - 1):
                    away_s[k, b0 + j] = done[k + 1].astype(BF)
                carry = dkv[STRIDE:]
            edge_s[...] = carry

        def strided(g):
            at = pl.ds(pl.multiple_of(8 * g, 8), 8)
            qkv = qkv1_s[l, g]
            probs = p1_s[l, g]
            do = o1_s[:, at, :].reshape(8 * blocks, HEAD).astype(BF)
            dp = dot_nt(do, qkv[:, 2 * HEAD :])
            wide_p = probs.astype(F32)
            ds = (wide_p * (dp - jnp.sum(wide_p * dp, -1, keepdims=True)) * SCALE).astype(BF)
            dq = dot(ds, qkv[:, HEAD : 2 * HEAD])
            dk = dot_tn(ds, qkv[:, :HEAD])
            dv = dot_tn(probs, do)
            stage[:, at, :] = jnp.concatenate([dq, dk, dv], 1).reshape(blocks, 8, 3 * HEAD)

        def mix(i):
            b0 = i * chunk
            at = pl.ds(b0, chunk)
            dkv = own_s[pl.ds(b0 + 1, chunk)]
            for k in range(group - 1):
                dkv = dkv + back_s[l % 2, k, at].astype(F32)
            d1 = stage[at]
            dqkv = jnp.concatenate(
                [
                    dq0_s[at],
                    d1[..., :HEAD].astype(BF),
                    dkv[..., :HEAD].astype(BF),
                    d1[..., HEAD : 2 * HEAD].astype(BF),
                    dkv[..., HEAD:].astype(BF),
                    d1[..., 2 * HEAD :].astype(BF),
                ],
                -1,
            ).reshape(rows, 6 * HEAD)
            unit, rstd = normalise(x_s[l, at].reshape(rows, D))
            gain = norm_s[4 * l]
            h = (unit * (1.0 + gain) + norm_s[4 * l + 1]).astype(BF)
            add_to(grads, C_IN, dot_tn(h, dqkv))
            dh = dot_nt(dqkv, layer_table(l, C_IN))
            dx, g_gain, g_bias = normalise_back(dh, unit, rstd, gain)
            gnorm[4 * l] += g_gain
            gnorm[4 * l + 1] += g_bias
            dx_s[at] += dx.reshape(chunk, res, D)

        loop(chunks, feed)
        after_feed()
        edge_s[...] = jnp.zeros_like(edge_s)
        loop(blocks // batch, window)
        last = edge_s[...].reshape(group, res, 2 * HEAD)
        own_s[blocks] = last[0]
        for k in range(group - 1):
            away_s[k, blocks] = last[k + 1].astype(BF)
        copies = [give(l, k) for k in range(group - 1)]
        for copy in copies:
            copy.start()
        after_window()
        loop(n_groups, strided)
        after_strided()
        for copy in copies:
            copy.wait()
        loop(chunks, mix)

    def section(index, ref, cols, base):
        width = cols[1] - cols[0]
        cut = slice(base, base + width)
        grad = ref.at[..., cols[0] : cols[1]]
        first = push(s1.at[..., cut], r1.at[..., cut], rs_send.at[index, 0], rs_recv.at[index, 0], sibling)
        second = push(s2.at[..., cut], r2.at[..., cut], rs_send.at[index, 1], rs_recv.at[index, 1], beside)
        third = [
            push(
                s3.at[lax.rem(z + k, depth), :, cut],
                r3.at[k - 1, :, cut],
                rs_send.at[index, 1 + k],
                rs_recv.at[index, 1 + k],
                peers[k - 1],
            )
            for k in range(1, depth)
        ]
        fourth = [
            push(
                r4.at[x_img, :, cut],
                r4.at[x_img, :, cut],
                rs_send.at[index, depth + 1 + k],
                rs_recv.at[index, depth + 1 + k],
                across[k],
            )
            for k in range(m - 1)
        ]

        def go_core():
            s1[..., cut] = grad[every, pair, 1 - core].astype(BF)
            first.start()

        def go_y():
            first.wait()
            total = grad[every, 1 - y, core] + r1[every, 1 - y, :, cut].astype(F32)
            s2[..., cut] = total.astype(BF)
            second.start()

        def go_z():
            second.wait()
            total = grad[every, y, core] + r1[every, y, :, cut].astype(F32) + r2[..., cut].astype(F32)
            s3[..., cut] = total.astype(BF)
            for copy in third:
                copy.start()

        def go_img():
            for copy in third:
                copy.wait()
            total = s3[z, :, cut].astype(F32)
            for k in range(1, depth):
                total = total + r3[k - 1, :, cut].astype(F32)
            r4[x_img, :, cut] = total.astype(BF)
            for copy in fourth:
                copy.start()

        def end():
            for copy in fourth:
                copy.wait()
            total = r4[0, :, cut].astype(F32)
            for k in range(1, m):
                total = total + r4[k, :, cut].astype(F32)
            sums[:, cut] = total
            return jnp.sum(jnp.sum(total * total, 0, keepdims=True), 1, keepdims=True)

        return go_core, go_y, go_z, go_img, end

    two = section(0, g_layers.at[0], (0, C_LAYER), 2 * C_LAYER)
    one = section(1, g_layers.at[1], (0, C_LAYER), C_LAYER)
    zero_rest = section(2, g_layers.at[0], (C_OUT[0], C_LAYER), C_OUT[0])
    zero_in = section(3, g_layers.at[0], C_IN, 0)
    other = section(4, g_rest, (0, C_REST), LAYERS * C_LAYER)

    def run(*steps):
        def inner():
            for step in steps:
                step()

        return inner

    nothing = run()
    backward(2, nothing, nothing, nothing)
    two[0]()
    backward(1, two[1], two[2], two[3])
    squares = two[4]()
    one[0]()
    g_layers[0] = jnp.zeros(g_layers.shape[1:], F32)
    backward(0, run(zero_rest[0], one[1]), run(zero_rest[1], one[2]), run(zero_rest[2], one[3]))
    zero_in[0]()
    zero_rest[3]()
    squares = squares + one[4]()

    def embed_back(i):
        b0 = i * chunk
        hot = jnp.concatenate([one_hot(ids_s, b0), place_hot(b0)], 1).astype(BF)
        dx = dx_s[pl.ds(b0, chunk)].reshape(rows, D)
        high = dx.astype(BF)
        low = (dx - high.astype(F32)).astype(BF)
        add_to(g_rest, (C_TOK[0], C_POS[1]), dot_tn(high, hot) + dot_tn(low, hot))

    loop(chunks, embed_back)
    for i in range(2 * NORMS):
        wide[i : i + 1, :] = jnp.sum(gnorm[i], 0, keepdims=True)
    add_to(g_rest, C_NORM, jnp.transpose(wide[...]))
    other[0]()
    zero_in[1]()
    other[1]()
    zero_in[2]()
    other[2]()
    squares = squares + zero_rest[4]()
    zero_in[3]()
    other[3]()
    squares = squares + zero_in[4]()
    squares = squares + other[4]()

    for copy in st_across:
        copy.wait()
    told = st_img[0]
    for k in range(1, m):
        told = told + st_img[k]
    told = jnp.where(line == 2, squares, told)
    base = m - 1

    def swap(told, buffer, index, where, device):
        buffer[where] = told
        copy = push(buffer.at[where], buffer.at[where], st_send.at[base + index], st_recv.at[base + index], device)
        copy.start()
        copy.wait()
        return buffer[0] + buffer[1]

    told = swap(told, st_core, 0, core, sibling)
    told = swap(told, st_y, 1, y, beside)
    st_z[z] = told
    copies = [
        push(st_z.at[z], st_z.at[z], st_send.at[base + 1 + k], st_recv.at[base + 1 + k], peers[k - 1])
        for k in range(1, depth)
    ]
    for copy in copies:
        copy.start()
    for a in range(len(parts)):
        for k in range(depth - 1):
            gather_z(a, k).wait_send()
        gather_y(a).wait_send()
        gather_core(a).wait_send()
    for copy in copies:
        copy.wait()
    told = st_z[0]
    for k in range(1, depth):
        told = told + st_z[k]
    count = told[1:2, :1]
    norm = jnp.sqrt(told[2:3, :1]) / count
    factor = jnp.minimum(1.0, CLIP_NORM / norm) / count
    totals[...] = jnp.where(line == 2, norm, jnp.where(line == 3, factor, told))


def adam(master, gradient, first, second):
    first = BETA_ONE * first + (1.0 - BETA_ONE) * gradient
    second = BETA_TWO * second + (1.0 - BETA_TWO) * gradient * gradient
    moved = first / (1.0 - BETA_ONE**STEP) / (jnp.sqrt(second / (1.0 - BETA_TWO**STEP)) + ADAM_EPS)
    return master - LEARN_RATE * (moved + WEIGHT_DECAY * master), first, second


def update_kernel(rows, *refs):
    sums, totals = refs[:2]
    masters, firsts, seconds = refs[2:10], refs[10:18], refs[18:26]
    outs = (refs[26:34], refs[34:42], refs[42:50])
    turned = refs[50]
    factor = totals[3:4, :1]

    def put(index, at, gradient):
        result = adam(masters[index][at], gradient * factor, firsts[index][at], seconds[index][at])
        for k in range(3):
            outs[k][index][at] = result[k]

    base = LAYERS * C_LAYER
    put(0, ..., sums[:, base + C_TOK[0] : base + C_TOK[1]])
    put(1, ..., sums[:, base + C_POS[0] : base + C_POS[0] + POS])
    put(6, ..., sums[:, base + C_HEAD[0] : base + C_HEAD[1]])
    turned[...] = jnp.transpose(sums[:, base + C_NORM[0] : base + C_NORM[1]])
    for i in range(NORMS):
        put(7, i, turned[2 * i : 2 * i + 2, :])
    for l in range(LAYERS):
        for index, cols in ((2, C_IN), (3, C_OUT), (4, C_UP), (5, C_DOWN)):
            put(index, l, sums[:, l * C_LAYER + cols[0] : l * C_LAYER + cols[1]])


def turned(tok, pos, w_in, w_out, w_up, w_down, head, norms):
    return (tok.T, pos.T, w_in, w_out, w_up, jnp.swapaxes(w_down, 1, 2), head, norms)


def on_device(geo, pixels, loss_mask, *weights):
    masters, firsts, seconds = (turned(*weights[k : k + 8]) for k in (0, 8, 16))
    n_rows, depth, blocks, res, group = geo.rows, geo.depth, geo.blocks, geo.res, geo.group
    m = geo.m
    vmem = pl.BlockSpec(memory_space=pltpu.VMEM)
    chunk = 4
    batch = 4
    n_groups = res // 8
    side = 8 * blocks
    sums, totals = pl.pallas_call(
        functools.partial(step_kernel, geo, chunk, batch),
        out_shape=(
            jax.ShapeDtypeStruct((n_rows, C_ALL), F32),
            jax.ShapeDtypeStruct((8, 128), F32),
        ),
        in_specs=[vmem] * 10,
        out_specs=(vmem,) * 2,
        scratch_shapes=[
            pltpu.VMEM((depth, 2, 2, 2 * geo.own, geo.wide), BF),
            pltpu.VMEM((depth, 2, 2, n_rows, C_REST), BF),
            pltpu.VMEM((LAYERS, depth, 2, 2, n_rows, C_LAYER), BF),
            pltpu.VMEM((depth, 2, 2, n_rows, C_REST), F32),
            pltpu.VMEM((2, depth, 2, 2, n_rows, C_LAYER), F32),
            pltpu.VMEM((LAYERS + 1, blocks, res, D), F32),
            pltpu.VMEM((LAYERS, blocks, res, D), F32),
            pltpu.VMEM((LAYERS, blocks, res, HEAD), BF),
            pltpu.VMEM((LAYERS, blocks + 1, group, res, 2 * HEAD), BF),
            pltpu.VMEM((LAYERS, n_groups, side, 3 * HEAD), BF),
            pltpu.VMEM((LAYERS, blocks, res, 2 * STRIDE), BF),
            pltpu.VMEM((LAYERS, n_groups, side, side), BF),
            pltpu.VMEM((LAYERS, blocks, res, D), BF),
            pltpu.VMEM((LAYERS, blocks, res, FF), BF),
            pltpu.VMEM((LAYERS, blocks, res, FF), BF),
            pltpu.VMEM((blocks, res, 3 * HEAD), F32),
            pltpu.VMEM((blocks, res, HEAD), F32),
            pltpu.VMEM((blocks, res, HEAD), BF),
            pltpu.VMEM((blocks, res, HEAD), BF),
            pltpu.VMEM((blocks + 1, res, 2 * HEAD), F32),
            pltpu.VMEM((group - 1, blocks + 1, res, 2 * HEAD), BF),
            pltpu.VMEM((2, group - 1, blocks, res, 2 * HEAD), BF),
            pltpu.VMEM((STRIDE, 2 * HEAD), F32),
            pltpu.VMEM((blocks, res, D), F32),
            pltpu.VMEM((res, 128), F32),
            pltpu.VMEM((res, 128), F32),
            pltpu.VMEM((res, 128), F32),
            pltpu.VMEM((8, 128), F32),
            pltpu.VMEM((geo.images, 2 * geo.own, 128), F32),
            pltpu.VMEM((2, res, 2 * STRIDE), F32),
            pltpu.VMEM((side, side), F32),
            pltpu.VMEM((16, 1, D), F32),
            pltpu.VMEM((2 * NORMS, 8, D), F32),
            pltpu.VMEM((128, D), F32),
            pltpu.VMEM((depth, 2, n_rows, C_ALL), BF),
            pltpu.VMEM((depth, 2, n_rows, C_ALL), BF),
            pltpu.VMEM((depth, n_rows, C_ALL), BF),
            pltpu.VMEM((depth, n_rows, C_ALL), BF),
            pltpu.VMEM((depth, n_rows, C_ALL), BF),
            pltpu.VMEM((depth - 1, n_rows, C_ALL), BF),
            pltpu.VMEM((m, n_rows, C_ALL), BF),
            pltpu.VMEM((m, 8, 128), F32),
            pltpu.VMEM((2, 8, 128), F32),
            pltpu.VMEM((2, 8, 128), F32),
            pltpu.VMEM((depth, 8, 128), F32),
            pltpu.SemaphoreType.DMA((4 + LAYERS, depth + 1)),
            pltpu.SemaphoreType.DMA((4 + LAYERS, depth + 1)),
            pltpu.SemaphoreType.DMA((group - 1,)),
            pltpu.SemaphoreType.DMA((2 * LAYERS, group - 1)),
            pltpu.SemaphoreType.DMA((5, depth + m)),
            pltpu.SemaphoreType.DMA((5, depth + m)),
            pltpu.SemaphoreType.DMA((m + depth,)),
            pltpu.SemaphoreType.DMA((m + depth,)),
        ],
        compiler_params=pltpu.CompilerParams(
            collective_id=0, has_side_effects=True, vmem_limit_bytes=VMEM_LIMIT
        ),
        name="step",
    )(jnp.swapaxes(pixels, 1, 2), jnp.swapaxes(loss_mask, 1, 2), *masters)

    shapes = [jax.ShapeDtypeStruct(item.shape, F32) for item in masters]
    outs = pl.pallas_call(
        functools.partial(update_kernel, n_rows),
        out_shape=shapes * 3,
        in_specs=[vmem] * 26,
        out_specs=[vmem] * 24,
        scratch_shapes=[pltpu.VMEM((128, n_rows), F32)],
        name="update",
    )(sums, totals, *masters, *firsts, *seconds)
    return (
        totals[0, 0],
        totals[1, 0],
        totals[2, 0],
        *turned(*outs[:8]),
        *turned(*outs[8:16]),
        *turned(*outs[16:]),
    )


def solution(mesh):
    pixels = P("img", None, "seq")
    weights = (
        P(None, "seq"),
        P(None, "seq"),
        P(None, "seq", None),
        P(None, "seq", None),
        P(None, "seq", None),
        P(None, None, "seq"),
        P("seq", None),
        P(None, None, "seq"),
    )

    def body(pixels, loss_mask, *rest):
        geo = Geometry(mesh.shape["seq"], mesh.shape["img"], pixels.shape[0], pixels.shape[1])
        return on_device(geo, pixels, loss_mask, *rest)

    return jax.shard_map(
        body,
        mesh=mesh,
        in_specs=(pixels, pixels) + weights * 3,
        out_specs=(P(), P(), P()) + weights * 3,
        check_vma=False,
    )
```

```python
import functools
import math

import jax
import jax.numpy as jnp
from jax import lax
from jax.experimental import pallas as pl
from jax.experimental.pallas import tpu as pltpu
from jax.sharding import PartitionSpec as P

D = 256
HEAD = 128
FF = 512
V = 256
STRIDE = 128
LAYERS = 3
NORMS = 2 * LAYERS + 1
STEP = 10
SIDE = 32
POS = 2 * SIDE + 3
CLIP_NORM = 0.05
BETA_ONE = 0.9
BETA_TWO = 0.95
LEARN_RATE = 0.1
WEIGHT_DECAY = 0.1
ADAM_EPS = 1e-08
SMOOTHING = 0.1
NORM_EPS = 1e-05
SCALE = HEAD ** (-0.5)

C_IN, C_OUT, C_UP, C_DOWN = (0, 768), (768, 1024), (1024, 1536), (1536, 2048)
C_LAYER = 2048
C_TOK, C_POS, C_NORM, C_HEAD = (0, 256), (256, 384), (384, 512), (512, 768)
C_REST = 768
C_ALL = LAYERS * C_LAYER + C_REST

BF = jnp.bfloat16
F32 = jnp.float32
VMEM_LIMIT = 64 * 1024 * 1024


def dot(a, b):
    return lax.dot_general(a, b, (((1,), (0,)), ((), ())), preferred_element_type=F32)


def dot_nt(a, b):
    return lax.dot_general(a, b, (((1,), (1,)), ((), ())), preferred_element_type=F32)


def dot_tn(a, b):
    return lax.dot_general(a, b, (((0,), (0,)), ((), ())), preferred_element_type=F32)


class Geometry:
    def __init__(self, n, m, images, blocks):
        self.n, self.m, self.images, self.blocks = n, m, images, blocks
        self.depth = n // 4
        self.rows = D // n
        self.group = n // images
        self.res = STRIDE // self.group
        self.own = STRIDE // n
        self.wide = -(-images * blocks // 128) * 128

    def place(self):
        me = lax.axis_index("seq")
        return me // 4, me // 2 % 2, me % 2


def seq_id(z, y, core):
    return {"seq": z * 4 + y * 2 + core}


def greet(devices):
    barrier = pltpu.get_barrier_semaphore()
    for device in devices:
        pl.semaphore_signal(barrier, inc=1, device_id=device, device_id_type=pl.DeviceIdType.MESH)
    pl.semaphore_wait(barrier, len(devices))


def push(src, dst, send_sem, recv_sem, device):
    return pltpu.make_async_remote_copy(
        src_ref=src,
        dst_ref=dst,
        send_sem=send_sem,
        recv_sem=recv_sem,
        device_id=device,
        device_id_type=pl.DeviceIdType.MESH,
    )


def normalise(x):
    centre = x - jnp.mean(x, -1, keepdims=True)
    spread = jnp.mean(centre * centre, -1, keepdims=True)
    rstd = lax.rsqrt(spread + NORM_EPS)
    return centre * rstd, rstd


def fold(x):
    return jnp.sum(x.reshape(x.shape[0] // 8, 8, x.shape[1]), 0)


def normalise_back(dy, unit, rstd, gain):
    dxh = dy * (1.0 + gain)
    mean_one = jnp.mean(dxh, -1, keepdims=True)
    mean_two = jnp.mean(dxh * unit, -1, keepdims=True)
    return rstd * (dxh - mean_one - unit * mean_two), fold(dy * unit), fold(dy)


def gelu_both(u):
    c = math.sqrt(2.0 / math.pi)
    w = c + (0.044715 * c) * (u * u)
    half = 0.5 + 0.5 * jnp.tanh(u * w)
    a = u * half
    return a, half + a * (1.0 - half) * (6.0 * w - 4.0 * c)


def softmax(scores):
    e = jnp.exp(scores - jnp.max(scores, -1, keepdims=True))
    return e * (1.0 / jnp.sum(e, -1, keepdims=True))


def step_kernel(
    geo, chunk, batch, pack,
    pixels, mask, tok, pos, w_in, w_out, w_up, w_down, head, norms,
    sums, totals,
    px, rest, layers, g_rest, g_layers,
    x_s, x1_s, q0_s, kv_s, qkv1_s, p0_s, p1_s, o_s, a_s, slope_s, stage, o1_s, do0_s, dq0_s,
    away_s, back_s, edge_s, ids_s, tgt_s, msk_s, prev_s, pack_s, bias0, bias1, norm_s, gnorm, wide,
    s1, r1, s2, r2, s3, r3, r4, st_img, st_core, st_y, st_z,
    g_send, g_recv, kv_send, kv_recv, rs_send, rs_recv, st_send, st_recv,
):
    z, y, core = geo.place()
    me, x_img = lax.axis_index("seq"), lax.axis_index("img")
    depth, group, res, blocks, own, m = geo.depth, geo.group, geo.res, geo.blocks, geo.own, geo.m
    image, part = me // group, me % group
    siblings = [{"seq": image * group + lax.rem(part + k, group)} for k in range(1, group)]
    peers = [seq_id(lax.rem(z + k, depth), y, core) for k in range(1, depth)]
    beside, sibling = seq_id(z, 1 - y, core), seq_id(z, y, 1 - core)
    across = [{"img": lax.rem(x_img + k, m)} for k in range(1, m)]
    rows = chunk * res
    chunks = blocks // chunk
    n_groups = res // 8
    every, pair = pl.ds(0, depth), pl.ds(0, 2)

    rest[z, y, core, :, C_TOK[0] : C_TOK[1]] = tok[...].astype(BF)
    wide[...] = jnp.zeros_like(wide)
    wide[: geo.rows, :POS] = pos[...]
    rest[z, y, core, :, C_POS[0] : C_POS[1]] = wide[: geo.rows, :128].astype(BF)
    wide[...] = jnp.zeros_like(wide)
    for i in range(NORMS):
        wide[2 * i : 2 * i + 2, : geo.rows] = norms[i]
    rest[z, y, core, :, C_NORM[0] : C_NORM[1]] = jnp.transpose(wide[:, :128])[: geo.rows].astype(BF)
    rest[z, y, core, :, C_HEAD[0] : C_HEAD[1]] = head[...].astype(BF)
    for l in range(LAYERS):
        layers[l, z, y, core, :, C_IN[0] : C_IN[1]] = w_in[l].astype(BF)
        layers[l, z, y, core, :, C_OUT[0] : C_OUT[1]] = w_out[l].astype(BF)
        layers[l, z, y, core, :, C_UP[0] : C_UP[1]] = w_up[l].astype(BF)
        layers[l, z, y, core, :, C_DOWN[0] : C_DOWN[1]] = w_down[l].astype(BF)
    pack_s[...] = jnp.zeros_like(pack_s)
    pack_s[:, :own, :blocks] = pixels[...].astype(F32)
    pack_s[:, own:, :blocks] = mask[...].astype(F32)
    at = lax.broadcasted_iota(jnp.int32, (128, geo.wide), 0)
    to = lax.broadcasted_iota(jnp.int32, (128, geo.wide), 1)
    packed = jnp.zeros((2 * own, geo.wide), F32)
    for i in range(geo.images):
        spot = ((to == at + i * blocks) & (at < blocks)).astype(F32).astype(BF)
        packed = packed + dot(pack_s[i].astype(BF), spot)
    px[z, y, core] = packed.astype(BF)

    others = peers + [beside] + across
    others = others + (siblings if group > 2 else [sibling])
    if group > 2:
        others = [d for d in others if d is not beside]
    greet(others)

    parts = [px, rest.at[..., 0 : C_NORM[1]], layers.at[0, ..., 0 : C_IN[1]], layers.at[0, ..., C_OUT[0] : C_LAYER]]
    parts += [layers.at[1], rest.at[..., C_HEAD[0] : C_HEAD[1]], layers.at[2]]

    def gather_z(a, k):
        mine = parts[a].at[z, y, core]
        return push(mine, mine, g_send.at[a, k], g_recv.at[a, k], peers[k])

    def gather_y(a):
        column = parts[a].at[every, y, core]
        return push(column, column, g_send.at[a, depth - 1], g_recv.at[a, depth - 1], beside)

    def gather_core(a):
        half = parts[a].at[every, pair, core]
        return push(half, half, g_send.at[a, depth], g_recv.at[a, depth], sibling)

    def to_y(a):
        for k in range(depth - 1):
            gather_z(a, k).wait_recv()
        gather_y(a).start()

    def to_core(a):
        gather_y(a).wait_recv()
        gather_core(a).start()

    def arrived(a):
        gather_core(a).wait_recv()

    for a in range(len(parts)):
        for k in range(depth - 1):
            gather_z(a, k).start()

    def table(ref, cols):
        piece = ref[..., cols[0] : cols[1]]
        width = cols[1] - cols[0]
        if geo.rows % 16:
            return piece.astype(F32).reshape(D, width).astype(BF)
        return piece.reshape(D, width)

    def layer_table(l, cols):
        return table(layers.at[l], cols)

    def add_to(ref, cols, value):
        shape = (depth, 2, 2, geo.rows, cols[1] - cols[0])
        ref[..., cols[0] : cols[1]] += value.reshape(shape)

    for ref in (ids_s, tgt_s, msk_s, prev_s, wide, g_rest, g_layers, gnorm):
        ref[...] = jnp.zeros_like(ref)
    for l in range(LAYERS):
        kv_s[l, 0] = jnp.zeros((group, res, 2 * HEAD), BF)

    qi = part * res + lax.broadcasted_iota(jnp.int32, (res, 2 * STRIDE), 0)
    kj = lax.broadcasted_iota(jnp.int32, (res, 2 * STRIDE), 1)
    kj = kj // STRIDE * STRIDE + (kj % STRIDE + part * res) % STRIDE
    seen = (kj > qi) & (kj <= qi + STRIDE)
    bias0[0] = jnp.where(seen & (kj >= STRIDE), 0.0, -1e30)
    bias0[1] = jnp.where(seen, 0.0, -1e30)
    side = 8 * blocks
    ri = lax.broadcasted_iota(jnp.int32, (side, side), 0)
    ci = lax.broadcasted_iota(jnp.int32, (side, side), 1)
    bias1[...] = jnp.where(((ri & 7) == (ci & 7)) & (ri >= ci), 0.0, -1e30)

    to_y(0)
    to_y(1)
    to_y(2)
    to_core(0)
    to_core(1)
    to_y(3)
    to_core(2)
    arrived(0)

    span = depth // group
    at = lax.broadcasted_iota(jnp.int32, (geo.wide, 128), 0)
    to = lax.broadcasted_iota(jnp.int32, (geo.wide, 128), 1)
    spot = ((at == to + image * blocks) & (to < blocks)).astype(F32).astype(BF)
    for j in range(geo.images):
        piece = dot(px[part * span + j // 4, j // 2 % 2, j % 2], spot)
        tgt_s[j * own : (j + 1) * own, :] = piece[:own]
        msk_s[j * own : (j + 1) * own, :] = piece[own:]
    prev = dot(px[lax.rem(part * span + depth - 1, depth), 1, 1], spot)[:own]
    lane = lax.broadcasted_iota(jnp.int32, prev.shape, 1)
    moved = jnp.where(lane == 0, -1.0, pltpu.roll(prev, 1, 1))
    prev = jnp.where(part == 0, moved, prev)
    ids_s[0:1, :] = prev[own - 1 : own, :]
    ids_s[1:res, :] = tgt_s[0 : res - 1, :]

    arrived(1)
    norm_s[...] = jnp.transpose(table(rest, C_NORM).astype(F32))[:16].reshape(16, 1, D)

    def spread(ref, b0):
        values = ref[...].astype(BF)
        at = lax.broadcasted_iota(jnp.int32, (128, 128), 0)
        return jnp.concatenate(
            [dot(values, (at == b0 + j).astype(F32).astype(BF)) for j in range(chunk)], 0
        )

    def one_hot(ref, b0):
        value = spread(ref, b0)
        lane = lax.broadcasted_iota(jnp.int32, (rows, 128), 1).astype(F32)
        return jnp.concatenate([(value == lane).astype(F32), (value == lane + 128.0).astype(F32)], 1)

    def place_hot(b0):
        r = lax.broadcasted_iota(jnp.int32, (rows, 128), 0)
        lane = lax.broadcasted_iota(jnp.int32, (rows, 128), 1).astype(F32)
        p = ((b0 + r // res) * STRIDE + part * res + r % res).astype(F32)
        third = jnp.floor((p + 0.5) * (1.0 / 3.0))
        line = jnp.floor((third + 0.5) * (1.0 / SIDE))
        hits = (lane == line) | (lane == SIDE + third - SIDE * line)
        return (hits | (lane == 2 * SIDE + p - 3.0 * third)).astype(F32)

    def loop(count, body):
        lax.fori_loop(0, count, lambda i, carry: (body(i), carry)[1], 0)

    def embed(i):
        b0 = i * chunk
        hot = jnp.concatenate([one_hot(ids_s, b0), place_hot(b0)], 1).astype(BF)
        x = dot_nt(hot, table(rest, (C_TOK[0], C_POS[1])))
        x_s[0, pl.ds(b0, chunk)] = x.reshape(chunk, res, D)

    loop(chunks, embed)

    def exchange(l, k):
        mine = kv_s.at[l, pl.ds(1, blocks), 0]
        there = kv_s.at[l, pl.ds(1, blocks), group - 1 - k]
        return push(mine, there, kv_send.at[k], kv_recv.at[l, k], siblings[k])

    def forward(l):
        def mix(i):
            b0 = i * chunk
            at = pl.ds(b0, chunk)
            unit, _ = normalise(x_s[l, at].reshape(rows, D))
            h = (unit * (1.0 + norm_s[4 * l]) + norm_s[4 * l + 1]).astype(BF)
            qkv = dot(h, layer_table(l, C_IN)).reshape(chunk, res, 6 * HEAD)
            q0_s[l, at] = qkv[..., :HEAD].astype(BF)
            kv_s[l, pl.ds(b0 + 1, chunk), 0, :, :HEAD] = qkv[..., 2 * HEAD : 3 * HEAD].astype(BF)
            kv_s[l, pl.ds(b0 + 1, chunk), 0, :, HEAD:] = qkv[..., 4 * HEAD : 5 * HEAD].astype(BF)
            stage[at, :, :HEAD] = qkv[..., HEAD : 2 * HEAD]
            stage[at, :, HEAD : 2 * HEAD] = qkv[..., 3 * HEAD : 4 * HEAD]
            stage[at, :, 2 * HEAD :] = qkv[..., 5 * HEAD :]

        def strided(i):
            qkvs = []
            for j in range(pack):
                at = pl.ds(pl.multiple_of(8 * (i * pack + j), 8), 8)
                qkv = stage[:, at, :].reshape(side, 3 * HEAD).astype(BF)
                qkv1_s[l, i * pack + j] = qkv
                qkvs.append(qkv)
            raw = [dot_nt(qkv[:, :HEAD], qkv[:, HEAD : 2 * HEAD]) * SCALE + bias1[...] for qkv in qkvs]
            probs = softmax(jnp.concatenate(raw, 0)).astype(BF)
            p1_s[l, pl.ds(i * pack, pack)] = probs.reshape(pack, side, side)
            for j in range(pack):
                at = pl.ds(pl.multiple_of(8 * (i * pack + j), 8), 8)
                value = dot(probs[j * side : (j + 1) * side], qkvs[j][:, 2 * HEAD :])
                o1_s[:, at, :] = value.reshape(blocks, 8, HEAD)

        def window(i):
            b0 = i * batch
            kv = kv_s[l, pl.ds(b0, batch + 1)].reshape((batch + 1) * STRIDE, 2 * HEAD)
            raw = [
                dot_nt(q0_s[l, b0 + j], kv[j * STRIDE : (j + 2) * STRIDE, :HEAD]) * SCALE
                + bias0[jnp.minimum(b0 + j, 1)]
                for j in range(batch)
            ]
            probs = softmax(jnp.concatenate(raw, 0)).astype(BF)
            p0_s[l, pl.ds(b0, batch)] = probs.reshape(batch, res, 2 * STRIDE)
            for j in range(batch):
                value = dot(probs[j * res : (j + 1) * res], kv[j * STRIDE : (j + 2) * STRIDE, HEAD:])
                o_s[l, b0 + j, :, :HEAD] = value.astype(BF)

        def feed(i):
            b0 = i * chunk
            at = pl.ds(b0, chunk)
            o_s[l, at, :, HEAD:] = o1_s[at].astype(BF)
            x1 = x_s[l, at].reshape(rows, D) + dot(o_s[l, at].reshape(rows, D), layer_table(l, C_OUT))
            x1_s[l, at] = x1.reshape(chunk, res, D)
            unit, _ = normalise(x1)
            h = (unit * (1.0 + norm_s[4 * l + 2]) + norm_s[4 * l + 3]).astype(BF)
            a, slope = gelu_both(dot(h, layer_table(l, C_UP)))
            a = a.astype(BF)
            a_s[l, at] = a.reshape(chunk, res, FF)
            slope_s[l, at] = slope.astype(BF).reshape(chunk, res, FF)
            x2 = x1 + dot_nt(a, layer_table(l, C_DOWN))
            x_s[l + 1, at] = x2.reshape(chunk, res, D)

        arrived((2, 4, 6)[l])
        loop(chunks, mix)
        copies = [exchange(l, k) for k in range(group - 1)]
        for copy in copies:
            copy.start()
        if l == 0:
            to_core(3)
            to_y(4)
        if l == 1:
            to_core(5)
            to_core(6)
        loop(n_groups // pack, strided)
        for copy in copies:
            copy.wait()
        loop(blocks // batch, window)
        if l == 0:
            arrived(3)
            to_y(5)
        loop(chunks, feed)
        if l == 0:
            to_core(4)
            to_y(6)

    for l in range(LAYERS):
        forward(l)
    arrived(5)

    dx_s = x_s.at[LAYERS]

    def finish(i, loss):
        b0 = i * chunk
        at = pl.ds(b0, chunk)
        unit, rstd = normalise(x_s[LAYERS, at].reshape(rows, D))
        gain = norm_s[4 * LAYERS]
        h = (unit * (1.0 + gain) + norm_s[4 * LAYERS + 1]).astype(BF)
        table_head = table(rest, C_HEAD)
        logits = dot(h, table_head)
        hot = one_hot(tgt_s, b0)
        shift = logits - jnp.max(logits, -1, keepdims=True)
        e = jnp.exp(shift)
        total = jnp.sum(e, -1, keepdims=True)
        weight = spread(msk_s, b0)
        per = (
            jnp.log(total)
            - (1.0 - SMOOTHING) * jnp.sum(hot * shift, -1, keepdims=True)
            - SMOOTHING * jnp.mean(shift, -1, keepdims=True)
        )
        loss = loss + jnp.sum(weight[:, :1] * per, 0, keepdims=True)
        weight = jnp.concatenate([weight, weight], 1)
        d_logits = weight * (e * (1.0 / total) - (1.0 - SMOOTHING) * hot - SMOOTHING / V)
        d_logits = d_logits.astype(BF)
        add_to(g_rest, C_HEAD, dot_tn(h, d_logits))
        dx, g_gain, g_bias = normalise_back(dot_nt(d_logits, table_head), unit, rstd, gain)
        gnorm[4 * LAYERS] += g_gain
        gnorm[4 * LAYERS + 1] += g_bias
        dx_s[at] = dx.reshape(chunk, res, D)
        return loss

    loss = lax.fori_loop(0, chunks, finish, jnp.zeros((1, 1), F32))
    count = jnp.sum(jnp.sum(msk_s[...], 0, keepdims=True), 1, keepdims=True)
    line = lax.broadcasted_iota(jnp.int32, (8, 128), 0)
    st_img[x_img] = jnp.where(line == 0, loss, jnp.where(line == 1, count, 0.0))
    st_across = [
        push(st_img.at[x_img], st_img.at[x_img], st_send.at[k], st_recv.at[k], across[k]) for k in range(m - 1)
    ]
    for copy in st_across:
        copy.start()

    def give(l, k):
        return push(
            away_s.at[k, pl.ds(1, blocks)], back_s.at[l % 2, k], kv_send.at[k], kv_recv.at[LAYERS + l, k], siblings[k]
        )

    def backward(l, after_feed, after_window, after_strided):
        grads = g_layers.at[l % 2]
        own_s = x1_s.at[l]

        def feed(i):
            b0 = i * chunk
            at = pl.ds(b0, chunk)
            dx2 = dx_s[at].reshape(rows, D)
            g2 = dx2.astype(BF)
            a = a_s[l, at].reshape(rows, FF)
            add_to(grads, C_DOWN, dot_tn(g2, a))
            du = slope_s[l, at].reshape(rows, FF).astype(F32) * dot(g2, layer_table(l, C_DOWN))
            du = du.astype(BF)
            unit, rstd = normalise(x1_s[l, at].reshape(rows, D))
            gain = norm_s[4 * l + 2]
            h = (unit * (1.0 + gain) + norm_s[4 * l + 3]).astype(BF)
            add_to(grads, C_UP, dot_tn(h, du))
            dh = dot_nt(du, layer_table(l, C_UP))
            dx, g_gain, g_bias = normalise_back(dh, unit, rstd, gain)
            gnorm[4 * l + 2] += g_gain
            gnorm[4 * l + 3] += g_bias
            dx = dx + dx2
            dx_s[at] = dx.reshape(chunk, res, D)
            g1 = dx.astype(BF)
            add_to(grads, C_OUT, dot_tn(o_s[l, at].reshape(rows, D), g1))
            do = dot_nt(g1, layer_table(l, C_OUT)).reshape(chunk, res, D)
            do0_s[at] = do[..., :HEAD].astype(BF)
            o1_s[at] = do[..., HEAD:]

        def window(i):
            b0 = i * batch
            at = pl.ds(b0, batch)
            kv = kv_s[l, pl.ds(b0, batch + 1)].reshape((batch + 1) * STRIDE, 2 * HEAD)
            probs = p0_s[l, at].reshape(batch * res, 2 * STRIDE)
            do = [do0_s[b0 + j] for j in range(batch)]
            keys = [kv[j * STRIDE : (j + 2) * STRIDE, :HEAD] for j in range(batch)]
            dp = jnp.concatenate(
                [dot_nt(do[j], kv[j * STRIDE : (j + 2) * STRIDE, HEAD:]) for j in range(batch)], 0
            )
            wide_p = probs.astype(F32)
            ds = (wide_p * (dp - jnp.sum(wide_p * dp, -1, keepdims=True)) * SCALE).astype(BF)
            carry = edge_s[...]
            for j in range(batch):
                cut = slice(j * res, (j + 1) * res)
                dq0_s[b0 + j] = dot(ds[cut], keys[j]).astype(BF)
                dkv = jnp.concatenate([dot_tn(ds[cut], q0_s[l, b0 + j]), dot_tn(probs[cut], do[j])], 1)
                done = (carry + dkv[:STRIDE]).reshape(group, res, 2 * HEAD)
                own_s[b0 + j] = done[0]
                for k in range(group - 1):
                    away_s[k, b0 + j] = done[k + 1].astype(BF)
                carry = dkv[STRIDE:]
            edge_s[...] = carry

        def strided(i):
            probs = p1_s[l, pl.ds(i * pack, pack)].reshape(pack * side, side)
            qkvs = [qkv1_s[l, i * pack + j] for j in range(pack)]
            ats = [pl.ds(pl.multiple_of(8 * (i * pack + j), 8), 8) for j in range(pack)]
            dos = [o1_s[:, at, :].reshape(side, HEAD).astype(BF) for at in ats]
            dp = jnp.concatenate([dot_nt(do, qkv[:, 2 * HEAD :]) for do, qkv in zip(dos, qkvs)], 0)
            wide_p = probs.astype(F32)
            ds = (wide_p * (dp - jnp.sum(wide_p * dp, -1, keepdims=True)) * SCALE).astype(BF)
            for j in range(pack):
                cut = slice(j * side, (j + 1) * side)
                dq = dot(ds[cut], qkvs[j][:, HEAD : 2 * HEAD])
                dk = dot_tn(ds[cut], qkvs[j][:, :HEAD])
                dv = dot_tn(probs[cut], dos[j])
                stage[:, ats[j], :] = jnp.concatenate([dq, dk, dv], 1).reshape(blocks, 8, 3 * HEAD)

        def mix(i):
            b0 = i * chunk
            at = pl.ds(b0, chunk)
            dkv = own_s[pl.ds(b0 + 1, chunk)]
            for k in range(group - 1):
                dkv = dkv + back_s[l % 2, k, at].astype(F32)
            d1 = stage[at]
            dqkv = jnp.concatenate(
                [
                    dq0_s[at],
                    d1[..., :HEAD].astype(BF),
                    dkv[..., :HEAD].astype(BF),
                    d1[..., HEAD : 2 * HEAD].astype(BF),
                    dkv[..., HEAD:].astype(BF),
                    d1[..., 2 * HEAD :].astype(BF),
                ],
                -1,
            ).reshape(rows, 6 * HEAD)
            unit, rstd = normalise(x_s[l, at].reshape(rows, D))
            gain = norm_s[4 * l]
            h = (unit * (1.0 + gain) + norm_s[4 * l + 1]).astype(BF)
            add_to(grads, C_IN, dot_tn(h, dqkv))
            dh = dot_nt(dqkv, layer_table(l, C_IN))
            dx, g_gain, g_bias = normalise_back(dh, unit, rstd, gain)
            gnorm[4 * l] += g_gain
            gnorm[4 * l + 1] += g_bias
            dx_s[at] += dx.reshape(chunk, res, D)

        loop(chunks, feed)
        after_feed()
        edge_s[...] = jnp.zeros_like(edge_s)
        loop(blocks // batch, window)
        last = edge_s[...].reshape(group, res, 2 * HEAD)
        own_s[blocks] = last[0]
        for k in range(group - 1):
            away_s[k, blocks] = last[k + 1].astype(BF)
        copies = [give(l, k) for k in range(group - 1)]
        for copy in copies:
            copy.start()
        after_window()
        loop(n_groups // pack, strided)
        after_strided()
        for copy in copies:
            copy.wait()
        loop(chunks, mix)

    def section(index, ref, cols, base):
        width = cols[1] - cols[0]
        cut = slice(base, base + width)
        grad = ref.at[..., cols[0] : cols[1]]
        first = push(s1.at[..., cut], r1.at[..., cut], rs_send.at[index, 0], rs_recv.at[index, 0], sibling)
        second = push(s2.at[..., cut], r2.at[..., cut], rs_send.at[index, 1], rs_recv.at[index, 1], beside)
        third = [
            push(
                s3.at[lax.rem(z + k, depth), :, cut],
                r3.at[k - 1, :, cut],
                rs_send.at[index, 1 + k],
                rs_recv.at[index, 1 + k],
                peers[k - 1],
            )
            for k in range(1, depth)
        ]
        fourth = [
            push(
                r4.at[x_img, :, cut],
                r4.at[x_img, :, cut],
                rs_send.at[index, depth + 1 + k],
                rs_recv.at[index, depth + 1 + k],
                across[k],
            )
            for k in range(m - 1)
        ]

        def go_core():
            s1[..., cut] = grad[every, pair, 1 - core].astype(BF)
            first.start()

        def go_y():
            first.wait()
            total = grad[every, 1 - y, core] + r1[every, 1 - y, :, cut].astype(F32)
            s2[..., cut] = total.astype(BF)
            second.start()

        def go_z():
            second.wait()
            total = grad[every, y, core] + r1[every, y, :, cut].astype(F32) + r2[..., cut].astype(F32)
            s3[..., cut] = total.astype(BF)
            for copy in third:
                copy.start()

        def go_img():
            for copy in third:
                copy.wait()
            total = s3[z, :, cut].astype(F32)
            for k in range(1, depth):
                total = total + r3[k - 1, :, cut].astype(F32)
            r4[x_img, :, cut] = total.astype(BF)
            for copy in fourth:
                copy.start()

        def end():
            for copy in fourth:
                copy.wait()
            total = r4[0, :, cut].astype(F32)
            for k in range(1, m):
                total = total + r4[k, :, cut].astype(F32)
            sums[:, cut] = total
            return jnp.sum(jnp.sum(total * total, 0, keepdims=True), 1, keepdims=True)

        return go_core, go_y, go_z, go_img, end

    two = section(0, g_layers.at[0], (0, C_LAYER), 2 * C_LAYER)
    one = section(1, g_layers.at[1], (0, C_LAYER), C_LAYER)
    zero_rest = section(2, g_layers.at[0], (C_OUT[0], C_LAYER), C_OUT[0])
    zero_in = section(3, g_layers.at[0], C_IN, 0)
    other = section(4, g_rest, (0, C_REST), LAYERS * C_LAYER)

    def run(*steps):
        def inner():
            for step in steps:
                step()

        return inner

    nothing = run()
    backward(2, nothing, nothing, nothing)
    two[0]()
    backward(1, two[1], two[2], two[3])
    squares = two[4]()
    one[0]()
    g_layers[0] = jnp.zeros(g_layers.shape[1:], F32)
    backward(0, run(zero_rest[0], one[1]), run(zero_rest[1], one[2]), run(zero_rest[2], one[3]))
    zero_in[0]()
    zero_rest[3]()
    squares = squares + one[4]()

    def embed_back(i):
        b0 = i * chunk
        hot = jnp.concatenate([one_hot(ids_s, b0), place_hot(b0)], 1).astype(BF)
        dx = dx_s[pl.ds(b0, chunk)].reshape(rows, D)
        high = dx.astype(BF)
        low = (dx - high.astype(F32)).astype(BF)
        add_to(g_rest, (C_TOK[0], C_POS[1]), dot_tn(high, hot) + dot_tn(low, hot))

    loop(chunks, embed_back)
    for i in range(2 * NORMS):
        wide[i : i + 1, :] = jnp.sum(gnorm[i], 0, keepdims=True)
    add_to(g_rest, C_NORM, jnp.transpose(wide[...]))
    other[0]()
    zero_in[1]()
    other[1]()
    zero_in[2]()
    other[2]()
    squares = squares + zero_rest[4]()
    zero_in[3]()
    other[3]()
    squares = squares + zero_in[4]()
    squares = squares + other[4]()

    for copy in st_across:
        copy.wait()
    told = st_img[0]
    for k in range(1, m):
        told = told + st_img[k]
    told = jnp.where(line == 2, squares, told)
    base = m - 1

    def swap(told, buffer, index, where, device):
        buffer[where] = told
        copy = push(buffer.at[where], buffer.at[where], st_send.at[base + index], st_recv.at[base + index], device)
        copy.start()
        copy.wait()
        return buffer[0] + buffer[1]

    told = swap(told, st_core, 0, core, sibling)
    told = swap(told, st_y, 1, y, beside)
    st_z[z] = told
    copies = [
        push(st_z.at[z], st_z.at[z], st_send.at[base + 1 + k], st_recv.at[base + 1 + k], peers[k - 1])
        for k in range(1, depth)
    ]
    for copy in copies:
        copy.start()
    for a in range(len(parts)):
        for k in range(depth - 1):
            gather_z(a, k).wait_send()
        gather_y(a).wait_send()
        gather_core(a).wait_send()
    for copy in copies:
        copy.wait()
    told = st_z[0]
    for k in range(1, depth):
        told = told + st_z[k]
    count = told[1:2, :1]
    norm = jnp.sqrt(told[2:3, :1]) / count
    factor = jnp.minimum(1.0, CLIP_NORM / norm) / count
    totals[...] = jnp.where(line == 2, norm, jnp.where(line == 3, factor, told))


def adam(master, gradient, first, second):
    first = BETA_ONE * first + (1.0 - BETA_ONE) * gradient
    second = BETA_TWO * second + (1.0 - BETA_TWO) * gradient * gradient
    moved = first / (1.0 - BETA_ONE**STEP) / (jnp.sqrt(second / (1.0 - BETA_TWO**STEP)) + ADAM_EPS)
    return master - LEARN_RATE * (moved + WEIGHT_DECAY * master), first, second


def update_kernel(rows, *refs):
    sums, totals = refs[:2]
    masters, firsts, seconds = refs[2:10], refs[10:18], refs[18:26]
    outs = (refs[26:34], refs[34:42], refs[42:50])
    turned = refs[50]
    factor = totals[3:4, :1]

    def put(index, at, gradient):
        result = adam(masters[index][at], gradient * factor, firsts[index][at], seconds[index][at])
        for k in range(3):
            outs[k][index][at] = result[k]

    base = LAYERS * C_LAYER
    put(0, ..., sums[:, base + C_TOK[0] : base + C_TOK[1]])
    put(1, ..., sums[:, base + C_POS[0] : base + C_POS[0] + POS])
    put(6, ..., sums[:, base + C_HEAD[0] : base + C_HEAD[1]])
    turned[...] = jnp.transpose(sums[:, base + C_NORM[0] : base + C_NORM[1]])
    for i in range(NORMS):
        put(7, i, turned[2 * i : 2 * i + 2, :])
    for l in range(LAYERS):
        for index, cols in ((2, C_IN), (3, C_OUT), (4, C_UP), (5, C_DOWN)):
            put(index, l, sums[:, l * C_LAYER + cols[0] : l * C_LAYER + cols[1]])


def turned(tok, pos, w_in, w_out, w_up, w_down, head, norms):
    return (tok.T, pos.T, w_in, w_out, w_up, jnp.swapaxes(w_down, 1, 2), head, norms)


def on_device(geo, pixels, loss_mask, *weights):
    masters, firsts, seconds = (turned(*weights[k : k + 8]) for k in (0, 8, 16))
    n_rows, depth, blocks, res, group = geo.rows, geo.depth, geo.blocks, geo.res, geo.group
    m = geo.m
    vmem = pl.BlockSpec(memory_space=pltpu.VMEM)
    chunk = 12
    batch = 12
    pack = 4
    n_groups = res // 8
    side = 8 * blocks
    sums, totals = pl.pallas_call(
        functools.partial(step_kernel, geo, chunk, batch, pack),
        out_shape=(
            jax.ShapeDtypeStruct((n_rows, C_ALL), F32),
            jax.ShapeDtypeStruct((8, 128), F32),
        ),
        in_specs=[vmem] * 10,
        out_specs=(vmem,) * 2,
        scratch_shapes=[
            pltpu.VMEM((depth, 2, 2, 2 * geo.own, geo.wide), BF),
            pltpu.VMEM((depth, 2, 2, n_rows, C_REST), BF),
            pltpu.VMEM((LAYERS, depth, 2, 2, n_rows, C_LAYER), BF),
            pltpu.VMEM((depth, 2, 2, n_rows, C_REST), F32),
            pltpu.VMEM((2, depth, 2, 2, n_rows, C_LAYER), F32),
            pltpu.VMEM((LAYERS + 1, blocks, res, D), F32),
            pltpu.VMEM((LAYERS, blocks + 1, res, D), F32),
            pltpu.VMEM((LAYERS, blocks, res, HEAD), BF),
            pltpu.VMEM((LAYERS, blocks + 1, group, res, 2 * HEAD), BF),
            pltpu.VMEM((LAYERS, n_groups, side, 3 * HEAD), BF),
            pltpu.VMEM((LAYERS, blocks, res, 2 * STRIDE), BF),
            pltpu.VMEM((LAYERS, n_groups, side, side), BF),
            pltpu.VMEM((LAYERS, blocks, res, D), BF),
            pltpu.VMEM((LAYERS, blocks, res, FF), BF),
            pltpu.VMEM((LAYERS, blocks, res, FF), BF),
            pltpu.VMEM((blocks, res, 3 * HEAD), F32),
            pltpu.VMEM((blocks, res, HEAD), F32),
            pltpu.VMEM((blocks, res, HEAD), BF),
            pltpu.VMEM((blocks, res, HEAD), BF),
            pltpu.VMEM((group - 1, blocks + 1, res, 2 * HEAD), BF),
            pltpu.VMEM((2, group - 1, blocks, res, 2 * HEAD), BF),
            pltpu.VMEM((STRIDE, 2 * HEAD), F32),
            pltpu.VMEM((res, 128), F32),
            pltpu.VMEM((res, 128), F32),
            pltpu.VMEM((res, 128), F32),
            pltpu.VMEM((8, 128), F32),
            pltpu.VMEM((geo.images, 2 * geo.own, 128), F32),
            pltpu.VMEM((2, res, 2 * STRIDE), F32),
            pltpu.VMEM((side, side), F32),
            pltpu.VMEM((16, 1, D), F32),
            pltpu.VMEM((2 * NORMS, 8, D), F32),
            pltpu.VMEM((128, D), F32),
            pltpu.VMEM((depth, 2, n_rows, C_ALL), BF),
            pltpu.VMEM((depth, 2, n_rows, C_ALL), BF),
            pltpu.VMEM((depth, n_rows, C_ALL), BF),
            pltpu.VMEM((depth, n_rows, C_ALL), BF),
            pltpu.VMEM((depth, n_rows, C_ALL), BF),
            pltpu.VMEM((depth - 1, n_rows, C_ALL), BF),
            pltpu.VMEM((m, n_rows, C_ALL), BF),
            pltpu.VMEM((m, 8, 128), F32),
            pltpu.VMEM((2, 8, 128), F32),
            pltpu.VMEM((2, 8, 128), F32),
            pltpu.VMEM((depth, 8, 128), F32),
            pltpu.SemaphoreType.DMA((4 + LAYERS, depth + 1)),
            pltpu.SemaphoreType.DMA((4 + LAYERS, depth + 1)),
            pltpu.SemaphoreType.DMA((group - 1,)),
            pltpu.SemaphoreType.DMA((2 * LAYERS, group - 1)),
            pltpu.SemaphoreType.DMA((5, depth + m)),
            pltpu.SemaphoreType.DMA((5, depth + m)),
            pltpu.SemaphoreType.DMA((m + depth,)),
            pltpu.SemaphoreType.DMA((m + depth,)),
        ],
        compiler_params=pltpu.CompilerParams(
            collective_id=0, has_side_effects=True, vmem_limit_bytes=VMEM_LIMIT
        ),
        name="step",
    )(jnp.swapaxes(pixels, 1, 2), jnp.swapaxes(loss_mask, 1, 2), *masters)

    shapes = [jax.ShapeDtypeStruct(item.shape, F32) for item in masters]
    outs = pl.pallas_call(
        functools.partial(update_kernel, n_rows),
        out_shape=shapes * 3,
        in_specs=[vmem] * 26,
        out_specs=[vmem] * 24,
        scratch_shapes=[pltpu.VMEM((128, n_rows), F32)],
        name="update",
    )(sums, totals, *masters, *firsts, *seconds)
    return (
        totals[0, 0],
        totals[1, 0],
        totals[2, 0],
        *turned(*outs[:8]),
        *turned(*outs[8:16]),
        *turned(*outs[16:]),
    )


def solution(mesh):
    pixels = P("img", None, "seq")
    weights = (
        P(None, "seq"),
        P(None, "seq"),
        P(None, "seq", None),
        P(None, "seq", None),
        P(None, "seq", None),
        P(None, None, "seq"),
        P("seq", None),
        P(None, None, "seq"),
    )

    def body(pixels, loss_mask, *rest):
        geo = Geometry(mesh.shape["seq"], mesh.shape["img"], pixels.shape[0], pixels.shape[1])
        return on_device(geo, pixels, loss_mask, *rest)

    return jax.shard_map(
        body,
        mesh=mesh,
        in_specs=(pixels, pixels) + weights * 3,
        out_specs=(P(), P(), P()) + weights * 3,
        check_vma=False,
    )
```

```python
import functools
import math

import jax
import jax.numpy as jnp
from jax import lax
from jax.experimental import pallas as pl
from jax.experimental.pallas import tpu as pltpu
from jax.sharding import PartitionSpec as P

D = 256
HEAD = 128
FF = 512
V = 256
STRIDE = 128
LAYERS = 3
NORMS = 2 * LAYERS + 1
STEP = 10
SIDE = 32
POS = 2 * SIDE + 3
CLIP_NORM = 0.05
BETA_ONE = 0.9
BETA_TWO = 0.95
LEARN_RATE = 0.1
WEIGHT_DECAY = 0.1
ADAM_EPS = 1e-08
SMOOTHING = 0.1
NORM_EPS = 1e-05
SCALE = HEAD ** (-0.5)

C_IN, C_OUT, C_UP, C_DOWN = (0, 768), (768, 1024), (1024, 1536), (1536, 2048)
C_LAYER = 2048
C_TOK, C_POS, C_HEAD = (0, 256), (256, 384), (384, 640)
C_REST = 640
C_ALL = LAYERS * C_LAYER + C_REST

BF = jnp.bfloat16
F32 = jnp.float32
VMEM_LIMIT = 64 * 1024 * 1024


def dot(a, b):
    return lax.dot_general(a, b, (((1,), (0,)), ((), ())), preferred_element_type=F32)


def dot_nt(a, b):
    return lax.dot_general(a, b, (((1,), (1,)), ((), ())), preferred_element_type=F32)


def dot_tn(a, b):
    return lax.dot_general(a, b, (((0,), (0,)), ((), ())), preferred_element_type=F32)


class Geometry:
    def __init__(self, n, m, images, blocks):
        self.n, self.m, self.images, self.blocks = n, m, images, blocks
        self.depth = n // 4
        self.rows = D // n
        self.group = n // images
        self.res = STRIDE // self.group
        self.own = STRIDE // n
        self.wide = -(-images * blocks // 128) * 128

    def place(self):
        me = lax.axis_index("seq")
        return me // 4, me // 2 % 2, me % 2


def seq_id(z, y, core):
    return {"seq": z * 4 + y * 2 + core}


def greet(devices):
    barrier = pltpu.get_barrier_semaphore()
    for device in devices:
        pl.semaphore_signal(barrier, inc=1, device_id=device, device_id_type=pl.DeviceIdType.MESH)


def greeted(devices):
    pl.semaphore_wait(pltpu.get_barrier_semaphore(), len(devices))


def push(src, dst, send_sem, recv_sem, device):
    return pltpu.make_async_remote_copy(
        src_ref=src,
        dst_ref=dst,
        send_sem=send_sem,
        recv_sem=recv_sem,
        device_id=device,
        device_id_type=pl.DeviceIdType.MESH,
    )


def normalise(x):
    centre = x - jnp.mean(x, -1, keepdims=True)
    spread = jnp.mean(centre * centre, -1, keepdims=True)
    rstd = lax.rsqrt(spread + NORM_EPS)
    return centre * rstd, rstd


def fold(x):
    return jnp.sum(x.reshape(x.shape[0] // 8, 8, x.shape[1]), 0)


def normalise_back(dy, unit, rstd, gain):
    dxh = dy * (1.0 + gain)
    mean_one = jnp.mean(dxh, -1, keepdims=True)
    mean_two = jnp.mean(dxh * unit, -1, keepdims=True)
    return rstd * (dxh - mean_one - unit * mean_two), fold(dy * unit), fold(dy)


def gelu_both(u):
    c = math.sqrt(2.0 / math.pi)
    w = c + (0.044715 * c) * (u * u)
    half = 0.5 + 0.5 * jnp.tanh(u * w)
    a = u * half
    return a, half + a * (1.0 - half) * (6.0 * w - 4.0 * c)


def softmax(scores):
    e = jnp.exp(scores - jnp.max(scores, -1, keepdims=True))
    return e * (1.0 / jnp.sum(e, -1, keepdims=True))


def step_kernel(
    geo, chunk, batch, pack,
    pixels, mask, tok, pos, w_in, w_out, w_up, w_down, head, norms,
    sums, totals,
    px, rest, layers, g_rest, g_layers,
    x_s, x1_s, q0_s, kv_s, qkv1_s, p0_s, p1_s, o_s, a_s, slope_s, stage, o1_s, do0_s, dq0_s,
    away_s, back_s, edge_s, ids_s, tgt_s, msk_s, prev_s, pack_s, bias0, bias1, norm_s, gnorm, wide, squares,
    s1, r1, r2, r4, st_img, st_core, st_plane,
    g_send, g_recv, kv_send, kv_recv, rs_send, rs_recv, st_send, st_recv,
):
    z, y, core = geo.place()
    me, x_img = lax.axis_index("seq"), lax.axis_index("img")
    depth, group, res, blocks, own, m = geo.depth, geo.group, geo.res, geo.blocks, geo.own, geo.m
    image, part = me // group, me % group
    siblings = [{"seq": image * group + lax.rem(part + k, group)} for k in range(1, group)]
    peers = [seq_id(lax.rem(z + k, depth), y, core) for k in range(1, depth)]
    beside, sibling = seq_id(z, 1 - y, core), seq_id(z, y, 1 - core)
    columns = 2 * depth
    column = z * 2 + y
    plane = [lax.rem(column + k, columns) for k in range(1, columns)]
    across = [{"img": lax.rem(x_img + k, m)} for k in range(1, m)]
    others = [seq_id(q // 2, q % 2, core) for q in plane] + across + [sibling]
    if group > 2:
        others.append(seq_id(z, 1 - y, 1 - core))
    greet(others)
    rows = chunk * res
    chunks = blocks // chunk
    n_groups = res // 8
    every, pair = pl.ds(0, depth), pl.ds(0, 2)

    pack_s[...] = jnp.zeros_like(pack_s)
    pack_s[:, :own, :blocks] = pixels[...].astype(F32)
    pack_s[:, own:, :blocks] = mask[...].astype(F32)
    at = lax.broadcasted_iota(jnp.int32, (128, geo.wide), 0)
    to = lax.broadcasted_iota(jnp.int32, (128, geo.wide), 1)
    packed = jnp.zeros((2 * own, geo.wide), F32)
    for i in range(geo.images):
        spot = ((to == at + i * blocks) & (at < blocks)).astype(F32).astype(BF)
        packed = packed + dot(pack_s[i].astype(BF), spot)
    px[z, y, core] = packed.astype(BF)
    rest[z, y, core, :, C_TOK[0] : C_TOK[1]] = tok[...].astype(BF)
    wide[...] = jnp.zeros_like(wide)
    for i in range(NORMS):
        wide[POS + 2 * i : POS + 2 * i + 2, : geo.rows] = norms[i]
    flipped = jnp.transpose(wide[:, :128])[: geo.rows]
    wide[: geo.rows, :128] = flipped
    wide[: geo.rows, :POS] = pos[...]
    rest[z, y, core, :, C_POS[0] : C_POS[1]] = wide[: geo.rows, :128].astype(BF)

    parts = [px, rest.at[..., 0 : C_POS[1]]]
    for l in range(LAYERS):
        parts += [layers.at[l, ..., 0 : C_IN[1]], layers.at[l, ..., C_OUT[0] : C_LAYER]]
    parts += [rest.at[..., C_HEAD[0] : C_HEAD[1]]]

    def gather_z(a, k):
        mine = parts[a].at[z, y, core]
        return push(mine, mine, g_send.at[a, k], g_recv.at[a, k], peers[k])

    def gather_y(a):
        column = parts[a].at[every, y, core]
        return push(column, column, g_send.at[a, depth - 1], g_recv.at[a, depth - 1], beside)

    def gather_core(a):
        half = parts[a].at[every, pair, core]
        return push(half, half, g_send.at[a, depth], g_recv.at[a, depth], sibling)

    def to_y(a):
        for k in range(depth - 1):
            gather_z(a, k).wait_recv()
        gather_y(a).start()

    def to_core(a):
        gather_y(a).wait_recv()
        gather_core(a).start()

    def arrived(a):
        gather_core(a).wait_recv()

    def to_z(a):
        for k in range(depth - 1):
            gather_z(a, k).start()

    greeted(others)
    to_z(0)
    to_z(1)
    for l in range(LAYERS):
        layers[l, z, y, core, :, C_IN[0] : C_IN[1]] = w_in[l].astype(BF)
        to_z(2 + 2 * l)
        layers[l, z, y, core, :, C_OUT[0] : C_OUT[1]] = w_out[l].astype(BF)
        layers[l, z, y, core, :, C_UP[0] : C_UP[1]] = w_up[l].astype(BF)
        layers[l, z, y, core, :, C_DOWN[0] : C_DOWN[1]] = w_down[l].astype(BF)
        to_z(3 + 2 * l)
    rest[z, y, core, :, C_HEAD[0] : C_HEAD[1]] = head[...].astype(BF)
    to_z(8)

    def table(ref, cols):
        piece = ref[..., cols[0] : cols[1]]
        width = cols[1] - cols[0]
        if geo.rows % 16:
            return piece.astype(F32).reshape(D, width).astype(BF)
        return piece.reshape(D, width)

    def layer_table(l, cols):
        return table(layers.at[l], cols)

    def add_to(ref, cols, value):
        shape = (depth, 2, 2, geo.rows, cols[1] - cols[0])
        ref[..., cols[0] : cols[1]] += value.reshape(shape)

    for ref in (ids_s, tgt_s, msk_s, prev_s, wide, g_rest, g_layers, gnorm):
        ref[...] = jnp.zeros_like(ref)
    for l in range(LAYERS):
        kv_s[l, 0] = jnp.zeros((group, res, 2 * HEAD), BF)

    qi = part * res + lax.broadcasted_iota(jnp.int32, (res, 2 * STRIDE), 0)
    kj = lax.broadcasted_iota(jnp.int32, (res, 2 * STRIDE), 1)
    kj = kj // STRIDE * STRIDE + (kj % STRIDE + part * res) % STRIDE
    seen = (kj > qi) & (kj <= qi + STRIDE)
    bias0[0] = jnp.where(seen & (kj >= STRIDE), 0.0, -1e30)
    bias0[1] = jnp.where(seen, 0.0, -1e30)
    side = 8 * blocks
    ri = lax.broadcasted_iota(jnp.int32, (side, side), 0)
    ci = lax.broadcasted_iota(jnp.int32, (side, side), 1)
    bias1[...] = jnp.where(((ri & 7) == (ci & 7)) & (ri >= ci), 0.0, -1e30)

    to_y(0)
    to_y(1)
    to_y(2)
    to_core(0)
    to_core(1)
    arrived(0)

    span = depth // group
    at = lax.broadcasted_iota(jnp.int32, (geo.wide, 128), 0)
    to = lax.broadcasted_iota(jnp.int32, (geo.wide, 128), 1)
    spot = ((at == to + image * blocks) & (to < blocks)).astype(F32).astype(BF)
    for j in range(geo.images):
        piece = dot(px[part * span + j // 4, j // 2 % 2, j % 2], spot)
        tgt_s[j * own : (j + 1) * own, :] = piece[:own]
        msk_s[j * own : (j + 1) * own, :] = piece[own:]
    prev = dot(px[lax.rem(part * span + depth - 1, depth), 1, 1], spot)[:own]
    lane = lax.broadcasted_iota(jnp.int32, prev.shape, 1)
    moved = jnp.where(lane == 0, -1.0, pltpu.roll(prev, 1, 1))
    prev = jnp.where(part == 0, moved, prev)
    ids_s[0:1, :] = prev[own - 1 : own, :]
    ids_s[1:res, :] = tgt_s[0 : res - 1, :]

    arrived(1)
    wide[...] = jnp.transpose(table(rest, C_POS).astype(F32))
    for i in range(2 * NORMS):
        norm_s[i] = wide[POS + i : POS + i + 1, :]
    wide[...] = jnp.zeros_like(wide)
    to_y(3)

    def spread(ref, b0):
        values = ref[...].astype(BF)
        at = lax.broadcasted_iota(jnp.int32, (128, 128), 0)
        return jnp.concatenate(
            [dot(values, (at == b0 + j).astype(F32).astype(BF)) for j in range(chunk)], 0
        )

    def one_hot(ref, b0):
        value = spread(ref, b0)
        lane = lax.broadcasted_iota(jnp.int32, (rows, 128), 1).astype(F32)
        return jnp.concatenate([(value == lane).astype(F32), (value == lane + 128.0).astype(F32)], 1)

    def place_hot(b0):
        r = lax.broadcasted_iota(jnp.int32, (rows, 128), 0)
        lane = lax.broadcasted_iota(jnp.int32, (rows, 128), 1).astype(F32)
        p = ((b0 + r // res) * STRIDE + part * res + r % res).astype(F32)
        third = jnp.floor((p + 0.5) * (1.0 / 3.0))
        line = jnp.floor((third + 0.5) * (1.0 / SIDE))
        hits = (lane == line) | (lane == SIDE + third - SIDE * line)
        return (hits | (lane == 2 * SIDE + p - 3.0 * third)).astype(F32)

    def loop(count, body, between=()):
        def inner(i, carry):
            if between:
                pl.when(i == count - 1)(lambda: [step() for step in between] and None)
            body(i)
            return carry

        lax.fori_loop(0, count, inner, 0)

    def embed(i):
        b0 = i * chunk
        hot = jnp.concatenate([one_hot(ids_s, b0), place_hot(b0)], 1).astype(BF)
        x = dot_nt(hot, table(rest, (C_TOK[0], C_POS[1])))
        x_s[0, pl.ds(b0, chunk)] = x.reshape(chunk, res, D)

    loop(chunks, embed)
    to_core(2)
    to_y(4)

    def exchange(l, k):
        mine = kv_s.at[l, pl.ds(1, blocks), 0]
        there = kv_s.at[l, pl.ds(1, blocks), group - 1 - k]
        return push(mine, there, kv_send.at[k], kv_recv.at[l, k], siblings[k])

    def forward(l):
        def mix(i):
            b0 = i * chunk
            at = pl.ds(b0, chunk)
            unit, _ = normalise(x_s[l, at].reshape(rows, D))
            h = (unit * (1.0 + norm_s[4 * l]) + norm_s[4 * l + 1]).astype(BF)
            qkv = dot(h, layer_table(l, C_IN)).reshape(chunk, res, 6 * HEAD)
            q0_s[l, at] = qkv[..., :HEAD].astype(BF)
            kv_s[l, pl.ds(b0 + 1, chunk), 0, :, :HEAD] = qkv[..., 2 * HEAD : 3 * HEAD].astype(BF)
            kv_s[l, pl.ds(b0 + 1, chunk), 0, :, HEAD:] = qkv[..., 4 * HEAD : 5 * HEAD].astype(BF)
            stage[at, :, :HEAD] = qkv[..., HEAD : 2 * HEAD]
            stage[at, :, HEAD : 2 * HEAD] = qkv[..., 3 * HEAD : 4 * HEAD]
            stage[at, :, 2 * HEAD :] = qkv[..., 5 * HEAD :]

        def strided(i):
            qkvs = []
            for j in range(pack):
                at = pl.ds(pl.multiple_of(8 * (i * pack + j), 8), 8)
                qkv = stage[:, at, :].reshape(side, 3 * HEAD).astype(BF)
                qkv1_s[l, i * pack + j] = qkv
                qkvs.append(qkv)
            raw = [dot_nt(qkv[:, :HEAD], qkv[:, HEAD : 2 * HEAD]) * SCALE + bias1[...] for qkv in qkvs]
            probs = softmax(jnp.concatenate(raw, 0)).astype(BF)
            p1_s[l, pl.ds(i * pack, pack)] = probs.reshape(pack, side, side)
            for j in range(pack):
                at = pl.ds(pl.multiple_of(8 * (i * pack + j), 8), 8)
                value = dot(probs[j * side : (j + 1) * side], qkvs[j][:, 2 * HEAD :])
                o1_s[:, at, :] = value.reshape(blocks, 8, HEAD)

        def window(i):
            b0 = i * batch
            kv = kv_s[l, pl.ds(b0, batch + 1)].reshape((batch + 1) * STRIDE, 2 * HEAD)
            raw = [
                dot_nt(q0_s[l, b0 + j], kv[j * STRIDE : (j + 2) * STRIDE, :HEAD]) * SCALE
                + bias0[jnp.minimum(b0 + j, 1)]
                for j in range(batch)
            ]
            probs = softmax(jnp.concatenate(raw, 0)).astype(BF)
            p0_s[l, pl.ds(b0, batch)] = probs.reshape(batch, res, 2 * STRIDE)
            for j in range(batch):
                value = dot(probs[j * res : (j + 1) * res], kv[j * STRIDE : (j + 2) * STRIDE, HEAD:])
                o_s[l, b0 + j, :, :HEAD] = value.astype(BF)

        def feed(i):
            b0 = i * chunk
            at = pl.ds(b0, chunk)
            o_s[l, at, :, HEAD:] = o1_s[at].astype(BF)
            x1 = x_s[l, at].reshape(rows, D) + dot(o_s[l, at].reshape(rows, D), layer_table(l, C_OUT))
            x1_s[l, at] = x1.reshape(chunk, res, D)
            unit, _ = normalise(x1)
            h = (unit * (1.0 + norm_s[4 * l + 2]) + norm_s[4 * l + 3]).astype(BF)
            a, slope = gelu_both(dot(h, layer_table(l, C_UP)))
            a = a.astype(BF)
            a_s[l, at] = a.reshape(chunk, res, FF)
            slope_s[l, at] = slope.astype(BF).reshape(chunk, res, FF)
            x2 = x1 + dot_nt(a, layer_table(l, C_DOWN))
            x_s[l + 1, at] = x2.reshape(chunk, res, D)

        arrived(2 + 2 * l)
        loop(chunks, mix)
        copies = [exchange(l, k) for k in range(group - 1)]
        for copy in copies:
            copy.start()
        if l == 1:
            to_core(5)
            to_y(7)
        loop(n_groups // pack, strided)
        if l == 0:
            to_core(3)
            to_y(5)
        if l == 1:
            to_core(6)
        if l == 2:
            to_core(8)
        for copy in copies:
            copy.wait()
        loop(blocks // batch, window)
        if l == 0:
            to_core(4)
        if l == 1:
            to_y(8)
        arrived(3 + 2 * l)
        loop(chunks, feed, [lambda: to_y(6)] if l == 0 else [])
        if l == 1:
            to_core(7)

    for l in range(LAYERS):
        forward(l)
    arrived(8)

    dx_s = x_s.at[LAYERS]

    def finish(i, loss):
        b0 = i * chunk
        at = pl.ds(b0, chunk)
        unit, rstd = normalise(x_s[LAYERS, at].reshape(rows, D))
        gain = norm_s[4 * LAYERS]
        h = (unit * (1.0 + gain) + norm_s[4 * LAYERS + 1]).astype(BF)
        table_head = table(rest, C_HEAD)
        logits = dot(h, table_head)
        hot = one_hot(tgt_s, b0)
        shift = logits - jnp.max(logits, -1, keepdims=True)
        e = jnp.exp(shift)
        total = jnp.sum(e, -1, keepdims=True)
        weight = spread(msk_s, b0)
        per = (
            jnp.log(total)
            - (1.0 - SMOOTHING) * jnp.sum(hot * shift, -1, keepdims=True)
            - SMOOTHING * jnp.mean(shift, -1, keepdims=True)
        )
        loss = loss + jnp.sum(weight[:, :1] * per, 0, keepdims=True)
        weight = jnp.concatenate([weight, weight], 1)
        d_logits = weight * (e * (1.0 / total) - (1.0 - SMOOTHING) * hot - SMOOTHING / V)
        d_logits = d_logits.astype(BF)
        add_to(g_rest, C_HEAD, dot_tn(h, d_logits))
        dx, g_gain, g_bias = normalise_back(dot_nt(d_logits, table_head), unit, rstd, gain)
        gnorm[4 * LAYERS] += g_gain
        gnorm[4 * LAYERS + 1] += g_bias
        dx_s[at] = dx.reshape(chunk, res, D)
        return loss

    loss = lax.fori_loop(0, chunks, finish, jnp.zeros((1, 1), F32))
    count = jnp.sum(jnp.sum(msk_s[...], 0, keepdims=True), 1, keepdims=True)
    line = lax.broadcasted_iota(jnp.int32, (8, 128), 0)
    st_img[x_img] = jnp.where(line == 0, loss, jnp.where(line == 1, count, 0.0))
    st_across = [
        push(st_img.at[x_img], st_img.at[x_img], st_send.at[k], st_recv.at[k], across[k]) for k in range(m - 1)
    ]
    for copy in st_across:
        copy.start()

    def give(l, k):
        return push(
            away_s.at[k, pl.ds(1, blocks)], back_s.at[l % 2, k], kv_send.at[k], kv_recv.at[LAYERS + l, k], siblings[k]
        )

    def backward(l, points):
        grads = g_layers.at[l % 2]
        own_s = x1_s.at[l]

        def feed(i):
            b0 = i * chunk
            at = pl.ds(b0, chunk)
            dx2 = dx_s[at].reshape(rows, D)
            g2 = dx2.astype(BF)
            a = a_s[l, at].reshape(rows, FF)
            add_to(grads, C_DOWN, dot_tn(g2, a))
            du = slope_s[l, at].reshape(rows, FF).astype(F32) * dot(g2, layer_table(l, C_DOWN))
            du = du.astype(BF)
            unit, rstd = normalise(x1_s[l, at].reshape(rows, D))
            gain = norm_s[4 * l + 2]
            h = (unit * (1.0 + gain) + norm_s[4 * l + 3]).astype(BF)
            add_to(grads, C_UP, dot_tn(h, du))
            dh = dot_nt(du, layer_table(l, C_UP))
            dx, g_gain, g_bias = normalise_back(dh, unit, rstd, gain)
            gnorm[4 * l + 2] += g_gain
            gnorm[4 * l + 3] += g_bias
            dx = dx + dx2
            dx_s[at] = dx.reshape(chunk, res, D)
            g1 = dx.astype(BF)
            add_to(grads, C_OUT, dot_tn(o_s[l, at].reshape(rows, D), g1))
            do = dot_nt(g1, layer_table(l, C_OUT)).reshape(chunk, res, D)
            do0_s[at] = do[..., :HEAD].astype(BF)
            o1_s[at] = do[..., HEAD:]

        def window(i):
            b0 = i * batch
            at = pl.ds(b0, batch)
            kv = kv_s[l, pl.ds(b0, batch + 1)].reshape((batch + 1) * STRIDE, 2 * HEAD)
            probs = p0_s[l, at].reshape(batch * res, 2 * STRIDE)
            do = [do0_s[b0 + j] for j in range(batch)]
            keys = [kv[j * STRIDE : (j + 2) * STRIDE, :HEAD] for j in range(batch)]
            dp = jnp.concatenate(
                [dot_nt(do[j], kv[j * STRIDE : (j + 2) * STRIDE, HEAD:]) for j in range(batch)], 0
            )
            wide_p = probs.astype(F32)
            ds = (wide_p * (dp - jnp.sum(wide_p * dp, -1, keepdims=True)) * SCALE).astype(BF)
            carry = edge_s[...]
            for j in range(batch):
                cut = slice(j * res, (j + 1) * res)
                dq0_s[b0 + j] = dot(ds[cut], keys[j]).astype(BF)
                dkv = jnp.concatenate([dot_tn(ds[cut], q0_s[l, b0 + j]), dot_tn(probs[cut], do[j])], 1)
                done = (carry + dkv[:STRIDE]).reshape(group, res, 2 * HEAD)
                own_s[b0 + j] = done[0]
                for k in range(group - 1):
                    away_s[k, b0 + j] = done[k + 1].astype(BF)
                carry = dkv[STRIDE:]
            edge_s[...] = carry

        def strided(i):
            probs = p1_s[l, pl.ds(i * pack, pack)].reshape(pack * side, side)
            qkvs = [qkv1_s[l, i * pack + j] for j in range(pack)]
            ats = [pl.ds(pl.multiple_of(8 * (i * pack + j), 8), 8) for j in range(pack)]
            dos = [o1_s[:, at, :].reshape(side, HEAD).astype(BF) for at in ats]
            dp = jnp.concatenate([dot_nt(do, qkv[:, 2 * HEAD :]) for do, qkv in zip(dos, qkvs)], 0)
            wide_p = probs.astype(F32)
            ds = (wide_p * (dp - jnp.sum(wide_p * dp, -1, keepdims=True)) * SCALE).astype(BF)
            for j in range(pack):
                cut = slice(j * side, (j + 1) * side)
                dq = dot(ds[cut], qkvs[j][:, HEAD : 2 * HEAD])
                dk = dot_tn(ds[cut], qkvs[j][:, :HEAD])
                dv = dot_tn(probs[cut], dos[j])
                stage[:, ats[j], :] = jnp.concatenate([dq, dk, dv], 1).reshape(blocks, 8, 3 * HEAD)

        def mixed(i):
            at = pl.ds(i * chunk, chunk)
            dkv = own_s[pl.ds(i * chunk + 1, chunk)]
            for k in range(group - 1):
                dkv = dkv + back_s[l % 2, k, at].astype(F32)
            d1 = stage[at]
            return jnp.concatenate(
                [
                    dq0_s[at],
                    d1[..., :HEAD].astype(BF),
                    dkv[..., :HEAD].astype(BF),
                    d1[..., HEAD : 2 * HEAD].astype(BF),
                    dkv[..., HEAD:].astype(BF),
                    d1[..., 2 * HEAD :].astype(BF),
                ],
                -1,
            ).reshape(rows, 6 * HEAD)

        def mix_grad(i, dqkv=None, unit=None):
            dqkv = mixed(i) if dqkv is None else dqkv
            if unit is None:
                unit, _ = normalise(x_s[l, pl.ds(i * chunk, chunk)].reshape(rows, D))
            h = (unit * (1.0 + norm_s[4 * l]) + norm_s[4 * l + 1]).astype(BF)
            add_to(grads, C_IN, dot_tn(h, dqkv))

        def mix_state(i, dqkv=None, both=None):
            at = pl.ds(i * chunk, chunk)
            dqkv = mixed(i) if dqkv is None else dqkv
            unit, rstd = normalise(x_s[l, at].reshape(rows, D)) if both is None else both
            dh = dot_nt(dqkv, layer_table(l, C_IN))
            dx, g_gain, g_bias = normalise_back(dh, unit, rstd, norm_s[4 * l])
            gnorm[4 * l] += g_gain
            gnorm[4 * l + 1] += g_bias
            dx_s[at] += dx.reshape(chunk, res, D)

        def mix(i):
            dqkv = mixed(i)
            both = normalise(x_s[l, pl.ds(i * chunk, chunk)].reshape(rows, D))
            mix_grad(i, dqkv, both[0])
            mix_state(i, dqkv, both)

        def take(point):
            for step in points.get(point, ()):
                step()

        loop(chunks, feed, points.get("feed", ()))
        take("window")
        edge_s[...] = jnp.zeros_like(edge_s)
        loop(blocks // batch, window)
        last = edge_s[...].reshape(group, res, 2 * HEAD)
        own_s[blocks] = last[0]
        for k in range(group - 1):
            away_s[k, blocks] = last[k + 1].astype(BF)
        copies = [give(l, k) for k in range(group - 1)]
        for copy in copies:
            copy.start()
        take("strided")
        loop(n_groups // pack, strided)
        for copy in copies:
            copy.wait()
        take("mix")
        if l > 0:
            loop(chunks, mix)
            take("end")
        else:
            loop(chunks, mix_grad)
            take("end")
            loop(chunks, mix_state)

    def section(index, ref, cols, base, at_once=False):
        cut = slice(base + cols[0], base + cols[1])
        grad = ref.at[..., cols[0] : cols[1]]

        def way(k, src, dst, device):
            return push(src, dst, rs_send.at[index, k], rs_recv.at[index, k], device)

        one = way(0, s1.at[..., cut], r1.at[..., cut], sibling)
        if at_once:
            direct = [
                way(1 + k, s1.at[q // 2, q % 2, :, cut], r2.at[k, :, cut], seq_id(q // 2, q % 2, core))
                for k, q in enumerate(plane)
            ]
        else:
            two = way(1, s1.at[every, 0, :, cut], r2.at[every, :, cut], beside)
            three = [
                way(1 + k, s1.at[lax.rem(z + k, depth), 1, :, cut], r2.at[depth + k - 1, :, cut], peers[k - 1])
                for k in range(1, depth)
            ]
        last = [
            way(columns + k, r4.at[x_img, :, cut], r4.at[x_img, :, cut], across[k]) for k in range(m - 1)
        ]

        def go_core():
            s1[..., cut] = grad[every, pair, 1 - core].astype(BF)
            one.start()

        def go_y():
            one.wait()
            total = grad[every, 1 - y, core] + r1[every, 1 - y, :, cut].astype(F32)
            s1[every, 0, :, cut] = total.astype(BF)
            two.start()

        def go_z():
            two.wait()
            total = grad[every, y, core] + r1[every, y, :, cut].astype(F32) + r2[every, :, cut].astype(F32)
            s1[every, 1, :, cut] = total.astype(BF)
            for copy in three:
                copy.start()

        def go_plane():
            one.wait()
            total = grad[every, pair, core] + r1[..., cut].astype(F32)
            s1[..., cut] = total.astype(BF)
            for copy in direct:
                copy.start()

        def to_img(copies, mine, first):
            for copy in copies:
                copy.wait()
            total = mine.astype(F32)
            for k in range(len(copies)):
                total = total + r2[first + k, :, cut].astype(F32)
            r4[x_img, :, cut] = total.astype(BF)
            for copy in last:
                copy.start()

        def go_img():
            to_img(three, s1[z, 1, :, cut], depth)

        def from_plane():
            to_img(direct, s1[z, y, :, cut], 0)

        def end():
            for copy in last:
                copy.wait()
            total = r4[0, :, cut].astype(F32)
            for k in range(1, m):
                total = total + r4[k, :, cut].astype(F32)
            sums[:, cut] = total
            square = jnp.sum(jnp.sum(total * total, 0, keepdims=True), 1, keepdims=True)
            squares[...] += jnp.broadcast_to(square, squares.shape)

        return (go_core, go_plane, from_plane, end) if at_once else (go_core, go_y, go_z, go_img, end)

    def of_layer(l):
        grads, base = g_layers.at[l % 2], l * C_LAYER
        return section(2 * l, grads, (C_OUT[0], C_LAYER), base), section(2 * l + 1, grads, C_IN, base, l == 0)

    (feed_two, mix_two), (feed_one, mix_one), (feed_zero, mix_zero) = (of_layer(l) for l in (2, 1, 0))
    head_sum = section(6, g_rest, C_HEAD, LAYERS * C_LAYER)
    first_sum = section(7, g_rest, (C_TOK[0], C_POS[1]), LAYERS * C_LAYER, True)

    squares[...] = jnp.zeros_like(squares)
    head_sum[0]()
    backward(
        2,
        {
            "window": [head_sum[1], feed_two[0]],
            "strided": [feed_two[1]],
            "mix": [head_sum[2]],
            "end": [mix_two[0]],
        },
    )
    backward(
        1,
        {
            "feed": [mix_two[1]],
            "window": [feed_two[2], feed_one[0]],
            "strided": [head_sum[3], feed_one[1]],
            "mix": [mix_two[2]],
            "end": [feed_two[3], head_sum[4], mix_one[0]],
        },
    )
    g_layers[0] = jnp.zeros(g_layers.shape[1:], F32)
    backward(
        0,
        {
            "feed": [mix_one[1]],
            "window": [feed_one[2], feed_zero[0], mix_two[3]],
            "strided": [feed_zero[1], feed_two[4]],
            "mix": [mix_one[2]],
            "end": [mix_zero[0], mix_two[4]],
        },
    )
    mix_zero[1]()

    def embed_back(i):
        b0 = i * chunk
        hot = jnp.concatenate([one_hot(ids_s, b0), place_hot(b0)], 1).astype(BF)
        dx = dx_s[pl.ds(b0, chunk)].reshape(rows, D)
        add_to(g_rest, (C_TOK[0], C_POS[1]), dot_tn(dx.astype(BF), hot))

    loop(chunks, embed_back)
    for i in range(2 * NORMS):
        wide[POS + i : POS + i + 1, :] = jnp.sum(gnorm[i], 0, keepdims=True)
    add_to(g_rest, C_POS, jnp.transpose(wide[...]))
    first_sum[0]()
    feed_zero[2]()
    first_sum[1]()
    feed_one[3]()
    mix_one[3]()
    mix_zero[2]()
    feed_zero[3]()
    first_sum[2]()
    for part_sum in (feed_one, mix_one, mix_zero, feed_zero, first_sum):
        part_sum[-1]()

    for copy in st_across:
        copy.wait()
    told = st_img[0]
    for k in range(1, m):
        told = told + st_img[k]
    told = jnp.where(line == 2, squares[...], told)
    st_plane[column] = told
    base = m - 1
    copies = [
        push(
            st_plane.at[column],
            st_plane.at[column],
            st_send.at[base + k],
            st_recv.at[base + k],
            seq_id(q // 2, q % 2, core),
        )
        for k, q in enumerate(plane)
    ]
    for copy in copies:
        copy.start()
    for a in range(len(parts)):
        for k in range(depth - 1):
            gather_z(a, k).wait_send()
        gather_y(a).wait_send()
        gather_core(a).wait_send()
    for copy in copies:
        copy.wait()
    told = st_plane[0]
    for k in range(1, columns):
        told = told + st_plane[k]
    st_core[core] = told
    copy = push(
        st_core.at[core], st_core.at[core], st_send.at[base + columns], st_recv.at[base + columns], sibling
    )
    copy.start()
    copy.wait()
    told = st_core[0] + st_core[1]
    count = told[1:2, :1]
    norm = jnp.sqrt(told[2:3, :1]) / count
    factor = jnp.minimum(1.0, CLIP_NORM / norm) / count
    totals[...] = jnp.where(line == 2, norm, jnp.where(line == 3, factor, told))


def adam(master, gradient, first, second):
    first = BETA_ONE * first + (1.0 - BETA_ONE) * gradient
    second = BETA_TWO * second + (1.0 - BETA_TWO) * gradient * gradient
    moved = first / (1.0 - BETA_ONE**STEP) / (jnp.sqrt(second / (1.0 - BETA_TWO**STEP)) + ADAM_EPS)
    return master - LEARN_RATE * (moved + WEIGHT_DECAY * master), first, second


def update_kernel(rows, *refs):
    sums, totals = refs[:2]
    masters, firsts, seconds = refs[2:10], refs[10:18], refs[18:26]
    outs = (refs[26:34], refs[34:42], refs[42:50])
    turned = refs[50]
    factor = totals[3:4, :1]

    def put(index, at, gradient):
        result = adam(masters[index][at], gradient * factor, firsts[index][at], seconds[index][at])
        for k in range(3):
            outs[k][index][at] = result[k]

    base = LAYERS * C_LAYER
    put(0, ..., sums[:, base + C_TOK[0] : base + C_TOK[1]])
    put(1, ..., sums[:, base + C_POS[0] : base + C_POS[0] + POS])
    put(6, ..., sums[:, base + C_HEAD[0] : base + C_HEAD[1]])
    turned[...] = jnp.transpose(sums[:, base + C_POS[0] : base + C_POS[1]])
    for i in range(NORMS):
        put(7, i, turned[POS + 2 * i : POS + 2 * i + 2, :])
    for l in range(LAYERS):
        for index, cols in ((2, C_IN), (3, C_OUT), (4, C_UP), (5, C_DOWN)):
            put(index, l, sums[:, l * C_LAYER + cols[0] : l * C_LAYER + cols[1]])


def turned(tok, pos, w_in, w_out, w_up, w_down, head, norms):
    return (tok.T, pos.T, w_in, w_out, w_up, jnp.swapaxes(w_down, 1, 2), head, norms)


def on_device(geo, pixels, loss_mask, *weights):
    masters, firsts, seconds = (turned(*weights[k : k + 8]) for k in (0, 8, 16))
    n_rows, depth, blocks, res, group = geo.rows, geo.depth, geo.blocks, geo.res, geo.group
    m = geo.m
    vmem = pl.BlockSpec(memory_space=pltpu.VMEM)
    chunk = 12
    batch = 12
    pack = 4
    n_groups = res // 8
    side = 8 * blocks
    sums, totals = pl.pallas_call(
        functools.partial(step_kernel, geo, chunk, batch, pack),
        out_shape=(
            jax.ShapeDtypeStruct((n_rows, C_ALL), F32),
            jax.ShapeDtypeStruct((8, 128), F32),
        ),
        in_specs=[vmem] * 10,
        out_specs=(vmem,) * 2,
        scratch_shapes=[
            pltpu.VMEM((depth, 2, 2, 2 * geo.own, geo.wide), BF),
            pltpu.VMEM((depth, 2, 2, n_rows, C_REST), BF),
            pltpu.VMEM((LAYERS, depth, 2, 2, n_rows, C_LAYER), BF),
            pltpu.VMEM((depth, 2, 2, n_rows, C_REST), F32),
            pltpu.VMEM((2, depth, 2, 2, n_rows, C_LAYER), F32),
            pltpu.VMEM((LAYERS + 1, blocks, res, D), F32),
            pltpu.VMEM((LAYERS, blocks + 1, res, D), F32),
            pltpu.VMEM((LAYERS, blocks, res, HEAD), BF),
            pltpu.VMEM((LAYERS, blocks + 1, group, res, 2 * HEAD), BF),
            pltpu.VMEM((LAYERS, n_groups, side, 3 * HEAD), BF),
            pltpu.VMEM((LAYERS, blocks, res, 2 * STRIDE), BF),
            pltpu.VMEM((LAYERS, n_groups, side, side), BF),
            pltpu.VMEM((LAYERS, blocks, res, D), BF),
            pltpu.VMEM((LAYERS, blocks, res, FF), BF),
            pltpu.VMEM((LAYERS, blocks, res, FF), BF),
            pltpu.VMEM((blocks, res, 3 * HEAD), F32),
            pltpu.VMEM((blocks, res, HEAD), F32),
            pltpu.VMEM((blocks, res, HEAD), BF),
            pltpu.VMEM((blocks, res, HEAD), BF),
            pltpu.VMEM((group - 1, blocks + 1, res, 2 * HEAD), BF),
            pltpu.VMEM((2, group - 1, blocks, res, 2 * HEAD), BF),
            pltpu.VMEM((STRIDE, 2 * HEAD), F32),
            pltpu.VMEM((res, 128), F32),
            pltpu.VMEM((res, 128), F32),
            pltpu.VMEM((res, 128), F32),
            pltpu.VMEM((8, 128), F32),
            pltpu.VMEM((geo.images, 2 * geo.own, 128), F32),
            pltpu.VMEM((2, res, 2 * STRIDE), F32),
            pltpu.VMEM((side, side), F32),
            pltpu.VMEM((16, 1, D), F32),
            pltpu.VMEM((2 * NORMS, 8, D), F32),
            pltpu.VMEM((128, D), F32),
            pltpu.VMEM((8, 128), F32),
            pltpu.VMEM((depth, 2, n_rows, C_ALL), BF),
            pltpu.VMEM((depth, 2, n_rows, C_ALL), BF),
            pltpu.VMEM((2 * depth - 1, n_rows, C_ALL), BF),
            pltpu.VMEM((m, n_rows, C_ALL), BF),
            pltpu.VMEM((m, 8, 128), F32),
            pltpu.VMEM((2, 8, 128), F32),
            pltpu.VMEM((2 * depth, 8, 128), F32),
            pltpu.SemaphoreType.DMA((3 + 2 * LAYERS, depth + 1)),
            pltpu.SemaphoreType.DMA((3 + 2 * LAYERS, depth + 1)),
            pltpu.SemaphoreType.DMA((group - 1,)),
            pltpu.SemaphoreType.DMA((2 * LAYERS, group - 1)),
            pltpu.SemaphoreType.DMA((2 * LAYERS + 2, 2 * depth + m)),
            pltpu.SemaphoreType.DMA((2 * LAYERS + 2, 2 * depth + m)),
            pltpu.SemaphoreType.DMA((2 * depth + m,)),
            pltpu.SemaphoreType.DMA((2 * depth + m,)),
        ],
        compiler_params=pltpu.CompilerParams(
            collective_id=0, has_side_effects=True, vmem_limit_bytes=VMEM_LIMIT
        ),
        name="step",
    )(jnp.swapaxes(pixels, 1, 2), jnp.swapaxes(loss_mask, 1, 2), *masters)

    shapes = [jax.ShapeDtypeStruct(item.shape, F32) for item in masters]
    outs = pl.pallas_call(
        functools.partial(update_kernel, n_rows),
        out_shape=shapes * 3,
        in_specs=[vmem] * 26,
        out_specs=[vmem] * 24,
        scratch_shapes=[pltpu.VMEM((128, n_rows), F32)],
        name="update",
    )(sums, totals, *masters, *firsts, *seconds)
    return (
        totals[0, 0],
        totals[1, 0],
        totals[2, 0],
        *turned(*outs[:8]),
        *turned(*outs[8:16]),
        *turned(*outs[16:]),
    )


def solution(mesh):
    pixels = P("img", None, "seq")
    weights = (
        P(None, "seq"),
        P(None, "seq"),
        P(None, "seq", None),
        P(None, "seq", None),
        P(None, "seq", None),
        P(None, None, "seq"),
        P("seq", None),
        P(None, None, "seq"),
    )

    def body(pixels, loss_mask, *rest):
        geo = Geometry(mesh.shape["seq"], mesh.shape["img"], pixels.shape[0], pixels.shape[1])
        return on_device(geo, pixels, loss_mask, *rest)

    return jax.shard_map(
        body,
        mesh=mesh,
        in_specs=(pixels, pixels) + weights * 3,
        out_specs=(P(), P(), P()) + weights * 3,
        check_vma=False,
    )
```

```python
import functools
import math

import jax
import jax.numpy as jnp
from jax import lax
from jax.experimental import pallas as pl
from jax.experimental.pallas import tpu as pltpu
from jax.sharding import PartitionSpec as P

D = 256
HEAD = 128
FF = 512
V = 256
STRIDE = 128
LAYERS = 3
NORMS = 2 * LAYERS + 1
STEP = 10
SIDE = 32
POS = 2 * SIDE + 3
CLIP_NORM = 0.05
BETA_ONE = 0.9
BETA_TWO = 0.95
LEARN_RATE = 0.1
WEIGHT_DECAY = 0.1
ADAM_EPS = 1e-08
SMOOTHING = 0.1
NORM_EPS = 1e-05
SCALE = HEAD ** (-0.5)

C_IN, C_OUT, C_UP, C_DOWN = (0, 768), (768, 1024), (1024, 1536), (1536, 2048)
C_LAYER = 2048
C_TOK, C_POS, C_HEAD = (0, 256), (256, 384), (384, 640)
C_REST = 640
C_ALL = LAYERS * C_LAYER + C_REST

BF = jnp.bfloat16
F32 = jnp.float32
VMEM_LIMIT = 64 * 1024 * 1024


def dot(a, b):
    return lax.dot_general(a, b, (((1,), (0,)), ((), ())), preferred_element_type=F32)


def dot_nt(a, b):
    return lax.dot_general(a, b, (((1,), (1,)), ((), ())), preferred_element_type=F32)


def dot_tn(a, b):
    return lax.dot_general(a, b, (((0,), (0,)), ((), ())), preferred_element_type=F32)


class Geometry:
    def __init__(self, n, m, images, blocks):
        self.n, self.m, self.images, self.blocks = n, m, images, blocks
        self.depth = n // 4
        self.rows = D // n
        self.group = n // images
        self.res = STRIDE // self.group
        self.own = STRIDE // n
        self.wide = -(-images * blocks // 128) * 128

    def place(self):
        me = lax.axis_index("seq")
        return me // 4, me // 2 % 2, me % 2


def seq_id(z, y, core):
    return {"seq": z * 4 + y * 2 + core}


def greet(devices):
    barrier = pltpu.get_barrier_semaphore()
    for device in devices:
        pl.semaphore_signal(barrier, inc=1, device_id=device, device_id_type=pl.DeviceIdType.MESH)


def greeted(devices):
    pl.semaphore_wait(pltpu.get_barrier_semaphore(), len(devices))


def push(src, dst, send_sem, recv_sem, device):
    return pltpu.make_async_remote_copy(
        src_ref=src,
        dst_ref=dst,
        send_sem=send_sem,
        recv_sem=recv_sem,
        device_id=device,
        device_id_type=pl.DeviceIdType.MESH,
    )


def normalise(x):
    centre = x - jnp.mean(x, -1, keepdims=True)
    spread = jnp.mean(centre * centre, -1, keepdims=True)
    rstd = lax.rsqrt(spread + NORM_EPS)
    return centre * rstd, rstd


def fold(x):
    return jnp.sum(x.reshape(x.shape[0] // 8, 8, x.shape[1]), 0)


def normalise_back(dy, unit, rstd, gain):
    dxh = dy * (1.0 + gain)
    mean_one = jnp.mean(dxh, -1, keepdims=True)
    mean_two = jnp.mean(dxh * unit, -1, keepdims=True)
    return rstd * (dxh - mean_one - unit * mean_two), fold(dy * unit), fold(dy)


def gelu_both(u):
    c = math.sqrt(2.0 / math.pi)
    square = u * u
    half = 0.5 + 0.5 * jnp.tanh(u * (c + (0.044715 * c) * square))
    a = u * half
    return a, half + a * (1.0 - half) * (2.0 * c + (6.0 * 0.044715 * c) * square)


def softmax(scores):
    e = jnp.exp(scores - jnp.max(scores, -1, keepdims=True))
    return e * (1.0 / jnp.sum(e, -1, keepdims=True))


def step_kernel(
    geo, chunk, batch, pack,
    pixels, mask, tok, pos, w_in, w_out, w_up, w_down, head, norms,
    sums, totals,
    px, rest, layers, g_rest, g_layers,
    x_s, unit_s, rstd_s, own_s, q0_s, kv_s, qkv1_s, p0_s, p1_s, o_s, a_s, slope_s, stage, o1_s, do0_s, dq0_s,
    away_s, back_s, edge_s, ids_s, tgt_s, msk_s, prev_s, pack_s, bias0, bias1, norm_s, gnorm, wide, squares,
    s1, r1, r2, r4, st_img, st_core, st_plane,
    g_send, g_recv, kv_send, kv_recv, rs_send, rs_recv, st_send, st_recv,
):
    z, y, core = geo.place()
    me, x_img = lax.axis_index("seq"), lax.axis_index("img")
    depth, group, res, blocks, own, m = geo.depth, geo.group, geo.res, geo.blocks, geo.own, geo.m
    image, part = me // group, me % group
    siblings = [{"seq": image * group + lax.rem(part + k, group)} for k in range(1, group)]
    peers = [seq_id(lax.rem(z + k, depth), y, core) for k in range(1, depth)]
    beside, sibling = seq_id(z, 1 - y, core), seq_id(z, y, 1 - core)
    columns = 2 * depth
    column = z * 2 + y
    plane = [lax.rem(column + k, columns) for k in range(1, columns)]
    across = [{"img": lax.rem(x_img + k, m)} for k in range(1, m)]
    others = [seq_id(q // 2, q % 2, core) for q in plane] + across + [sibling]
    if group > 2:
        others.append(seq_id(z, 1 - y, 1 - core))
    greet(others)
    rows = chunk * res
    chunks = blocks // chunk
    n_groups = res // 8
    every, pair = pl.ds(0, depth), pl.ds(0, 2)

    pack_s[...] = jnp.zeros_like(pack_s)
    pack_s[:, :own, :blocks] = pixels[...].astype(F32)
    pack_s[:, own:, :blocks] = mask[...].astype(F32)
    at = lax.broadcasted_iota(jnp.int32, (128, geo.wide), 0)
    to = lax.broadcasted_iota(jnp.int32, (128, geo.wide), 1)
    packed = jnp.zeros((2 * own, geo.wide), F32)
    for i in range(geo.images):
        spot = ((to == at + i * blocks) & (at < blocks)).astype(F32).astype(BF)
        packed = packed + dot(pack_s[i].astype(BF), spot)
    px[z, y, core] = packed.astype(BF)
    rest[z, y, core, :, C_TOK[0] : C_TOK[1]] = tok[...].astype(BF)
    wide[...] = jnp.zeros_like(wide)
    for i in range(NORMS):
        wide[POS + 2 * i : POS + 2 * i + 2, : geo.rows] = norms[i]
    flipped = jnp.transpose(wide[:, :128])[: geo.rows]
    wide[: geo.rows, :128] = flipped
    wide[: geo.rows, :POS] = pos[...]
    rest[z, y, core, :, C_POS[0] : C_POS[1]] = wide[: geo.rows, :128].astype(BF)

    parts = [px, rest.at[..., 0 : C_POS[1]]]
    for l in range(LAYERS):
        parts += [layers.at[l, ..., 0 : C_IN[1]], layers.at[l, ..., C_OUT[0] : C_LAYER]]
    parts += [rest.at[..., C_HEAD[0] : C_HEAD[1]]]

    def gather_z(a, k):
        mine = parts[a].at[z, y, core]
        return push(mine, mine, g_send.at[a, k], g_recv.at[a, k], peers[k])

    def gather_y(a):
        column = parts[a].at[every, y, core]
        return push(column, column, g_send.at[a, depth - 1], g_recv.at[a, depth - 1], beside)

    def gather_core(a):
        half = parts[a].at[every, pair, core]
        return push(half, half, g_send.at[a, depth], g_recv.at[a, depth], sibling)

    def to_y(a):
        for k in range(depth - 1):
            gather_z(a, k).wait_recv()
        gather_y(a).start()

    def to_core(a):
        gather_y(a).wait_recv()
        gather_core(a).start()

    def arrived(a):
        gather_core(a).wait_recv()

    def to_z(a):
        for k in range(depth - 1):
            gather_z(a, k).start()

    greeted(others)
    to_z(0)
    to_z(1)
    for l in range(LAYERS):
        layers[l, z, y, core, :, C_IN[0] : C_IN[1]] = w_in[l].astype(BF)
        to_z(2 + 2 * l)
        layers[l, z, y, core, :, C_OUT[0] : C_OUT[1]] = w_out[l].astype(BF)
        layers[l, z, y, core, :, C_UP[0] : C_UP[1]] = w_up[l].astype(BF)
        layers[l, z, y, core, :, C_DOWN[0] : C_DOWN[1]] = w_down[l].astype(BF)
        to_z(3 + 2 * l)
    rest[z, y, core, :, C_HEAD[0] : C_HEAD[1]] = head[...].astype(BF)
    to_z(8)

    def table(ref, cols):
        piece = ref[..., cols[0] : cols[1]]
        width = cols[1] - cols[0]
        if geo.rows % 16:
            return piece.astype(F32).reshape(D, width).astype(BF)
        return piece.reshape(D, width)

    def layer_table(l, cols):
        return table(layers.at[l], cols)

    def add_to(ref, cols, value):
        shape = (depth, 2, 2, geo.rows, cols[1] - cols[0])
        ref[..., cols[0] : cols[1]] += value.reshape(shape)

    for ref in (ids_s, tgt_s, msk_s, prev_s, wide, g_rest, g_layers, gnorm):
        ref[...] = jnp.zeros_like(ref)
    for l in range(LAYERS):
        kv_s[l, 0] = jnp.zeros((group, res, 2 * HEAD), BF)

    qi = part * res + lax.broadcasted_iota(jnp.int32, (res, 2 * STRIDE), 0)
    kj = lax.broadcasted_iota(jnp.int32, (res, 2 * STRIDE), 1)
    kj = kj // STRIDE * STRIDE + (kj % STRIDE + part * res) % STRIDE
    seen = (kj > qi) & (kj <= qi + STRIDE)
    bias0[0] = jnp.where(seen & (kj >= STRIDE), 0.0, -1e30)
    bias0[1] = jnp.where(seen, 0.0, -1e30)
    side = 8 * blocks
    ri = lax.broadcasted_iota(jnp.int32, (side, side), 0)
    ci = lax.broadcasted_iota(jnp.int32, (side, side), 1)
    bias1[...] = jnp.where(((ri & 7) == (ci & 7)) & (ri >= ci), 0.0, -1e30)

    to_y(0)
    to_y(1)
    to_y(2)
    to_core(0)
    to_core(1)
    arrived(0)

    span = depth // group
    at = lax.broadcasted_iota(jnp.int32, (geo.wide, 128), 0)
    to = lax.broadcasted_iota(jnp.int32, (geo.wide, 128), 1)
    spot = ((at == to + image * blocks) & (to < blocks)).astype(F32).astype(BF)
    for j in range(geo.images):
        piece = dot(px[part * span + j // 4, j // 2 % 2, j % 2], spot)
        tgt_s[j * own : (j + 1) * own, :] = piece[:own]
        msk_s[j * own : (j + 1) * own, :] = piece[own:]
    prev = dot(px[lax.rem(part * span + depth - 1, depth), 1, 1], spot)[:own]
    lane = lax.broadcasted_iota(jnp.int32, prev.shape, 1)
    moved = jnp.where(lane == 0, -1.0, pltpu.roll(prev, 1, 1))
    prev = jnp.where(part == 0, moved, prev)
    ids_s[0:1, :] = prev[own - 1 : own, :]
    ids_s[1:res, :] = tgt_s[0 : res - 1, :]

    arrived(1)
    wide[...] = jnp.transpose(table(rest, C_POS).astype(F32))
    for i in range(2 * NORMS):
        norm_s[i] = wide[POS + i : POS + i + 1, :]
    wide[...] = jnp.zeros_like(wide)
    to_y(3)

    def spread(ref, b0):
        values = ref[...].astype(BF)
        at = lax.broadcasted_iota(jnp.int32, (128, 128), 0)
        return jnp.concatenate(
            [dot(values, (at == b0 + j).astype(F32).astype(BF)) for j in range(chunk)], 0
        )

    def one_hot(ref, b0):
        value = spread(ref, b0)
        lane = lax.broadcasted_iota(jnp.int32, (rows, 128), 1).astype(F32)
        return jnp.concatenate([(value == lane).astype(F32), (value == lane + 128.0).astype(F32)], 1)

    def place_hot(b0):
        r = lax.broadcasted_iota(jnp.int32, (rows, 128), 0)
        lane = lax.broadcasted_iota(jnp.int32, (rows, 128), 1).astype(F32)
        p = ((b0 + r // res) * STRIDE + part * res + r % res).astype(F32)
        third = jnp.floor((p + 0.5) * (1.0 / 3.0))
        line = jnp.floor((third + 0.5) * (1.0 / SIDE))
        hits = (lane == line) | (lane == SIDE + third - SIDE * line)
        return (hits | (lane == 2 * SIDE + p - 3.0 * third)).astype(F32)

    def loop(count, body, between=()):
        def inner(i, carry):
            if between:
                pl.when(i == count - 1)(lambda: [step() for step in between] and None)
            body(i)
            return carry

        if count == 1:
            inner(0, None)
        else:
            lax.fori_loop(0, count, inner, 0)

    def embed(i):
        b0 = i * chunk
        hot = jnp.concatenate([one_hot(ids_s, b0), place_hot(b0)], 1).astype(BF)
        x = dot_nt(hot, table(rest, (C_TOK[0], C_POS[1])))
        x_s[pl.ds(b0, chunk)] = x.reshape(chunk, res, D)

    loop(chunks, embed)
    to_core(2)
    to_y(4)

    def keep(k, at, x):
        unit, rstd = normalise(x)
        unit = unit.astype(BF)
        unit_s[k, at] = unit.reshape(x.shape[0] // res, res, D)
        rstd_s[at, :, k : k + 1] = rstd.reshape(x.shape[0] // res, res, 1)
        return (unit.astype(F32) * (1.0 + norm_s[2 * k]) + norm_s[2 * k + 1]).astype(BF)

    def kept(k, at):
        unit = unit_s[k, at].reshape(rows, D).astype(F32)
        h = (unit * (1.0 + norm_s[2 * k]) + norm_s[2 * k + 1]).astype(BF)
        return h, unit, rstd_s[at, :, k : k + 1].reshape(rows, 1)

    def exchange(l, k):
        mine = kv_s.at[l, pl.ds(1, blocks), 0]
        there = kv_s.at[l, pl.ds(1, blocks), group - 1 - k]
        return push(mine, there, kv_send.at[k], kv_recv.at[l, k], siblings[k])

    def forward(l):
        def mix(i):
            b0 = i * chunk
            at = pl.ds(b0, chunk)
            h = keep(2 * l, at, x_s[at].reshape(rows, D))
            qkv = dot(h, layer_table(l, C_IN)).reshape(chunk, res, 6 * HEAD)
            q0_s[l, at] = qkv[..., :HEAD].astype(BF)
            kv_s[l, pl.ds(b0 + 1, chunk), 0, :, :HEAD] = qkv[..., 2 * HEAD : 3 * HEAD].astype(BF)
            kv_s[l, pl.ds(b0 + 1, chunk), 0, :, HEAD:] = qkv[..., 4 * HEAD : 5 * HEAD].astype(BF)
            stage[at, :, :HEAD] = qkv[..., HEAD : 2 * HEAD]
            stage[at, :, HEAD : 2 * HEAD] = qkv[..., 3 * HEAD : 4 * HEAD]
            stage[at, :, 2 * HEAD :] = qkv[..., 5 * HEAD :]

        def strided(i):
            qkvs = []
            for j in range(pack):
                at = pl.ds(pl.multiple_of(8 * (i * pack + j), 8), 8)
                qkv = stage[:, at, :].reshape(side, 3 * HEAD).astype(BF)
                qkv1_s[l, i * pack + j] = qkv
                qkvs.append(qkv)
            raw = [dot_nt(qkv[:, :HEAD], qkv[:, HEAD : 2 * HEAD]) * SCALE + bias1[...] for qkv in qkvs]
            probs = softmax(jnp.concatenate(raw, 0)).astype(BF)
            p1_s[l, pl.ds(i * pack, pack)] = probs.reshape(pack, side, side)
            for j in range(pack):
                at = pl.ds(pl.multiple_of(8 * (i * pack + j), 8), 8)
                value = dot(probs[j * side : (j + 1) * side], qkvs[j][:, 2 * HEAD :])
                o1_s[:, at, :] = value.reshape(blocks, 8, HEAD)

        def window(i):
            b0 = i * batch
            kv = kv_s[l, pl.ds(b0, batch + 1)].reshape((batch + 1) * STRIDE, 2 * HEAD)
            raw = [
                dot_nt(q0_s[l, b0 + j], kv[j * STRIDE : (j + 2) * STRIDE, :HEAD]) * SCALE
                + bias0[jnp.minimum(b0 + j, 1)]
                for j in range(batch)
            ]
            probs = softmax(jnp.concatenate(raw, 0)).astype(BF)
            p0_s[l, pl.ds(b0, batch)] = probs.reshape(batch, res, 2 * STRIDE)
            for j in range(batch):
                value = dot(probs[j * res : (j + 1) * res], kv[j * STRIDE : (j + 2) * STRIDE, HEAD:])
                o_s[l, b0 + j, :, :HEAD] = value.astype(BF)

        def feed(i):
            b0 = i * chunk
            at = pl.ds(b0, chunk)
            o_s[l, at, :, HEAD:] = o1_s[at].astype(BF)
            x1 = x_s[at].reshape(rows, D) + dot(o_s[l, at].reshape(rows, D), layer_table(l, C_OUT))
            h = keep(2 * l + 1, at, x1)
            a, slope = gelu_both(dot(h, layer_table(l, C_UP)).astype(BF))
            a_s[l, at] = a.reshape(chunk, res, FF)
            slope_s[l, at] = slope.reshape(chunk, res, FF)
            x2 = x1 + dot_nt(a, layer_table(l, C_DOWN))
            x_s[at] = x2.reshape(chunk, res, D)

        arrived(2 + 2 * l)
        loop(chunks, mix)
        copies = [exchange(l, k) for k in range(group - 1)]
        for copy in copies:
            copy.start()
        if l == 1:
            to_core(5)
            to_y(7)
        loop(n_groups // pack, strided)
        if l == 0:
            to_core(3)
            to_y(5)
        if l == 1:
            to_core(6)
        if l == 2:
            to_core(8)
        for copy in copies:
            copy.wait()
        loop(blocks // batch, window)
        if l == 0:
            to_core(4)
        if l == 1:
            to_y(8)
        arrived(3 + 2 * l)
        loop(chunks, feed, [lambda: to_y(6)] if l == 0 else [])
        if l == 1:
            to_core(7)

    for l in range(LAYERS):
        forward(l)
    arrived(8)

    dx_s = x_s

    def finish(i, loss):
        b0 = i * chunk
        at = pl.ds(b0, chunk)
        unit, rstd = normalise(x_s[at].reshape(rows, D))
        gain = norm_s[4 * LAYERS]
        h = (unit * (1.0 + gain) + norm_s[4 * LAYERS + 1]).astype(BF)
        table_head = table(rest, C_HEAD)
        logits = dot(h, table_head)
        hot = one_hot(tgt_s, b0)
        shift = logits - jnp.max(logits, -1, keepdims=True)
        e = jnp.exp(shift)
        total = jnp.sum(e, -1, keepdims=True)
        weight = spread(msk_s, b0)
        goal = (1.0 - SMOOTHING) * hot + SMOOTHING / V
        per = jnp.log(total) - jnp.sum(goal * shift, -1, keepdims=True)
        loss = loss + jnp.sum(weight[:, :1] * per, 0, keepdims=True)
        weight = jnp.concatenate([weight, weight], 1)
        d_logits = weight * (e * (1.0 / total) - goal)
        d_logits = d_logits.astype(BF)
        add_to(g_rest, C_HEAD, dot_tn(h, d_logits))
        dx, g_gain, g_bias = normalise_back(dot_nt(d_logits, table_head), unit, rstd, gain)
        gnorm[4 * LAYERS] += g_gain
        gnorm[4 * LAYERS + 1] += g_bias
        dx_s[at] = dx.reshape(chunk, res, D)
        return loss

    loss = lax.fori_loop(0, chunks, finish, jnp.zeros((1, 1), F32))
    count = jnp.sum(jnp.sum(msk_s[...], 0, keepdims=True), 1, keepdims=True)
    line = lax.broadcasted_iota(jnp.int32, (8, 128), 0)
    st_img[x_img] = jnp.where(line == 0, loss, jnp.where(line == 1, count, 0.0))
    st_across = [
        push(st_img.at[x_img], st_img.at[x_img], st_send.at[k], st_recv.at[k], across[k]) for k in range(m - 1)
    ]
    for copy in st_across:
        copy.start()

    def give(l, k):
        return push(
            away_s.at[k, pl.ds(1, blocks)], back_s.at[l % 2, k], kv_send.at[k], kv_recv.at[LAYERS + l, k], siblings[k]
        )

    def backward(l, points):
        grads = g_layers.at[l % 2]

        def feed(i):
            b0 = i * chunk
            at = pl.ds(b0, chunk)
            dx2 = dx_s[at].reshape(rows, D)
            g2 = dx2.astype(BF)
            a = a_s[l, at].reshape(rows, FF)
            add_to(grads, C_DOWN, dot_tn(g2, a))
            du = slope_s[l, at].reshape(rows, FF) * dot(g2, layer_table(l, C_DOWN)).astype(BF)
            h, unit, rstd = kept(2 * l + 1, at)
            add_to(grads, C_UP, dot_tn(h, du))
            dh = dot_nt(du, layer_table(l, C_UP))
            dx, g_gain, g_bias = normalise_back(dh, unit, rstd, norm_s[4 * l + 2])
            gnorm[4 * l + 2] += g_gain
            gnorm[4 * l + 3] += g_bias
            dx = dx + dx2
            dx_s[at] = dx.reshape(chunk, res, D)
            g1 = dx.astype(BF)
            add_to(grads, C_OUT, dot_tn(o_s[l, at].reshape(rows, D), g1))
            do = dot_nt(g1, layer_table(l, C_OUT)).reshape(chunk, res, D)
            do0_s[at] = do[..., :HEAD].astype(BF)
            o1_s[at] = do[..., HEAD:]

        def window(i):
            b0 = i * batch
            at = pl.ds(b0, batch)
            kv = kv_s[l, pl.ds(b0, batch + 1)].reshape((batch + 1) * STRIDE, 2 * HEAD)
            probs = p0_s[l, at].reshape(batch * res, 2 * STRIDE)
            do = [do0_s[b0 + j] for j in range(batch)]
            keys = [kv[j * STRIDE : (j + 2) * STRIDE, :HEAD] for j in range(batch)]
            dp = jnp.concatenate(
                [dot_nt(do[j], kv[j * STRIDE : (j + 2) * STRIDE, HEAD:]) for j in range(batch)], 0
            )
            wide_p = probs.astype(F32)
            ds = (wide_p * (dp - jnp.sum(wide_p * dp, -1, keepdims=True)) * SCALE).astype(BF)
            carry = edge_s[...]
            for j in range(batch):
                cut = slice(j * res, (j + 1) * res)
                dq0_s[b0 + j] = dot(ds[cut], keys[j]).astype(BF)
                dkv = jnp.concatenate([dot_tn(ds[cut], q0_s[l, b0 + j]), dot_tn(probs[cut], do[j])], 1)
                done = (carry + dkv[:STRIDE]).reshape(group, res, 2 * HEAD)
                own_s[b0 + j] = done[0]
                for k in range(group - 1):
                    away_s[k, b0 + j] = done[k + 1].astype(BF)
                carry = dkv[STRIDE:]
            edge_s[...] = carry

        def strided(i):
            probs = p1_s[l, pl.ds(i * pack, pack)].reshape(pack * side, side)
            qkvs = [qkv1_s[l, i * pack + j] for j in range(pack)]
            ats = [pl.ds(pl.multiple_of(8 * (i * pack + j), 8), 8) for j in range(pack)]
            dos = [o1_s[:, at, :].reshape(side, HEAD).astype(BF) for at in ats]
            dp = jnp.concatenate([dot_nt(do, qkv[:, 2 * HEAD :]) for do, qkv in zip(dos, qkvs)], 0)
            wide_p = probs.astype(F32)
            ds = (wide_p * (dp - jnp.sum(wide_p * dp, -1, keepdims=True)) * SCALE).astype(BF)
            for j in range(pack):
                cut = slice(j * side, (j + 1) * side)
                dq = dot(ds[cut], qkvs[j][:, HEAD : 2 * HEAD])
                dk = dot_tn(ds[cut], qkvs[j][:, :HEAD])
                dv = dot_tn(probs[cut], dos[j])
                stage[:, ats[j], :] = jnp.concatenate([dq, dk, dv], 1).reshape(blocks, 8, 3 * HEAD)

        def mixed(i):
            at = pl.ds(i * chunk, chunk)
            dkv = own_s[pl.ds(i * chunk + 1, chunk)]
            for k in range(group - 1):
                dkv = dkv + back_s[l % 2, k, at].astype(F32)
            d1 = stage[at]
            return jnp.concatenate(
                [
                    dq0_s[at],
                    d1[..., :HEAD].astype(BF),
                    dkv[..., :HEAD].astype(BF),
                    d1[..., HEAD : 2 * HEAD].astype(BF),
                    dkv[..., HEAD:].astype(BF),
                    d1[..., 2 * HEAD :].astype(BF),
                ],
                -1,
            ).reshape(rows, 6 * HEAD)

        def mix_grad(i, dqkv=None, h=None):
            dqkv = mixed(i) if dqkv is None else dqkv
            if h is None:
                h, _, _ = kept(2 * l, pl.ds(i * chunk, chunk))
            add_to(grads, C_IN, dot_tn(h, dqkv))

        def mix_state(i, dqkv=None, both=None):
            at = pl.ds(i * chunk, chunk)
            dqkv = mixed(i) if dqkv is None else dqkv
            unit, rstd = kept(2 * l, at)[1:] if both is None else both
            dh = dot_nt(dqkv, layer_table(l, C_IN))
            dx, g_gain, g_bias = normalise_back(dh, unit, rstd, norm_s[4 * l])
            gnorm[4 * l] += g_gain
            gnorm[4 * l + 1] += g_bias
            dx_s[at] += dx.reshape(chunk, res, D)

        def mix(i):
            dqkv = mixed(i)
            h, unit, rstd = kept(2 * l, pl.ds(i * chunk, chunk))
            mix_grad(i, dqkv, h)
            mix_state(i, dqkv, (unit, rstd))

        def take(point):
            for step in points.get(point, ()):
                step()

        loop(chunks, feed, points.get("feed", ()))
        take("window")
        edge_s[...] = jnp.zeros_like(edge_s)
        loop(blocks // batch, window)
        last = edge_s[...].reshape(group, res, 2 * HEAD)
        own_s[blocks] = last[0]
        for k in range(group - 1):
            away_s[k, blocks] = last[k + 1].astype(BF)
        copies = [give(l, k) for k in range(group - 1)]
        for copy in copies:
            copy.start()
        take("strided")
        loop(n_groups // pack, strided)
        for copy in copies:
            copy.wait()
        take("mix")
        if l > 0:
            loop(chunks, mix)
            take("end")
        else:
            loop(chunks, mix_grad)
            take("end")
            loop(chunks, mix_state)

    def section(index, ref, cols, base, at_once=False):
        cut = slice(base + cols[0], base + cols[1])
        grad = ref.at[..., cols[0] : cols[1]]

        def way(k, src, dst, device):
            return push(src, dst, rs_send.at[index, k], rs_recv.at[index, k], device)

        one = way(0, s1.at[..., cut], r1.at[..., cut], sibling)
        if at_once:
            direct = [
                way(1 + k, s1.at[q // 2, q % 2, :, cut], r2.at[k, :, cut], seq_id(q // 2, q % 2, core))
                for k, q in enumerate(plane)
            ]
        else:
            two = way(1, s1.at[every, 0, :, cut], r2.at[every, :, cut], beside)
            three = [
                way(1 + k, s1.at[lax.rem(z + k, depth), 1, :, cut], r2.at[depth + k - 1, :, cut], peers[k - 1])
                for k in range(1, depth)
            ]
        last = [
            way(columns + k, r4.at[x_img, :, cut], r4.at[x_img, :, cut], across[k]) for k in range(m - 1)
        ]

        def go_core():
            s1[..., cut] = grad[every, pair, 1 - core].astype(BF)
            one.start()

        def go_y():
            one.wait()
            total = grad[every, 1 - y, core] + r1[every, 1 - y, :, cut].astype(F32)
            s1[every, 0, :, cut] = total.astype(BF)
            two.start()

        def go_z():
            two.wait()
            total = grad[every, y, core] + r1[every, y, :, cut].astype(F32) + r2[every, :, cut].astype(F32)
            s1[every, 1, :, cut] = total.astype(BF)
            for copy in three:
                copy.start()

        def go_plane():
            one.wait()
            total = grad[every, pair, core] + r1[..., cut].astype(F32)
            s1[..., cut] = total.astype(BF)
            for copy in direct:
                copy.start()

        def to_img(copies, mine, first):
            for copy in copies:
                copy.wait()
            total = mine.astype(F32)
            for k in range(len(copies)):
                total = total + r2[first + k, :, cut].astype(F32)
            r4[x_img, :, cut] = total.astype(BF)
            for copy in last:
                copy.start()

        def go_img():
            to_img(three, s1[z, 1, :, cut], depth)

        def from_plane():
            to_img(direct, s1[z, y, :, cut], 0)

        def end():
            for copy in last:
                copy.wait()
            total = r4[0, :, cut].astype(F32)
            for k in range(1, m):
                total = total + r4[k, :, cut].astype(F32)
            sums[:, cut] = total
            square = jnp.sum(jnp.sum(total * total, 0, keepdims=True), 1, keepdims=True)
            squares[...] += jnp.broadcast_to(square, squares.shape)

        return (go_core, go_plane, from_plane, end) if at_once else (go_core, go_y, go_z, go_img, end)

    def of_layer(l):
        grads, base = g_layers.at[l % 2], l * C_LAYER
        return section(2 * l, grads, (C_OUT[0], C_LAYER), base), section(2 * l + 1, grads, C_IN, base, l == 0)

    (feed_two, mix_two), (feed_one, mix_one), (feed_zero, mix_zero) = (of_layer(l) for l in (2, 1, 0))
    head_sum = section(6, g_rest, C_HEAD, LAYERS * C_LAYER)
    first_sum = section(7, g_rest, (C_TOK[0], C_POS[1]), LAYERS * C_LAYER, True)

    squares[...] = jnp.zeros_like(squares)
    head_sum[0]()
    backward(
        2,
        {
            "window": [head_sum[1], feed_two[0]],
            "strided": [feed_two[1]],
            "mix": [head_sum[2]],
            "end": [mix_two[0]],
        },
    )
    backward(
        1,
        {
            "feed": [mix_two[1]],
            "window": [feed_two[2], feed_one[0]],
            "strided": [head_sum[3], feed_one[1]],
            "mix": [mix_two[2]],
            "end": [feed_two[3], head_sum[4], mix_one[0]],
        },
    )
    g_layers[0] = jnp.zeros(g_layers.shape[1:], F32)
    backward(
        0,
        {
            "feed": [mix_one[1]],
            "window": [feed_one[2], feed_zero[0], mix_two[3]],
            "strided": [feed_zero[1], feed_two[4]],
            "mix": [mix_one[2]],
            "end": [mix_zero[0], mix_two[4]],
        },
    )
    mix_zero[1]()

    def embed_back(i):
        b0 = i * chunk
        hot = jnp.concatenate([one_hot(ids_s, b0), place_hot(b0)], 1).astype(BF)
        dx = dx_s[pl.ds(b0, chunk)].reshape(rows, D)
        add_to(g_rest, (C_TOK[0], C_POS[1]), dot_tn(dx.astype(BF), hot))

    loop(chunks, embed_back)
    for i in range(2 * NORMS):
        wide[POS + i : POS + i + 1, :] = jnp.sum(gnorm[i], 0, keepdims=True)
    add_to(g_rest, C_POS, jnp.transpose(wide[...]))
    first_sum[0]()
    feed_zero[2]()
    first_sum[1]()
    feed_one[3]()
    mix_one[3]()
    mix_zero[2]()
    feed_zero[3]()
    first_sum[2]()
    for part_sum in (feed_one, mix_one, mix_zero, feed_zero, first_sum):
        part_sum[-1]()

    for copy in st_across:
        copy.wait()
    told = st_img[0]
    for k in range(1, m):
        told = told + st_img[k]
    told = jnp.where(line == 2, squares[...], told)
    st_plane[column] = told
    base = m - 1
    copies = [
        push(
            st_plane.at[column],
            st_plane.at[column],
            st_send.at[base + k],
            st_recv.at[base + k],
            seq_id(q // 2, q % 2, core),
        )
        for k, q in enumerate(plane)
    ]
    for copy in copies:
        copy.start()
    for a in range(len(parts)):
        for k in range(depth - 1):
            gather_z(a, k).wait_send()
        gather_y(a).wait_send()
        gather_core(a).wait_send()
    for copy in copies:
        copy.wait()
    told = st_plane[0]
    for k in range(1, columns):
        told = told + st_plane[k]
    st_core[core] = told
    copy = push(
        st_core.at[core], st_core.at[core], st_send.at[base + columns], st_recv.at[base + columns], sibling
    )
    copy.start()
    copy.wait()
    told = st_core[0] + st_core[1]
    count = told[1:2, :1]
    norm = jnp.sqrt(told[2:3, :1]) / count
    factor = jnp.minimum(1.0, CLIP_NORM / norm) / count
    totals[...] = jnp.where(line == 2, norm, jnp.where(line == 3, factor, told))


def adam(master, gradient, first, second):
    first = BETA_ONE * first + (1.0 - BETA_ONE) * gradient
    second = BETA_TWO * second + (1.0 - BETA_TWO) * gradient * gradient
    moved = first / (1.0 - BETA_ONE**STEP) / (jnp.sqrt(second / (1.0 - BETA_TWO**STEP)) + ADAM_EPS)
    return master - LEARN_RATE * (moved + WEIGHT_DECAY * master), first, second


def update_kernel(rows, *refs):
    sums, totals = refs[:2]
    masters, firsts, seconds = refs[2:10], refs[10:18], refs[18:26]
    outs = (refs[26:34], refs[34:42], refs[42:50])
    scalars, turned = refs[50:53], refs[53]
    factor = totals[3:4, :1]
    for k in range(3):
        scalars[k][0, 0] = totals[k, 0]

    def put(index, at, gradient):
        result = adam(masters[index][at], gradient * factor, firsts[index][at], seconds[index][at])
        for k in range(3):
            outs[k][index][at] = result[k]

    base = LAYERS * C_LAYER
    put(0, ..., sums[:, base + C_TOK[0] : base + C_TOK[1]])
    put(1, ..., sums[:, base + C_POS[0] : base + C_POS[0] + POS])
    put(6, ..., sums[:, base + C_HEAD[0] : base + C_HEAD[1]])
    turned[...] = jnp.transpose(sums[:, base + C_POS[0] : base + C_POS[1]])
    for i in range(NORMS):
        put(7, i, turned[POS + 2 * i : POS + 2 * i + 2, :])
    for l in range(LAYERS):
        for index, cols in ((2, C_IN), (3, C_OUT), (4, C_UP), (5, C_DOWN)):
            put(index, l, sums[:, l * C_LAYER + cols[0] : l * C_LAYER + cols[1]])


def turned(tok, pos, w_in, w_out, w_up, w_down, head, norms):
    return (tok.T, pos.T, w_in, w_out, w_up, jnp.swapaxes(w_down, 1, 2), head, norms)


def on_device(geo, pixels, loss_mask, *weights):
    masters, firsts, seconds = (turned(*weights[k : k + 8]) for k in (0, 8, 16))
    n_rows, depth, blocks, res, group = geo.rows, geo.depth, geo.blocks, geo.res, geo.group
    m = geo.m
    vmem = pl.BlockSpec(memory_space=pltpu.VMEM)
    chunk = 12
    batch = 24
    pack = 4
    n_groups = res // 8
    side = 8 * blocks
    sums, totals = pl.pallas_call(
        functools.partial(step_kernel, geo, chunk, batch, pack),
        out_shape=(
            jax.ShapeDtypeStruct((n_rows, C_ALL), F32),
            jax.ShapeDtypeStruct((8, 128), F32),
        ),
        in_specs=[vmem] * 10,
        out_specs=(vmem,) * 2,
        scratch_shapes=[
            pltpu.VMEM((depth, 2, 2, 2 * geo.own, geo.wide), BF),
            pltpu.VMEM((depth, 2, 2, n_rows, C_REST), BF),
            pltpu.VMEM((LAYERS, depth, 2, 2, n_rows, C_LAYER), BF),
            pltpu.VMEM((depth, 2, 2, n_rows, C_REST), F32),
            pltpu.VMEM((2, depth, 2, 2, n_rows, C_LAYER), F32),
            pltpu.VMEM((blocks, res, D), F32),
            pltpu.VMEM((2 * LAYERS, blocks, res, D), BF),
            pltpu.VMEM((blocks, res, 128), F32),
            pltpu.VMEM((blocks + 1, res, 2 * HEAD), F32),
            pltpu.VMEM((LAYERS, blocks, res, HEAD), BF),
            pltpu.VMEM((LAYERS, blocks + 1, group, res, 2 * HEAD), BF),
            pltpu.VMEM((LAYERS, n_groups, side, 3 * HEAD), BF),
            pltpu.VMEM((LAYERS, blocks, res, 2 * STRIDE), BF),
            pltpu.VMEM((LAYERS, n_groups, side, side), BF),
            pltpu.VMEM((LAYERS, blocks, res, D), BF),
            pltpu.VMEM((LAYERS, blocks, res, FF), BF),
            pltpu.VMEM((LAYERS, blocks, res, FF), BF),
            pltpu.VMEM((blocks, res, 3 * HEAD), F32),
            pltpu.VMEM((blocks, res, HEAD), F32),
            pltpu.VMEM((blocks, res, HEAD), BF),
            pltpu.VMEM((blocks, res, HEAD), BF),
            pltpu.VMEM((group - 1, blocks + 1, res, 2 * HEAD), BF),
            pltpu.VMEM((2, group - 1, blocks, res, 2 * HEAD), BF),
            pltpu.VMEM((STRIDE, 2 * HEAD), F32),
            pltpu.VMEM((res, 128), F32),
            pltpu.VMEM((res, 128), F32),
            pltpu.VMEM((res, 128), F32),
            pltpu.VMEM((8, 128), F32),
            pltpu.VMEM((geo.images, 2 * geo.own, 128), F32),
            pltpu.VMEM((2, res, 2 * STRIDE), F32),
            pltpu.VMEM((side, side), F32),
            pltpu.VMEM((16, 1, D), F32),
            pltpu.VMEM((2 * NORMS, 8, D), F32),
            pltpu.VMEM((128, D), F32),
            pltpu.VMEM((8, 128), F32),
            pltpu.VMEM((depth, 2, n_rows, C_ALL), BF),
            pltpu.VMEM((depth, 2, n_rows, C_ALL), BF),
            pltpu.VMEM((2 * depth - 1, n_rows, C_ALL), BF),
            pltpu.VMEM((m, n_rows, C_ALL), BF),
            pltpu.VMEM((m, 8, 128), F32),
            pltpu.VMEM((2, 8, 128), F32),
            pltpu.VMEM((2 * depth, 8, 128), F32),
            pltpu.SemaphoreType.DMA((3 + 2 * LAYERS, depth + 1)),
            pltpu.SemaphoreType.DMA((3 + 2 * LAYERS, depth + 1)),
            pltpu.SemaphoreType.DMA((group - 1,)),
            pltpu.SemaphoreType.DMA((2 * LAYERS, group - 1)),
            pltpu.SemaphoreType.DMA((2 * LAYERS + 2, 2 * depth + m)),
            pltpu.SemaphoreType.DMA((2 * LAYERS + 2, 2 * depth + m)),
            pltpu.SemaphoreType.DMA((2 * depth + m,)),
            pltpu.SemaphoreType.DMA((2 * depth + m,)),
        ],
        compiler_params=pltpu.CompilerParams(
            collective_id=0, has_side_effects=True, vmem_limit_bytes=VMEM_LIMIT
        ),
        name="step",
    )(jnp.swapaxes(pixels, 1, 2), jnp.swapaxes(loss_mask, 1, 2), *masters)

    shapes = [jax.ShapeDtypeStruct(item.shape, F32) for item in masters]
    outs = pl.pallas_call(
        functools.partial(update_kernel, n_rows),
        out_shape=shapes * 3 + [jax.ShapeDtypeStruct((1, 1), F32)] * 3,
        in_specs=[vmem] * 26,
        out_specs=[vmem] * 24 + [pl.BlockSpec(memory_space=pltpu.SMEM)] * 3,
        scratch_shapes=[pltpu.VMEM((128, n_rows), F32)],
        name="update",
    )(sums, totals, *masters, *firsts, *seconds)
    return (
        *(item.reshape(()) for item in outs[24:]),
        *turned(*outs[:8]),
        *turned(*outs[8:16]),
        *turned(*outs[16:24]),
    )


def solution(mesh):
    pixels = P("img", None, "seq")
    weights = (
        P(None, "seq"),
        P(None, "seq"),
        P(None, "seq", None),
        P(None, "seq", None),
        P(None, "seq", None),
        P(None, None, "seq"),
        P("seq", None),
        P(None, None, "seq"),
    )

    def body(pixels, loss_mask, *rest):
        geo = Geometry(mesh.shape["seq"], mesh.shape["img"], pixels.shape[0], pixels.shape[1])
        return on_device(geo, pixels, loss_mask, *rest)

    return jax.shard_map(
        body,
        mesh=mesh,
        in_specs=(pixels, pixels) + weights * 3,
        out_specs=(P(), P(), P()) + weights * 3,
        check_vma=False,
    )
```

```python
import functools
import math

import jax
import jax.numpy as jnp
from jax import lax
from jax.experimental import pallas as pl
from jax.experimental.pallas import tpu as pltpu
from jax.sharding import PartitionSpec as P

D = 256
HEAD = 128
FF = 512
V = 256
STRIDE = 128
LAYERS = 3
NORMS = 2 * LAYERS + 1
STEP = 10
SIDE = 32
POS = 2 * SIDE + 3
CLIP_NORM = 0.05
BETA_ONE = 0.9
BETA_TWO = 0.95
LEARN_RATE = 0.1
WEIGHT_DECAY = 0.1
ADAM_EPS = 1e-08
SMOOTHING = 0.1
NORM_EPS = 1e-05
SCALE = HEAD ** (-0.5)

C_IN, C_OUT, C_UP, C_DOWN = (0, 768), (768, 1024), (1024, 1536), (1536, 2048)
C_LAYER = 2048
C_TOK, C_POS, C_HEAD = (0, 256), (256, 384), (384, 640)
C_REST = 640
C_ALL = LAYERS * C_LAYER + C_REST

BF = jnp.bfloat16
F32 = jnp.float32
VMEM_LIMIT = 64 * 1024 * 1024


def dot(a, b):
    return lax.dot_general(a, b, (((1,), (0,)), ((), ())), preferred_element_type=F32)


def dot_nt(a, b):
    return lax.dot_general(a, b, (((1,), (1,)), ((), ())), preferred_element_type=F32)


def dot_tn(a, b):
    return lax.dot_general(a, b, (((0,), (0,)), ((), ())), preferred_element_type=F32)


class Geometry:
    def __init__(self, n, m, images, blocks):
        self.n, self.m, self.images, self.blocks = n, m, images, blocks
        self.depth = n // 4
        self.rows = D // n
        self.group = n // images
        self.res = STRIDE // self.group
        self.own = STRIDE // n
        self.wide = -(-images * blocks // 128) * 128

    def place(self):
        me = lax.axis_index("seq")
        return me // 4, me // 2 % 2, me % 2


def seq_id(z, y, core):
    return {"seq": z * 4 + y * 2 + core}


def greet(devices):
    barrier = pltpu.get_barrier_semaphore()
    for device in devices:
        pl.semaphore_signal(barrier, inc=1, device_id=device, device_id_type=pl.DeviceIdType.MESH)


def greeted(devices):
    pl.semaphore_wait(pltpu.get_barrier_semaphore(), len(devices))


def push(src, dst, send_sem, recv_sem, device):
    return pltpu.make_async_remote_copy(
        src_ref=src,
        dst_ref=dst,
        send_sem=send_sem,
        recv_sem=recv_sem,
        device_id=device,
        device_id_type=pl.DeviceIdType.MESH,
    )


def normalise(x):
    centre = x - jnp.mean(x, -1, keepdims=True)
    spread = jnp.mean(centre * centre, -1, keepdims=True)
    rstd = lax.rsqrt(spread + NORM_EPS)
    return centre * rstd, rstd


def fold(x):
    return jnp.sum(x.reshape(x.shape[0] // 8, 8, x.shape[1]), 0)


def normalise_back(dy, unit, rstd, gain):
    dxh = dy * (1.0 + gain)
    mean_one = jnp.mean(dxh, -1, keepdims=True)
    mean_two = jnp.mean(dxh * unit, -1, keepdims=True)
    return rstd * (dxh - mean_one - unit * mean_two), fold(dy * unit), fold(dy)


def gelu_both(u):
    c = math.sqrt(2.0 / math.pi)
    square = u * u
    half = 0.5 + 0.5 * jnp.tanh(u * (c + (0.044715 * c) * square))
    a = u * half
    return a, half + a * (1.0 - half) * (2.0 * c + (6.0 * 0.044715 * c) * square)


def softmax(scores):
    e = jnp.exp(scores - jnp.max(scores, -1, keepdims=True))
    return e * (1.0 / jnp.sum(e, -1, keepdims=True))


def step_kernel(
    geo, chunk, batch, pack,
    pixels, mask, tok, pos, w_in, w_out, w_up, w_down, head, norms,
    sums, totals,
    px, rest, layers, g_rest, g_layers,
    x_s, unit_s, rstd_s, own_s, q0_s, kv_s, qkv1_s, p0_s, p1_s, o_s, a_s, slope_s, stage, o1_s, do0_s, dq0_s,
    away_s, back_s, edge_s, ids_s, tgt_s, msk_s, prev_s, pack_s, bias0, bias1, norm_s, gnorm, wide, squares,
    s1, r1, r2, r4, r_cross, r_first, st_core, st_all,
    g_send, g_recv, kv_send, kv_recv, rs_send, rs_recv, c_send, c_recv, cb_send, cb_recv, f_send, f_recv, b_send, b_recv, st_send, st_recv,
):
    z, y, core = geo.place()
    me, x_img = lax.axis_index("seq"), lax.axis_index("img")
    depth, group, res, blocks, own, m = geo.depth, geo.group, geo.res, geo.blocks, geo.own, geo.m
    image, part = me // group, me % group
    siblings = [{"seq": image * group + lax.rem(part + k, group)} for k in range(1, group)]
    peers = [seq_id(lax.rem(z + k, depth), y, core) for k in range(1, depth)]
    beside, sibling = seq_id(z, 1 - y, core), seq_id(z, y, 1 - core)
    columns = 2 * depth
    column = z * 2 + y
    plane = [lax.rem(column + k, columns) for k in range(1, columns)]
    across = [{"img": lax.rem(x_img + k, m)} for k in range(1, m)]
    off_plane = [{**seq_id(q // 2, q % 2, core), "img": lax.rem(x_img + k, m)} for k in range(1, m) for q in plane]
    others = [seq_id(q // 2, q % 2, core) for q in plane] + across + [sibling] + off_plane
    if group > 2:
        others.append(seq_id(z, 1 - y, 1 - core))
    greet(others)
    rows = chunk * res
    chunks = blocks // chunk
    n_groups = res // 8
    every, pair = pl.ds(0, depth), pl.ds(0, 2)

    pack_s[...] = jnp.zeros_like(pack_s)
    pack_s[:, :own, :blocks] = pixels[...].astype(F32)
    pack_s[:, own:, :blocks] = mask[...].astype(F32)
    at = lax.broadcasted_iota(jnp.int32, (128, geo.wide), 0)
    to = lax.broadcasted_iota(jnp.int32, (128, geo.wide), 1)
    packed = jnp.zeros((2 * own, geo.wide), F32)
    for i in range(geo.images):
        spot = ((to == at + i * blocks) & (at < blocks)).astype(F32).astype(BF)
        packed = packed + dot(pack_s[i].astype(BF), spot)
    px[z, y, core] = packed.astype(BF)
    rest[z, y, core, :, C_TOK[0] : C_TOK[1]] = tok[...].astype(BF)
    wide[...] = jnp.zeros_like(wide)
    for i in range(NORMS):
        wide[POS + 2 * i : POS + 2 * i + 2, : geo.rows] = norms[i]
    flipped = jnp.transpose(wide[:, :128])[: geo.rows]
    wide[: geo.rows, :128] = flipped
    wide[: geo.rows, :POS] = pos[...]
    rest[z, y, core, :, C_POS[0] : C_POS[1]] = wide[: geo.rows, :128].astype(BF)

    parts = [px, rest.at[..., 0 : C_POS[1]]]
    for l in range(LAYERS):
        parts += [layers.at[l, ..., 0 : C_IN[1]], layers.at[l, ..., C_OUT[0] : C_LAYER]]
    parts += [rest.at[..., C_HEAD[0] : C_HEAD[1]]]

    def gather_z(a, k):
        mine = parts[a].at[z, y, core]
        return push(mine, mine, g_send.at[a, k], g_recv.at[a, k], peers[k])

    def gather_y(a):
        column = parts[a].at[every, y, core]
        return push(column, column, g_send.at[a, depth - 1], g_recv.at[a, depth - 1], beside)

    def gather_core(a):
        half = parts[a].at[every, pair, core]
        return push(half, half, g_send.at[a, depth], g_recv.at[a, depth], sibling)

    def to_y(a):
        for k in range(depth - 1):
            gather_z(a, k).wait_recv()
        gather_y(a).start()

    def to_core(a):
        gather_y(a).wait_recv()
        gather_core(a).start()

    def arrived(a):
        gather_core(a).wait_recv()

    def to_z(a):
        for k in range(depth - 1):
            gather_z(a, k).start()

    greeted(others)
    to_z(0)
    to_z(1)
    for l in range(LAYERS):
        layers[l, z, y, core, :, C_IN[0] : C_IN[1]] = w_in[l].astype(BF)
        to_z(2 + 2 * l)
        layers[l, z, y, core, :, C_OUT[0] : C_OUT[1]] = w_out[l].astype(BF)
        layers[l, z, y, core, :, C_UP[0] : C_UP[1]] = w_up[l].astype(BF)
        layers[l, z, y, core, :, C_DOWN[0] : C_DOWN[1]] = w_down[l].astype(BF)
        to_z(3 + 2 * l)
    rest[z, y, core, :, C_HEAD[0] : C_HEAD[1]] = head[...].astype(BF)
    to_z(8)

    def table(ref, cols):
        piece = ref[..., cols[0] : cols[1]]
        width = cols[1] - cols[0]
        if geo.rows % 16:
            return piece.astype(F32).reshape(D, width).astype(BF)
        return piece.reshape(D, width)

    def layer_table(l, cols):
        return table(layers.at[l], cols)

    def add_to(ref, cols, value):
        shape = (depth, 2, 2, geo.rows, cols[1] - cols[0])
        ref[..., cols[0] : cols[1]] += value.reshape(shape)

    for ref in (ids_s, tgt_s, msk_s, prev_s, wide, g_rest, g_layers, gnorm):
        ref[...] = jnp.zeros_like(ref)
    for l in range(LAYERS):
        kv_s[l, 0] = jnp.zeros((group, res, 2 * HEAD), BF)

    qi = part * res + lax.broadcasted_iota(jnp.int32, (res, 2 * STRIDE), 0)
    kj = lax.broadcasted_iota(jnp.int32, (res, 2 * STRIDE), 1)
    kj = kj // STRIDE * STRIDE + (kj % STRIDE + part * res) % STRIDE
    seen = (kj > qi) & (kj <= qi + STRIDE)
    bias0[0] = jnp.where(seen & (kj >= STRIDE), 0.0, -1e30)
    bias0[1] = jnp.where(seen, 0.0, -1e30)
    side = 8 * blocks
    ri = lax.broadcasted_iota(jnp.int32, (side, side), 0)
    ci = lax.broadcasted_iota(jnp.int32, (side, side), 1)
    bias1[...] = jnp.where(((ri & 7) == (ci & 7)) & (ri >= ci), 0.0, -1e30)

    to_y(0)
    to_y(1)
    to_y(2)
    to_core(0)
    to_core(1)
    arrived(0)

    span = depth // group
    at = lax.broadcasted_iota(jnp.int32, (geo.wide, 128), 0)
    to = lax.broadcasted_iota(jnp.int32, (geo.wide, 128), 1)
    spot = ((at == to + image * blocks) & (to < blocks)).astype(F32).astype(BF)
    for j in range(geo.images):
        piece = dot(px[part * span + j // 4, j // 2 % 2, j % 2], spot)
        tgt_s[j * own : (j + 1) * own, :] = piece[:own]
        msk_s[j * own : (j + 1) * own, :] = piece[own:]
    prev = dot(px[lax.rem(part * span + depth - 1, depth), 1, 1], spot)[:own]
    lane = lax.broadcasted_iota(jnp.int32, prev.shape, 1)
    moved = jnp.where(lane == 0, -1.0, pltpu.roll(prev, 1, 1))
    prev = jnp.where(part == 0, moved, prev)
    ids_s[0:1, :] = prev[own - 1 : own, :]
    ids_s[1:res, :] = tgt_s[0 : res - 1, :]

    arrived(1)
    wide[...] = jnp.transpose(table(rest, C_POS).astype(F32))
    for i in range(2 * NORMS):
        norm_s[i] = wide[POS + i : POS + i + 1, :]
    wide[...] = jnp.zeros_like(wide)
    to_y(3)

    def spread(ref, b0):
        values = ref[...].astype(BF)
        at = lax.broadcasted_iota(jnp.int32, (128, 128), 0)
        return jnp.concatenate(
            [dot(values, (at == b0 + j).astype(F32).astype(BF)) for j in range(chunk)], 0
        )

    def one_hot(ref, b0):
        value = spread(ref, b0)
        lane = lax.broadcasted_iota(jnp.int32, (rows, 128), 1).astype(F32)
        return jnp.concatenate([(value == lane).astype(F32), (value == lane + 128.0).astype(F32)], 1)

    def place_hot(b0):
        r = lax.broadcasted_iota(jnp.int32, (rows, 128), 0)
        lane = lax.broadcasted_iota(jnp.int32, (rows, 128), 1).astype(F32)
        p = ((b0 + r // res) * STRIDE + part * res + r % res).astype(F32)
        third = jnp.floor((p + 0.5) * (1.0 / 3.0))
        line = jnp.floor((third + 0.5) * (1.0 / SIDE))
        hits = (lane == line) | (lane == SIDE + third - SIDE * line)
        return (hits | (lane == 2 * SIDE + p - 3.0 * third)).astype(F32)

    def loop(count, body, between=()):
        def inner(i, carry):
            if between:
                pl.when(i == count - 1)(lambda: [step() for step in between] and None)
            body(i)
            return carry

        if count == 1:
            inner(0, None)
        else:
            lax.fori_loop(0, count, inner, 0)

    def embed(i):
        b0 = i * chunk
        hot = jnp.concatenate([one_hot(ids_s, b0), place_hot(b0)], 1).astype(BF)
        x = dot_nt(hot, table(rest, (C_TOK[0], C_POS[1])))
        x_s[pl.ds(b0, chunk)] = x.reshape(chunk, res, D)

    loop(chunks, embed)
    to_core(2)
    to_y(4)

    def keep(k, at, x):
        unit, rstd = normalise(x)
        unit = unit.astype(BF)
        unit_s[k, at] = unit.reshape(x.shape[0] // res, res, D)
        rstd_s[at, :, k : k + 1] = rstd.reshape(x.shape[0] // res, res, 1)
        return (unit.astype(F32) * (1.0 + norm_s[2 * k]) + norm_s[2 * k + 1]).astype(BF)

    def kept(k, at):
        unit = unit_s[k, at].reshape(rows, D).astype(F32)
        h = (unit * (1.0 + norm_s[2 * k]) + norm_s[2 * k + 1]).astype(BF)
        return h, unit, rstd_s[at, :, k : k + 1].reshape(rows, 1)

    def exchange(l, k):
        mine = kv_s.at[l, pl.ds(1, blocks), 0]
        there = kv_s.at[l, pl.ds(1, blocks), group - 1 - k]
        return push(mine, there, kv_send.at[k], kv_recv.at[l, k], siblings[k])

    def forward(l):
        def mix(i):
            b0 = i * chunk
            at = pl.ds(b0, chunk)
            h = keep(2 * l, at, x_s[at].reshape(rows, D))
            qkv = dot(h, layer_table(l, C_IN)).reshape(chunk, res, 6 * HEAD)
            q0_s[l, at] = qkv[..., :HEAD].astype(BF)
            kv_s[l, pl.ds(b0 + 1, chunk), 0, :, :HEAD] = qkv[..., 2 * HEAD : 3 * HEAD].astype(BF)
            kv_s[l, pl.ds(b0 + 1, chunk), 0, :, HEAD:] = qkv[..., 4 * HEAD : 5 * HEAD].astype(BF)
            stage[at, :, :HEAD] = qkv[..., HEAD : 2 * HEAD]
            stage[at, :, HEAD : 2 * HEAD] = qkv[..., 3 * HEAD : 4 * HEAD]
            stage[at, :, 2 * HEAD :] = qkv[..., 5 * HEAD :]

        def strided(i):
            qkvs = []
            for j in range(pack):
                at = pl.ds(pl.multiple_of(8 * (i * pack + j), 8), 8)
                qkv = stage[:, at, :].reshape(side, 3 * HEAD).astype(BF)
                qkv1_s[l, i * pack + j] = qkv
                qkvs.append(qkv)
            raw = [dot_nt(qkv[:, :HEAD], qkv[:, HEAD : 2 * HEAD]) * SCALE + bias1[...] for qkv in qkvs]
            probs = softmax(jnp.concatenate(raw, 0)).astype(BF)
            p1_s[l, pl.ds(i * pack, pack)] = probs.reshape(pack, side, side)
            for j in range(pack):
                at = pl.ds(pl.multiple_of(8 * (i * pack + j), 8), 8)
                value = dot(probs[j * side : (j + 1) * side], qkvs[j][:, 2 * HEAD :])
                o1_s[:, at, :] = value.reshape(blocks, 8, HEAD)

        def window(i):
            b0 = i * batch
            kv = kv_s[l, pl.ds(b0, batch + 1)].reshape((batch + 1) * STRIDE, 2 * HEAD)
            raw = [
                dot_nt(q0_s[l, b0 + j], kv[j * STRIDE : (j + 2) * STRIDE, :HEAD]) * SCALE
                + bias0[jnp.minimum(b0 + j, 1)]
                for j in range(batch)
            ]
            probs = softmax(jnp.concatenate(raw, 0)).astype(BF)
            p0_s[l, pl.ds(b0, batch)] = probs.reshape(batch, res, 2 * STRIDE)
            for j in range(batch):
                value = dot(probs[j * res : (j + 1) * res], kv[j * STRIDE : (j + 2) * STRIDE, HEAD:])
                o_s[l, b0 + j, :, :HEAD] = value.astype(BF)

        def feed(i):
            b0 = i * chunk
            at = pl.ds(b0, chunk)
            o_s[l, at, :, HEAD:] = o1_s[at].astype(BF)
            x1 = x_s[at].reshape(rows, D) + dot(o_s[l, at].reshape(rows, D), layer_table(l, C_OUT))
            h = keep(2 * l + 1, at, x1)
            a, slope = gelu_both(dot(h, layer_table(l, C_UP)).astype(BF))
            a_s[l, at] = a.reshape(chunk, res, FF)
            slope_s[l, at] = slope.reshape(chunk, res, FF)
            x2 = x1 + dot_nt(a, layer_table(l, C_DOWN))
            x_s[at] = x2.reshape(chunk, res, D)

        arrived(2 + 2 * l)
        loop(chunks, mix)
        copies = [exchange(l, k) for k in range(group - 1)]
        for copy in copies:
            copy.start()
        if l == 1:
            to_core(5)
            to_y(7)
        loop(n_groups // pack, strided)
        if l == 0:
            to_core(3)
            to_y(5)
        if l == 1:
            to_core(6)
        if l == 2:
            to_core(8)
        for copy in copies:
            copy.wait()
        loop(blocks // batch, window)
        if l == 0:
            to_core(4)
        if l == 1:
            to_y(8)
        arrived(3 + 2 * l)
        loop(chunks, feed, [lambda: to_y(6)] if l == 0 else [])
        if l == 1:
            to_core(7)

    for l in range(LAYERS):
        forward(l)
    arrived(8)

    dx_s = x_s

    def finish(i, loss):
        b0 = i * chunk
        at = pl.ds(b0, chunk)
        unit, rstd = normalise(x_s[at].reshape(rows, D))
        gain = norm_s[4 * LAYERS]
        h = (unit * (1.0 + gain) + norm_s[4 * LAYERS + 1]).astype(BF)
        table_head = table(rest, C_HEAD)
        logits = dot(h, table_head)
        hot = one_hot(tgt_s, b0)
        shift = logits - jnp.max(logits, -1, keepdims=True)
        e = jnp.exp(shift)
        total = jnp.sum(e, -1, keepdims=True)
        weight = spread(msk_s, b0)
        goal = (1.0 - SMOOTHING) * hot + SMOOTHING / V
        per = jnp.log(total) - jnp.sum(goal * shift, -1, keepdims=True)
        loss = loss + jnp.sum(weight[:, :1] * per, 0, keepdims=True)
        weight = jnp.concatenate([weight, weight], 1)
        d_logits = weight * (e * (1.0 / total) - goal)
        d_logits = d_logits.astype(BF)
        add_to(g_rest, C_HEAD, dot_tn(h, d_logits))
        dx, g_gain, g_bias = normalise_back(dot_nt(d_logits, table_head), unit, rstd, gain)
        gnorm[4 * LAYERS] += g_gain
        gnorm[4 * LAYERS + 1] += g_bias
        dx_s[at] = dx.reshape(chunk, res, D)
        return loss

    loss = lax.fori_loop(0, chunks, finish, jnp.zeros((1, 1), F32))
    count = jnp.sum(jnp.sum(msk_s[...], 0, keepdims=True), 1, keepdims=True)
    line = lax.broadcasted_iota(jnp.int32, (8, 128), 0)
    told = jnp.where(line == 0, loss, jnp.where(line == 1, count, 0.0))

    def give(l, k):
        return push(
            away_s.at[k, pl.ds(1, blocks)], back_s.at[l % 2, k], kv_send.at[k], kv_recv.at[LAYERS + l, k], siblings[k]
        )

    def backward(l, points):
        grads = g_layers.at[l % 2]

        def feed(i):
            b0 = i * chunk
            at = pl.ds(b0, chunk)
            dx2 = dx_s[at].reshape(rows, D)
            g2 = dx2.astype(BF)
            a = a_s[l, at].reshape(rows, FF)
            du = slope_s[l, at].reshape(rows, FF) * dot(g2, layer_table(l, C_DOWN)).astype(BF)
            h, unit, rstd = kept(2 * l + 1, at)
            dh = dot_nt(du, layer_table(l, C_UP))
            add_to(grads, C_DOWN, dot_tn(g2, a))
            dx, g_gain, g_bias = normalise_back(dh, unit, rstd, norm_s[4 * l + 2])
            add_to(grads, C_UP, dot_tn(h, du))
            gnorm[4 * l + 2] += g_gain
            gnorm[4 * l + 3] += g_bias
            dx = dx + dx2
            dx_s[at] = dx.reshape(chunk, res, D)
            g1 = dx.astype(BF)
            add_to(grads, C_OUT, dot_tn(o_s[l, at].reshape(rows, D), g1))
            do = dot_nt(g1, layer_table(l, C_OUT)).reshape(chunk, res, D)
            do0_s[at] = do[..., :HEAD].astype(BF)
            o1_s[at] = do[..., HEAD:]

        def window(i):
            b0 = i * batch
            at = pl.ds(b0, batch)
            kv = kv_s[l, pl.ds(b0, batch + 1)].reshape((batch + 1) * STRIDE, 2 * HEAD)
            probs = p0_s[l, at].reshape(batch * res, 2 * STRIDE)
            do = [do0_s[b0 + j] for j in range(batch)]
            keys = [kv[j * STRIDE : (j + 2) * STRIDE, :HEAD] for j in range(batch)]
            dp = jnp.concatenate(
                [dot_nt(do[j], kv[j * STRIDE : (j + 2) * STRIDE, HEAD:]) for j in range(batch)], 0
            )
            wide_p = probs.astype(F32)
            ds = (wide_p * (dp - jnp.sum(wide_p * dp, -1, keepdims=True)) * SCALE).astype(BF)
            carry = edge_s[...]
            for j in range(batch):
                cut = slice(j * res, (j + 1) * res)
                dq0_s[b0 + j] = dot(ds[cut], keys[j]).astype(BF)
                dkv = jnp.concatenate([dot_tn(ds[cut], q0_s[l, b0 + j]), dot_tn(probs[cut], do[j])], 1)
                done = (carry + dkv[:STRIDE]).reshape(group, res, 2 * HEAD)
                own_s[b0 + j] = done[0]
                for k in range(group - 1):
                    away_s[k, b0 + j] = done[k + 1].astype(BF)
                carry = dkv[STRIDE:]
            edge_s[...] = carry

        def strided(i):
            probs = p1_s[l, pl.ds(i * pack, pack)].reshape(pack * side, side)
            qkvs = [qkv1_s[l, i * pack + j] for j in range(pack)]
            ats = [pl.ds(pl.multiple_of(8 * (i * pack + j), 8), 8) for j in range(pack)]
            dos = [o1_s[:, at, :].reshape(side, HEAD).astype(BF) for at in ats]
            dp = jnp.concatenate([dot_nt(do, qkv[:, 2 * HEAD :]) for do, qkv in zip(dos, qkvs)], 0)
            wide_p = probs.astype(F32)
            ds = (wide_p * (dp - jnp.sum(wide_p * dp, -1, keepdims=True)) * SCALE).astype(BF)
            for j in range(pack):
                cut = slice(j * side, (j + 1) * side)
                dq = dot(ds[cut], qkvs[j][:, HEAD : 2 * HEAD])
                dk = dot_tn(ds[cut], qkvs[j][:, :HEAD])
                dv = dot_tn(probs[cut], dos[j])
                stage[:, ats[j], :] = jnp.concatenate([dq, dk, dv], 1).reshape(blocks, 8, 3 * HEAD)

        def mixed(i):
            at = pl.ds(i * chunk, chunk)
            dkv = own_s[pl.ds(i * chunk + 1, chunk)]
            for k in range(group - 1):
                dkv = dkv + back_s[l % 2, k, at].astype(F32)
            d1 = stage[at]
            return jnp.concatenate(
                [
                    dq0_s[at],
                    d1[..., :HEAD].astype(BF),
                    dkv[..., :HEAD].astype(BF),
                    d1[..., HEAD : 2 * HEAD].astype(BF),
                    dkv[..., HEAD:].astype(BF),
                    d1[..., 2 * HEAD :].astype(BF),
                ],
                -1,
            ).reshape(rows, 6 * HEAD)

        def mix_grad(i, dqkv=None, h=None):
            dqkv = mixed(i) if dqkv is None else dqkv
            if h is None:
                h, _, _ = kept(2 * l, pl.ds(i * chunk, chunk))
            add_to(grads, C_IN, dot_tn(h, dqkv))

        def mix_state(i, dqkv=None, both=None):
            at = pl.ds(i * chunk, chunk)
            dqkv = mixed(i) if dqkv is None else dqkv
            unit, rstd = kept(2 * l, at)[1:] if both is None else both
            dh = dot_nt(dqkv, layer_table(l, C_IN))
            dx, g_gain, g_bias = normalise_back(dh, unit, rstd, norm_s[4 * l])
            gnorm[4 * l] += g_gain
            gnorm[4 * l + 1] += g_bias
            dx_s[at] += dx.reshape(chunk, res, D)

        def mix(i):
            dqkv = mixed(i)
            h, unit, rstd = kept(2 * l, pl.ds(i * chunk, chunk))
            mix_grad(i, dqkv, h)
            mix_state(i, dqkv, (unit, rstd))

        def take(point):
            for step in points.get(point, ()):
                step()

        loop(chunks, feed, points.get("feed", ()))
        take("window")
        edge_s[...] = jnp.zeros_like(edge_s)
        loop(blocks // batch, window)
        last = edge_s[...].reshape(group, res, 2 * HEAD)
        own_s[blocks] = last[0]
        for k in range(group - 1):
            away_s[k, blocks] = last[k + 1].astype(BF)
        copies = [give(l, k) for k in range(group - 1)]
        for copy in copies:
            copy.start()
        take("strided")
        loop(n_groups // pack, strided)
        for copy in copies:
            copy.wait()
        take("mix")
        if l > 0:
            loop(chunks, mix)
            take("end")
        else:
            loop(chunks, mix_grad)
            take("end")
            loop(chunks, mix_state)

    def section(index, ref, cols, base, at_once=False):
        cut = slice(base + cols[0], base + cols[1])
        grad = ref.at[..., cols[0] : cols[1]]

        def way(k, src, dst, device):
            return push(src, dst, rs_send.at[index, k], rs_recv.at[index, k], device)

        one = way(0, s1.at[..., cut], r1.at[..., cut], sibling)
        def two():
            return way(1, s1.at[every, 0, :, cut], r2.at[every, :, cut], beside)

        def three(k):
            return way(1 + k, s1.at[lax.rem(z + k, depth), 1, :, cut], r2.at[depth + k - 1, :, cut], peers[k - 1])

        def direct(k):
            q = plane[k - 1]
            return way(k, s1.at[q // 2, q % 2, :, cut], r2.at[k - 1, :, cut], seq_id(q // 2, q % 2, core))

        def last(k):
            return way(columns + k - 1, r4.at[x_img, :, cut], r4.at[x_img, :, cut], across[k - 1])

        def go_core():
            s1[..., cut] = grad[every, pair, 1 - core].astype(BF)
            one.start()

        def go_y():
            one.wait()
            total = grad[every, 1 - y, core] + r1[every, 1 - y, :, cut].astype(F32)
            s1[every, 0, :, cut] = total.astype(BF)
            two().start()

        def go_z():
            two().wait()
            total = grad[every, y, core] + r1[every, y, :, cut].astype(F32) + r2[every, :, cut].astype(F32)
            s1[every, 1, :, cut] = total.astype(BF)
            for k in range(1, depth):
                three(k).start()

        def go_plane(start=True):
            one.wait()
            total = grad[every, pair, core] + r1[..., cut].astype(F32)
            s1[..., cut] = total.astype(BF)
            if start:
                for k in range(1, columns):
                    direct(k).start()

        def to_img(copy, number, mine, first):
            for k in range(1, number):
                copy(k).wait()
            total = mine.astype(F32)
            for k in range(1, number):
                total = total + r2[first + k - 1, :, cut].astype(F32)
            r4[x_img, :, cut] = total.astype(BF)
            for k in range(1, m):
                last(k).start()

        def go_img():
            to_img(three, depth, s1[z, 1, :, cut], depth)

        def from_plane():
            to_img(direct, columns, s1[z, y, :, cut], 0)

        def end():
            for k in range(1, m):
                last(k).wait()
            total = r4[0, :, cut].astype(F32)
            for k in range(1, m):
                total = total + r4[k, :, cut].astype(F32)
            sums[:, cut] = total
            square = jnp.sum(jnp.sum(total * total, 0, keepdims=True), 1, keepdims=True)
            squares[...] += jnp.broadcast_to(square, squares.shape)

        return (go_core, go_plane, from_plane, end) if at_once else (go_core, go_y, go_z, go_img, end)

    def crossed(index, ref, cols, base):
        tiles = (cols[1] - cols[0]) // 128
        cut = slice(base + cols[0], base + cols[1])
        grad = ref.at[..., cols[0] : cols[1]]
        ends = [128 * (tiles * p // m) for p in range(m + 1)]
        shares = [slice(cut.start + ends[p], cut.start + ends[p + 1]) for p in range(m)]
        widths = [ends[p + 1] - ends[p] for p in range(m)]
        one = push(s1.at[..., cut], r1.at[..., cut], rs_send.at[index, 0], rs_recv.at[index, 0], sibling)

        def over(p, group_at):
            there = r_cross.at[group_at, every, pair, :, 0 : widths[p]]
            return push(s1.at[..., shares[p]], there, c_send.at[p], c_recv.at[group_at], {"img": p})

        def direct(p, k):
            q = plane[k - 1]
            return push(
                s1.at[q // 2, q % 2, :, shares[p]],
                r2.at[k - 1, :, shares[p]],
                rs_send.at[index, k],
                rs_recv.at[index, k],
                seq_id(q // 2, q % 2, core),
            )

        def share(p, k):
            there = sums.at[:, shares[p]]
            return push(there, there, cb_send.at[k], cb_recv.at[p], across[k])

        def mine(p, step):
            if widths[p]:
                pl.when(x_img == p)(step)

        def not_mine(p, step):
            if widths[p]:
                pl.when(x_img != p)(step)

        def go_core():
            s1[..., cut] = grad[every, pair, 1 - core].astype(BF)
            one.start()

        def go_img():
            one.wait()
            total = grad[every, pair, core] + r1[..., cut].astype(F32)
            s1[..., cut] = total.astype(BF)
            for p in range(m):
                not_mine(p, lambda: over(p, x_img).start())

        def go_plane():
            for p in range(m):

                def step():
                    total = s1[..., shares[p]].astype(F32)
                    for group_at in range(m):
                        if group_at != p:
                            over(p, group_at).wait_recv()
                            total = total + r_cross[group_at, ..., 0 : widths[p]].astype(F32)
                    s1[..., shares[p]] = total.astype(BF)
                    for k in range(1, columns):
                        direct(p, k).start()

                mine(p, step)

        def end():
            for p in range(m):

                def step():
                    total = s1[z, y, :, shares[p]].astype(F32)
                    for k in range(1, columns):
                        direct(p, k).wait()
                        total = total + r2[k - 1, :, shares[p]].astype(F32)
                    sums[:, shares[p]] = total
                    for k in range(m - 1):
                        share(p, k).start()
                    square = jnp.sum(jnp.sum(total * total, 0, keepdims=True), 1, keepdims=True)
                    squares[...] += jnp.broadcast_to(square, squares.shape)

                mine(p, step)

        def drain():
            for p in range(m):

                def sent():
                    over(p, x_img).wait_send()
                    share(p, 0).wait_recv()

                def shared():
                    for k in range(m - 1):
                        share(p, k).wait_send()

                not_mine(p, sent)
                mine(p, shared)

        return go_core, go_img, go_plane, end, drain

    def of_layer(l):
        grads, base = g_layers.at[l % 2], l * C_LAYER
        kind = crossed if l == 0 else section
        return kind(2 * l, grads, (C_OUT[0], C_LAYER), base), section(2 * l + 1, grads, C_IN, base, l == 0)

    (feed_two, mix_two), (feed_one, mix_one), (feed_zero, mix_zero) = (of_layer(l) for l in (2, 1, 0))
    head_sum = section(6, g_rest, C_HEAD, LAYERS * C_LAYER)
    first_sum = section(7, g_rest, (C_TOK[0], C_POS[1]), LAYERS * C_LAYER, True)

    first_base = LAYERS * C_LAYER
    first_cuts = [slice(first_base + 128 * b, first_base + 128 * (b + 1)) for b in range(C_POS[1] // 128)]

    def first_send(b, k):
        own_place = k == columns - 1
        q = column if own_place else plane[k]
        device = {"img": b % m} if own_place else {**seq_id(q // 2, q % 2, core), "img": b % m}
        here = s1.at[q // 2, q % 2, :, first_cuts[b]]
        there = r_first.at[x_img, k, :, 128 * b : 128 * (b + 1)]
        return push(here, there, f_send.at[b, k], f_recv.at[b, x_img, k], device)

    def first_came(b, group_at, k):
        there = r_first.at[group_at, k, :, 128 * b : 128 * (b + 1)]
        return push(there, there, f_send.at[b, k], f_recv.at[b, group_at, k], sibling)

    def first_share(b, k):
        there = sums.at[:, first_cuts[b]]
        return push(there, there, b_send.at[b, k], b_recv.at[b], across[k])

    def first_start():
        first_sum[1](start=False)
        for b in range(len(first_cuts)):
            for k in range(columns - 1):
                first_send(b, k).start()

            @pl.when(x_img != b % m)
            def _():
                first_send(b, columns - 1).start()

    def first_end():
        for b in range(len(first_cuts)):

            @pl.when(x_img == b % m)
            def _():
                total = s1[z, y, :, first_cuts[b]].astype(F32)
                for group_at in range(m):
                    for k in range(columns - 1):
                        first_came(b, group_at, k).wait_recv()
                        total = total + r_first[group_at, k, :, 128 * b : 128 * (b + 1)].astype(F32)
                    if group_at != b % m:
                        first_came(b, group_at, columns - 1).wait_recv()
                        total = total + r_first[group_at, columns - 1, :, 128 * b : 128 * (b + 1)].astype(F32)
                sums[:, first_cuts[b]] = total
                for k in range(m - 1):
                    first_share(b, k).start()
                square = jnp.sum(jnp.sum(total * total, 0, keepdims=True), 1, keepdims=True)
                squares[...] += jnp.broadcast_to(square, squares.shape)

    def first_drain():
        for b in range(len(first_cuts)):
            for k in range(columns - 1):
                first_send(b, k).wait_send()

            @pl.when(x_img != b % m)
            def _():
                first_send(b, columns - 1).wait_send()
                first_share(b, 0).wait_recv()

            @pl.when(x_img == b % m)
            def _():
                for k in range(m - 1):
                    first_share(b, k).wait_send()

    squares[...] = jnp.zeros_like(squares)
    head_sum[0]()
    backward(
        2,
        {
            "window": [head_sum[1], feed_two[0]],
            "strided": [feed_two[1]],
            "mix": [head_sum[2]],
            "end": [mix_two[0]],
        },
    )
    backward(
        1,
        {
            "feed": [mix_two[1]],
            "window": [feed_two[2], feed_one[0]],
            "strided": [head_sum[3], feed_one[1]],
            "mix": [mix_two[2]],
            "end": [feed_two[3], head_sum[4], mix_one[0]],
        },
    )
    g_layers[0] = jnp.zeros(g_layers.shape[1:], F32)
    backward(
        0,
        {
            "feed": [mix_one[1]],
            "window": [feed_one[2], feed_zero[0], mix_two[3]],
            "strided": [feed_zero[1], feed_two[4]],
            "mix": [mix_one[2]],
            "end": [mix_zero[0], mix_two[4]],
        },
    )
    mix_zero[1]()

    def embed_back(i):
        b0 = i * chunk
        hot = jnp.concatenate([one_hot(ids_s, b0), place_hot(b0)], 1).astype(BF)
        dx = dx_s[pl.ds(b0, chunk)].reshape(rows, D)
        add_to(g_rest, (C_TOK[0], C_POS[1]), dot_tn(dx.astype(BF), hot))

    loop(chunks, embed_back)
    for i in range(2 * NORMS):
        wide[POS + i : POS + i + 1, :] = jnp.sum(gnorm[i], 0, keepdims=True)
    add_to(g_rest, C_POS, jnp.transpose(wide[...]))
    first_sum[0]()
    first_start()
    feed_zero[2]()
    feed_one[3]()
    mix_one[3]()
    mix_zero[2]()
    for part_sum in (feed_one, mix_one, mix_zero):
        part_sum[-1]()
    squares[...] = jnp.where(x_img == 0, squares[...], 0.0)
    first_end()
    feed_zero[3]()

    told = jnp.where(line == 2, squares[...], told)
    st_all[x_img, column] = told
    mine = st_all.at[x_img, column]
    plane_places = [(x_img, q) for q in plane]
    plane_places += [(lax.rem(x_img + k, m), lax.rem(column + j, columns)) for k in range(1, m) for j in range(columns)]
    copies = []
    for k, (group_at, q) in enumerate(plane_places, 1):
        spot = (k // columns, k % columns)
        device = {**seq_id(q // 2, q % 2, core), "img": group_at}
        copies.append(push(mine, mine, st_send.at[spot], st_recv.at[spot], device))
    for copy in copies:
        copy.start()
    for a in range(len(parts)):
        for k in range(depth - 1):
            gather_z(a, k).wait_send()
        gather_y(a).wait_send()
        gather_core(a).wait_send()
    for copy in copies:
        copy.wait()
    told = jnp.zeros((8, 128), F32)
    for group_at in range(m):
        for q in range(columns):
            told = told + st_all[group_at, q]
    st_core[core] = told
    copy = push(st_core.at[core], st_core.at[core], st_send.at[0, 0], st_recv.at[0, 0], sibling)
    copy.start()
    first_drain()
    feed_zero[4]()
    copy.wait()
    told = st_core[0] + st_core[1]
    count = told[1:2, :1]
    norm = jnp.sqrt(told[2:3, :1]) / count
    factor = jnp.minimum(1.0, CLIP_NORM / norm) / count
    totals[...] = jnp.where(line == 2, norm, jnp.where(line == 3, factor, told))


def adam(master, gradient, first, second):
    first = BETA_ONE * first + (1.0 - BETA_ONE) * gradient
    second = BETA_TWO * second + (1.0 - BETA_TWO) * gradient * gradient
    moved = first / (1.0 - BETA_ONE**STEP) / (jnp.sqrt(second / (1.0 - BETA_TWO**STEP)) + ADAM_EPS)
    return master - LEARN_RATE * (moved + WEIGHT_DECAY * master), first, second


def update_kernel(rows, *refs):
    sums, totals = refs[:2]
    masters, firsts, seconds = refs[2:10], refs[10:18], refs[18:26]
    outs = (refs[26:34], refs[34:42], refs[42:50])
    scalars, turned = refs[50:53], refs[53]
    factor = totals[3:4, :1]
    for k in range(3):
        scalars[k][0, 0] = totals[k, 0]

    def put(index, at, gradient):
        result = adam(masters[index][at], gradient * factor, firsts[index][at], seconds[index][at])
        for k in range(3):
            outs[k][index][at] = result[k]

    base = LAYERS * C_LAYER
    put(0, ..., sums[:, base + C_TOK[0] : base + C_TOK[1]])
    put(1, ..., sums[:, base + C_POS[0] : base + C_POS[0] + POS])
    put(6, ..., sums[:, base + C_HEAD[0] : base + C_HEAD[1]])
    turned[...] = jnp.transpose(sums[:, base + C_POS[0] : base + C_POS[1]])
    for i in range(NORMS):
        put(7, i, turned[POS + 2 * i : POS + 2 * i + 2, :])
    for l in range(LAYERS):
        for index, cols in ((2, C_IN), (3, C_OUT), (4, C_UP), (5, C_DOWN)):
            put(index, l, sums[:, l * C_LAYER + cols[0] : l * C_LAYER + cols[1]])


def turned(tok, pos, w_in, w_out, w_up, w_down, head, norms):
    return (tok.T, pos.T, w_in, w_out, w_up, jnp.swapaxes(w_down, 1, 2), head, norms)


def on_device(geo, pixels, loss_mask, *weights):
    masters, firsts, seconds = (turned(*weights[k : k + 8]) for k in (0, 8, 16))
    n_rows, depth, blocks, res, group = geo.rows, geo.depth, geo.blocks, geo.res, geo.group
    m = geo.m
    vmem = pl.BlockSpec(memory_space=pltpu.VMEM)
    chunk = 12
    batch = 24
    pack = 4
    n_groups = res // 8
    side = 8 * blocks
    sums, totals = pl.pallas_call(
        functools.partial(step_kernel, geo, chunk, batch, pack),
        out_shape=(
            jax.ShapeDtypeStruct((n_rows, C_ALL), F32),
            jax.ShapeDtypeStruct((8, 128), F32),
        ),
        in_specs=[vmem] * 10,
        out_specs=(vmem,) * 2,
        scratch_shapes=[
            pltpu.VMEM((depth, 2, 2, 2 * geo.own, geo.wide), BF),
            pltpu.VMEM((depth, 2, 2, n_rows, C_REST), BF),
            pltpu.VMEM((LAYERS, depth, 2, 2, n_rows, C_LAYER), BF),
            pltpu.VMEM((depth, 2, 2, n_rows, C_REST), F32),
            pltpu.VMEM((2, depth, 2, 2, n_rows, C_LAYER), F32),
            pltpu.VMEM((blocks, res, D), F32),
            pltpu.VMEM((2 * LAYERS, blocks, res, D), BF),
            pltpu.VMEM((blocks, res, 128), F32),
            pltpu.VMEM((blocks + 1, res, 2 * HEAD), F32),
            pltpu.VMEM((LAYERS, blocks, res, HEAD), BF),
            pltpu.VMEM((LAYERS, blocks + 1, group, res, 2 * HEAD), BF),
            pltpu.VMEM((LAYERS, n_groups, side, 3 * HEAD), BF),
            pltpu.VMEM((LAYERS, blocks, res, 2 * STRIDE), BF),
            pltpu.VMEM((LAYERS, n_groups, side, side), BF),
            pltpu.VMEM((LAYERS, blocks, res, D), BF),
            pltpu.VMEM((LAYERS, blocks, res, FF), BF),
            pltpu.VMEM((LAYERS, blocks, res, FF), BF),
            pltpu.VMEM((blocks, res, 3 * HEAD), F32),
            pltpu.VMEM((blocks, res, HEAD), F32),
            pltpu.VMEM((blocks, res, HEAD), BF),
            pltpu.VMEM((blocks, res, HEAD), BF),
            pltpu.VMEM((group - 1, blocks + 1, res, 2 * HEAD), BF),
            pltpu.VMEM((2, group - 1, blocks, res, 2 * HEAD), BF),
            pltpu.VMEM((STRIDE, 2 * HEAD), F32),
            pltpu.VMEM((res, 128), F32),
            pltpu.VMEM((res, 128), F32),
            pltpu.VMEM((res, 128), F32),
            pltpu.VMEM((8, 128), F32),
            pltpu.VMEM((geo.images, 2 * geo.own, 128), F32),
            pltpu.VMEM((2, res, 2 * STRIDE), F32),
            pltpu.VMEM((side, side), F32),
            pltpu.VMEM((16, 1, D), F32),
            pltpu.VMEM((2 * NORMS, 8, D), F32),
            pltpu.VMEM((128, D), F32),
            pltpu.VMEM((8, 128), F32),
            pltpu.VMEM((depth, 2, n_rows, C_ALL), BF),
            pltpu.VMEM((depth, 2, n_rows, C_ALL), BF),
            pltpu.VMEM((2 * depth - 1, n_rows, C_ALL), BF),
            pltpu.VMEM((m, n_rows, C_ALL), BF),
            pltpu.VMEM((m, depth, 2, n_rows, 128 * -(-(C_LAYER - C_OUT[0]) // 128 // m)), BF),
            pltpu.VMEM((m, 2 * depth, n_rows, C_POS[1]), BF),
            pltpu.VMEM((2, 8, 128), F32),
            pltpu.VMEM((m, 2 * depth, 8, 128), F32),
            pltpu.SemaphoreType.DMA((3 + 2 * LAYERS, depth + 1)),
            pltpu.SemaphoreType.DMA((3 + 2 * LAYERS, depth + 1)),
            pltpu.SemaphoreType.DMA((group - 1,)),
            pltpu.SemaphoreType.DMA((2 * LAYERS, group - 1)),
            pltpu.SemaphoreType.DMA((2 * LAYERS + 2, 2 * depth + m)),
            pltpu.SemaphoreType.DMA((2 * LAYERS + 2, 2 * depth + m)),
            pltpu.SemaphoreType.DMA((m,)),
            pltpu.SemaphoreType.DMA((m,)),
            pltpu.SemaphoreType.DMA((m,)),
            pltpu.SemaphoreType.DMA((m,)),
            pltpu.SemaphoreType.DMA((C_POS[1] // 128, 2 * depth)),
            pltpu.SemaphoreType.DMA((C_POS[1] // 128, m, 2 * depth)),
            pltpu.SemaphoreType.DMA((C_POS[1] // 128, m)),
            pltpu.SemaphoreType.DMA((C_POS[1] // 128,)),
            pltpu.SemaphoreType.DMA((m, 2 * depth)),
            pltpu.SemaphoreType.DMA((m, 2 * depth)),
        ],
        compiler_params=pltpu.CompilerParams(
            collective_id=0, has_side_effects=True, vmem_limit_bytes=VMEM_LIMIT
        ),
        name="step",
    )(jnp.swapaxes(pixels, 1, 2), jnp.swapaxes(loss_mask, 1, 2), *masters)

    shapes = [jax.ShapeDtypeStruct(item.shape, F32) for item in masters]
    outs = pl.pallas_call(
        functools.partial(update_kernel, n_rows),
        out_shape=shapes * 3 + [jax.ShapeDtypeStruct((1, 1), F32)] * 3,
        in_specs=[vmem] * 26,
        out_specs=[vmem] * 24 + [pl.BlockSpec(memory_space=pltpu.SMEM)] * 3,
        scratch_shapes=[pltpu.VMEM((128, n_rows), F32)],
        name="update",
    )(sums, totals, *masters, *firsts, *seconds)
    return (
        *(item.reshape(()) for item in outs[24:]),
        *turned(*outs[:8]),
        *turned(*outs[8:16]),
        *turned(*outs[16:24]),
    )


def solution(mesh):
    pixels = P("img", None, "seq")
    weights = (
        P(None, "seq"),
        P(None, "seq"),
        P(None, "seq", None),
        P(None, "seq", None),
        P(None, "seq", None),
        P(None, None, "seq"),
        P("seq", None),
        P(None, None, "seq"),
    )

    def body(pixels, loss_mask, *rest):
        geo = Geometry(mesh.shape["seq"], mesh.shape["img"], pixels.shape[0], pixels.shape[1])
        return on_device(geo, pixels, loss_mask, *rest)

    return jax.shard_map(
        body,
        mesh=mesh,
        in_specs=(pixels, pixels) + weights * 3,
        out_specs=(P(), P(), P()) + weights * 3,
        check_vma=False,
    )
```

```python
import functools
import math

import jax
import jax.numpy as jnp
from jax import lax
from jax.experimental import pallas as pl
from jax.experimental.pallas import tpu as pltpu
from jax.sharding import PartitionSpec as P

D = 256
HEAD = 128
FF = 512
V = 256
STRIDE = 128
LAYERS = 3
NORMS = 2 * LAYERS + 1
STEP = 10
SIDE = 32
POS = 2 * SIDE + 3
CLIP_NORM = 0.05
BETA_ONE = 0.9
BETA_TWO = 0.95
LEARN_RATE = 0.1
WEIGHT_DECAY = 0.1
ADAM_EPS = 1e-08
SMOOTHING = 0.1
NORM_EPS = 1e-05
SCALE = HEAD ** (-0.5)

C_IN, C_OUT, C_UP, C_DOWN = (0, 768), (768, 1024), (1024, 1536), (1536, 2048)
C_LAYER = 2048
C_TOK, C_POS, C_HEAD = (0, 256), (256, 384), (384, 640)
C_REST = 640
C_ALL = LAYERS * C_LAYER + C_REST

BF = jnp.bfloat16
F32 = jnp.float32
VMEM_LIMIT = 64 * 1024 * 1024


def dot(a, b):
    return lax.dot_general(a, b, (((1,), (0,)), ((), ())), preferred_element_type=F32)


def dot_nt(a, b):
    return lax.dot_general(a, b, (((1,), (1,)), ((), ())), preferred_element_type=F32)


def dot_tn(a, b):
    return lax.dot_general(a, b, (((0,), (0,)), ((), ())), preferred_element_type=F32)


class Geometry:
    def __init__(self, n, m, images, blocks):
        self.n, self.m, self.images, self.blocks = n, m, images, blocks
        self.depth = n // 4
        self.rows = D // n
        self.group = n // images
        self.res = STRIDE // self.group
        self.own = STRIDE // n
        self.wide = -(-images * blocks // 128) * 128

    def place(self):
        me = lax.axis_index("seq")
        return me // 4, me // 2 % 2, me % 2


def seq_id(z, y, core):
    return {"seq": z * 4 + y * 2 + core}


def greet(devices):
    barrier = pltpu.get_barrier_semaphore()
    for device in devices:
        pl.semaphore_signal(barrier, inc=1, device_id=device, device_id_type=pl.DeviceIdType.MESH)


def greeted(devices):
    pl.semaphore_wait(pltpu.get_barrier_semaphore(), len(devices))


def push(src, dst, send_sem, recv_sem, device):
    return pltpu.make_async_remote_copy(
        src_ref=src,
        dst_ref=dst,
        send_sem=send_sem,
        recv_sem=recv_sem,
        device_id=device,
        device_id_type=pl.DeviceIdType.MESH,
    )


def normalise(x):
    centre = x - jnp.mean(x, -1, keepdims=True)
    spread = jnp.mean(centre * centre, -1, keepdims=True)
    rstd = lax.rsqrt(spread + NORM_EPS)
    return centre * rstd, rstd


def fold(x):
    return jnp.sum(x.reshape(x.shape[0] // 8, 8, x.shape[1]), 0)


def normalise_back(dy, unit, rstd, gain):
    dxh = dy * (1.0 + gain)
    mean_one = jnp.mean(dxh, -1, keepdims=True)
    mean_two = jnp.mean(dxh * unit, -1, keepdims=True)
    return rstd * (dxh - mean_one - unit * mean_two), fold(dy * unit), fold(dy)


def gelu_both(u):
    c = math.sqrt(2.0 / math.pi)
    square = u * u
    half = 0.5 + 0.5 * jnp.tanh(u * (c + (0.044715 * c) * square))
    a = u * half
    return a, half + a * (1.0 - half) * (2.0 * c + (6.0 * 0.044715 * c) * square)


def softmax(scores):
    e = jnp.exp(scores - jnp.max(scores, -1, keepdims=True))
    return e * (1.0 / jnp.sum(e, -1, keepdims=True))


def step_kernel(
    geo, chunk, batch, pack,
    pixels, mask, tok, pos, w_in, w_out, w_up, w_down, head, norms,
    sums, totals,
    px, rest, layers, g_rest, g_layers,
    x_s, unit_s, rstd_s, own_s, q0_s, kv_s, qkv1_s, p0_s, p1_s, o_s, a_s, slope_s, stage, o1_s, do0_s, dq0_s,
    away_s, back_s, edge_s, ids_s, tgt_s, msk_s, prev_s, pack_s, bias0, bias1, norm_s, gnorm, wide, squares,
    s1, r1, r2, r4, r_cross, r_first, st_core, st_all,
    g_send, g_recv, kv_send, kv_recv, rs_send, rs_recv, c_send, c_recv, cb_send, cb_recv, f_send, f_recv, b_send, b_recv, st_send, st_recv,
):
    z, y, core = geo.place()
    me, x_img = lax.axis_index("seq"), lax.axis_index("img")
    depth, group, res, blocks, own, m = geo.depth, geo.group, geo.res, geo.blocks, geo.own, geo.m
    image, part = me // group, me % group
    siblings = [{"seq": image * group + lax.rem(part + k, group)} for k in range(1, group)]
    peers = [seq_id(lax.rem(z + k, depth), y, core) for k in range(1, depth)]
    beside, sibling = seq_id(z, 1 - y, core), seq_id(z, y, 1 - core)
    columns = 2 * depth
    column = z * 2 + y
    plane = [lax.rem(column + k, columns) for k in range(1, columns)]
    across = [{"img": lax.rem(x_img + k, m)} for k in range(1, m)]
    off_plane = [{**seq_id(q // 2, q % 2, core), "img": lax.rem(x_img + k, m)} for k in range(1, m) for q in plane]
    others = [seq_id(q // 2, q % 2, core) for q in plane] + across + [sibling] + off_plane
    if group > 2:
        others.append(seq_id(z, 1 - y, 1 - core))
    greet(others)
    rows = chunk * res
    chunks = blocks // chunk
    n_groups = res // 8
    every, pair = pl.ds(0, depth), pl.ds(0, 2)

    pack_s[...] = jnp.zeros_like(pack_s)
    pack_s[:, :own, :blocks] = pixels[...].astype(F32)
    pack_s[:, own:, :blocks] = mask[...].astype(F32)
    at = lax.broadcasted_iota(jnp.int32, (128, geo.wide), 0)
    to = lax.broadcasted_iota(jnp.int32, (128, geo.wide), 1)
    packed = jnp.zeros((2 * own, geo.wide), F32)
    for i in range(geo.images):
        spot = ((to == at + i * blocks) & (at < blocks)).astype(F32).astype(BF)
        packed = packed + dot(pack_s[i].astype(BF), spot)
    px[z, y, core] = packed.astype(BF)
    rest[z, y, core, :, C_TOK[0] : C_TOK[1]] = tok[...].astype(BF)
    wide[...] = jnp.zeros_like(wide)
    for i in range(NORMS):
        wide[POS + 2 * i : POS + 2 * i + 2, : geo.rows] = norms[i]
    flipped = jnp.transpose(wide[:, :128])[: geo.rows]
    wide[: geo.rows, :128] = flipped
    wide[: geo.rows, :POS] = pos[...]
    rest[z, y, core, :, C_POS[0] : C_POS[1]] = wide[: geo.rows, :128].astype(BF)

    parts = [px, rest.at[..., 0 : C_POS[1]]]
    for l in range(LAYERS):
        parts += [layers.at[l, ..., 0 : C_IN[1]], layers.at[l, ..., C_OUT[0] : C_LAYER]]
    parts += [rest.at[..., C_HEAD[0] : C_HEAD[1]]]

    def gather_z(a, k):
        mine = parts[a].at[z, y, core]
        return push(mine, mine, g_send.at[a, k], g_recv.at[a, k], peers[k])

    def gather_y(a):
        column = parts[a].at[every, y, core]
        return push(column, column, g_send.at[a, depth - 1], g_recv.at[a, depth - 1], beside)

    def gather_core(a):
        half = parts[a].at[every, pair, core]
        return push(half, half, g_send.at[a, depth], g_recv.at[a, depth], sibling)

    def to_y(a):
        for k in range(depth - 1):
            gather_z(a, k).wait_recv()
        gather_y(a).start()

    def to_core(a):
        gather_y(a).wait_recv()
        gather_core(a).start()

    def arrived(a):
        gather_core(a).wait_recv()

    def to_z(a):
        for k in range(depth - 1):
            gather_z(a, k).start()

    greeted(others)
    to_z(0)
    to_z(1)
    for l in range(LAYERS):
        layers[l, z, y, core, :, C_IN[0] : C_IN[1]] = w_in[l].astype(BF)
        if l == 0:
            to_z(2)
        layers[l, z, y, core, :, C_OUT[0] : C_OUT[1]] = w_out[l].astype(BF)
        layers[l, z, y, core, :, C_UP[0] : C_UP[1]] = w_up[l].astype(BF)
        layers[l, z, y, core, :, C_DOWN[0] : C_DOWN[1]] = w_down[l].astype(BF)
    rest[z, y, core, :, C_HEAD[0] : C_HEAD[1]] = head[...].astype(BF)

    def table(ref, cols):
        piece = ref[..., cols[0] : cols[1]]
        width = cols[1] - cols[0]
        if geo.rows % 16:
            return piece.astype(F32).reshape(D, width).astype(BF)
        return piece.reshape(D, width)

    def layer_table(l, cols):
        return table(layers.at[l], cols)

    def add_to(ref, cols, value):
        shape = (depth, 2, 2, geo.rows, cols[1] - cols[0])
        ref[..., cols[0] : cols[1]] += value.reshape(shape)

    for ref in (ids_s, tgt_s, msk_s, prev_s, wide, g_rest, g_layers, gnorm):
        ref[...] = jnp.zeros_like(ref)
    for l in range(LAYERS):
        kv_s[l, 0] = jnp.zeros((group, res, 2 * HEAD), BF)

    qi = part * res + lax.broadcasted_iota(jnp.int32, (res, 2 * STRIDE), 0)
    kj = lax.broadcasted_iota(jnp.int32, (res, 2 * STRIDE), 1)
    kj = kj // STRIDE * STRIDE + (kj % STRIDE + part * res) % STRIDE
    seen = (kj > qi) & (kj <= qi + STRIDE)
    bias0[0] = jnp.where(seen & (kj >= STRIDE), 0.0, -1e30)
    bias0[1] = jnp.where(seen, 0.0, -1e30)
    side = 8 * blocks
    ri = lax.broadcasted_iota(jnp.int32, (side, side), 0)
    ci = lax.broadcasted_iota(jnp.int32, (side, side), 1)
    bias1[...] = jnp.where(((ri & 7) == (ci & 7)) & (ri >= ci), 0.0, -1e30)

    to_y(0)
    to_y(1)
    to_z(3)
    to_y(2)
    to_z(4)
    to_core(0)
    to_core(1)
    arrived(0)

    span = depth // group
    at = lax.broadcasted_iota(jnp.int32, (geo.wide, 128), 0)
    to = lax.broadcasted_iota(jnp.int32, (geo.wide, 128), 1)
    spot = ((at == to + image * blocks) & (to < blocks)).astype(F32).astype(BF)
    for j in range(geo.images):
        piece = dot(px[part * span + j // 4, j // 2 % 2, j % 2], spot)
        tgt_s[j * own : (j + 1) * own, :] = piece[:own]
        msk_s[j * own : (j + 1) * own, :] = piece[own:]
    prev = dot(px[lax.rem(part * span + depth - 1, depth), 1, 1], spot)[:own]
    lane = lax.broadcasted_iota(jnp.int32, prev.shape, 1)
    moved = jnp.where(lane == 0, -1.0, pltpu.roll(prev, 1, 1))
    prev = jnp.where(part == 0, moved, prev)
    ids_s[0:1, :] = prev[own - 1 : own, :]
    ids_s[1:res, :] = tgt_s[0 : res - 1, :]

    arrived(1)
    wide[...] = jnp.transpose(table(rest, C_POS).astype(F32))
    for i in range(2 * NORMS):
        norm_s[i] = wide[POS + i : POS + i + 1, :]
    wide[...] = jnp.zeros_like(wide)
    to_y(3)
    to_z(5)

    def spread(ref, b0):
        values = ref[...].astype(BF)
        at = lax.broadcasted_iota(jnp.int32, (128, 128), 0)
        return jnp.concatenate(
            [dot(values, (at == b0 + j).astype(F32).astype(BF)) for j in range(chunk)], 0
        )

    def one_hot(ref, b0):
        value = spread(ref, b0)
        lane = lax.broadcasted_iota(jnp.int32, (rows, 128), 1).astype(F32)
        return jnp.concatenate([(value == lane).astype(F32), (value == lane + 128.0).astype(F32)], 1)

    def place_hot(b0):
        r = lax.broadcasted_iota(jnp.int32, (rows, 128), 0)
        lane = lax.broadcasted_iota(jnp.int32, (rows, 128), 1).astype(F32)
        p = ((b0 + r // res) * STRIDE + part * res + r % res).astype(F32)
        third = jnp.floor((p + 0.5) * (1.0 / 3.0))
        line = jnp.floor((third + 0.5) * (1.0 / SIDE))
        hits = (lane == line) | (lane == SIDE + third - SIDE * line)
        return (hits | (lane == 2 * SIDE + p - 3.0 * third)).astype(F32)

    def loop(count, body, between=()):
        def inner(i, carry):
            if between:
                pl.when(i == count - 1)(lambda: [step() for step in between] and None)
            body(i)
            return carry

        if count == 1:
            inner(0, None)
        else:
            lax.fori_loop(0, count, inner, 0)

    def embed(i):
        b0 = i * chunk
        hot = jnp.concatenate([one_hot(ids_s, b0), place_hot(b0)], 1).astype(BF)
        x = dot_nt(hot, table(rest, (C_TOK[0], C_POS[1])))
        x_s[pl.ds(b0, chunk)] = x.reshape(chunk, res, D)

    loop(chunks, embed)
    to_core(2)
    to_y(4)
    to_z(6)

    def keep(k, at, x):
        unit, rstd = normalise(x)
        unit = unit.astype(BF)
        unit_s[k, at] = unit.reshape(x.shape[0] // res, res, D)
        rstd_s[at, :, k : k + 1] = rstd.reshape(x.shape[0] // res, res, 1)
        return (unit.astype(F32) * (1.0 + norm_s[2 * k]) + norm_s[2 * k + 1]).astype(BF)

    def kept(k, at):
        unit = unit_s[k, at].reshape(rows, D).astype(F32)
        h = (unit * (1.0 + norm_s[2 * k]) + norm_s[2 * k + 1]).astype(BF)
        return h, unit, rstd_s[at, :, k : k + 1].reshape(rows, 1)

    def exchange(l, k):
        mine = kv_s.at[l, pl.ds(1, blocks), 0]
        there = kv_s.at[l, pl.ds(1, blocks), group - 1 - k]
        return push(mine, there, kv_send.at[k], kv_recv.at[l, k], siblings[k])

    def forward(l):
        def mix(i):
            b0 = i * chunk
            at = pl.ds(b0, chunk)
            h = keep(2 * l, at, x_s[at].reshape(rows, D))
            qkv = dot(h, layer_table(l, C_IN)).reshape(chunk, res, 6 * HEAD)
            q0_s[l, at] = qkv[..., :HEAD].astype(BF)
            kv_s[l, pl.ds(b0 + 1, chunk), 0, :, :HEAD] = qkv[..., 2 * HEAD : 3 * HEAD].astype(BF)
            kv_s[l, pl.ds(b0 + 1, chunk), 0, :, HEAD:] = qkv[..., 4 * HEAD : 5 * HEAD].astype(BF)
            stage[at, :, :HEAD] = qkv[..., HEAD : 2 * HEAD]
            stage[at, :, HEAD : 2 * HEAD] = qkv[..., 3 * HEAD : 4 * HEAD]
            stage[at, :, 2 * HEAD :] = qkv[..., 5 * HEAD :]

        def strided(i):
            qkvs = []
            for j in range(pack):
                at = pl.ds(pl.multiple_of(8 * (i * pack + j), 8), 8)
                qkv = stage[:, at, :].reshape(side, 3 * HEAD).astype(BF)
                qkv1_s[l, i * pack + j] = qkv
                qkvs.append(qkv)
            raw = [dot_nt(qkv[:, :HEAD], qkv[:, HEAD : 2 * HEAD]) * SCALE + bias1[...] for qkv in qkvs]
            probs = softmax(jnp.concatenate(raw, 0)).astype(BF)
            p1_s[l, pl.ds(i * pack, pack)] = probs.reshape(pack, side, side)
            for j in range(pack):
                at = pl.ds(pl.multiple_of(8 * (i * pack + j), 8), 8)
                value = dot(probs[j * side : (j + 1) * side], qkvs[j][:, 2 * HEAD :])
                o1_s[:, at, :] = value.reshape(blocks, 8, HEAD)

        def window(i):
            b0 = i * batch
            kv = kv_s[l, pl.ds(b0, batch + 1)].reshape((batch + 1) * STRIDE, 2 * HEAD)
            raw = [
                dot_nt(q0_s[l, b0 + j], kv[j * STRIDE : (j + 2) * STRIDE, :HEAD]) * SCALE
                + bias0[jnp.minimum(b0 + j, 1)]
                for j in range(batch)
            ]
            probs = softmax(jnp.concatenate(raw, 0)).astype(BF)
            p0_s[l, pl.ds(b0, batch)] = probs.reshape(batch, res, 2 * STRIDE)
            for j in range(batch):
                value = dot(probs[j * res : (j + 1) * res], kv[j * STRIDE : (j + 2) * STRIDE, HEAD:])
                o_s[l, b0 + j, :, :HEAD] = value.astype(BF)

        def feed(i):
            b0 = i * chunk
            at = pl.ds(b0, chunk)
            o_s[l, at, :, HEAD:] = o1_s[at].astype(BF)
            x1 = x_s[at].reshape(rows, D) + dot(o_s[l, at].reshape(rows, D), layer_table(l, C_OUT))
            h = keep(2 * l + 1, at, x1)
            a, slope = gelu_both(dot(h, layer_table(l, C_UP)).astype(BF))
            a_s[l, at] = a.reshape(chunk, res, FF)
            slope_s[l, at] = slope.reshape(chunk, res, FF)
            x2 = x1 + dot_nt(a, layer_table(l, C_DOWN))
            x_s[at] = x2.reshape(chunk, res, D)

        arrived(2 + 2 * l)
        loop(chunks, mix)
        copies = [exchange(l, k) for k in range(group - 1)]
        for copy in copies:
            copy.start()
        if l == 0:
            to_z(7)
        if l == 1:
            to_core(5)
            to_y(7)
        loop(n_groups // pack, strided)
        if l == 0:
            to_core(3)
            to_y(5)
            to_z(8)
        if l == 1:
            to_core(6)
        if l == 2:
            to_core(8)
        for copy in copies:
            copy.wait()
        loop(blocks // batch, window)
        if l == 0:
            to_core(4)
        if l == 1:
            to_y(8)
        arrived(3 + 2 * l)
        loop(chunks, feed, [lambda: to_y(6)] if l == 0 else [])
        if l == 1:
            to_core(7)

    for l in range(LAYERS):
        forward(l)
    arrived(8)

    dx_s = x_s

    def finish(i, loss):
        b0 = i * chunk
        at = pl.ds(b0, chunk)
        unit, rstd = normalise(x_s[at].reshape(rows, D))
        gain = norm_s[4 * LAYERS]
        h = (unit * (1.0 + gain) + norm_s[4 * LAYERS + 1]).astype(BF)
        table_head = table(rest, C_HEAD)
        logits = dot(h, table_head)
        hot = one_hot(tgt_s, b0)
        shift = logits - jnp.max(logits, -1, keepdims=True)
        e = jnp.exp(shift)
        total = jnp.sum(e, -1, keepdims=True)
        weight = spread(msk_s, b0)
        goal = (1.0 - SMOOTHING) * hot + SMOOTHING / V
        per = jnp.log(total) - jnp.sum(goal * shift, -1, keepdims=True)
        loss = loss + jnp.sum(weight[:, :1] * per, 0, keepdims=True)
        weight = jnp.concatenate([weight, weight], 1)
        d_logits = weight * (e * (1.0 / total) - goal)
        d_logits = d_logits.astype(BF)
        add_to(g_rest, C_HEAD, dot_tn(h, d_logits))
        dx, g_gain, g_bias = normalise_back(dot_nt(d_logits, table_head), unit, rstd, gain)
        gnorm[4 * LAYERS] += g_gain
        gnorm[4 * LAYERS + 1] += g_bias
        dx_s[at] = dx.reshape(chunk, res, D)
        return loss

    loss = lax.fori_loop(0, chunks, finish, jnp.zeros((1, 1), F32))
    count = jnp.sum(jnp.sum(msk_s[...], 0, keepdims=True), 1, keepdims=True)
    line = lax.broadcasted_iota(jnp.int32, (8, 128), 0)
    told = jnp.where(line == 0, loss, jnp.where(line == 1, count, 0.0))

    def give(l, k):
        return push(
            away_s.at[k, pl.ds(1, blocks)], back_s.at[l % 2, k], kv_send.at[k], kv_recv.at[LAYERS + l, k], siblings[k]
        )

    def backward(l, points):
        grads = g_layers.at[l % 2]

        def feed(i):
            b0 = i * chunk
            at = pl.ds(b0, chunk)
            dx2 = dx_s[at].reshape(rows, D)
            g2 = dx2.astype(BF)
            a = a_s[l, at].reshape(rows, FF)
            du = slope_s[l, at].reshape(rows, FF) * dot(g2, layer_table(l, C_DOWN)).astype(BF)
            h, unit, rstd = kept(2 * l + 1, at)
            dh = dot_nt(du, layer_table(l, C_UP))
            add_to(grads, C_DOWN, dot_tn(g2, a))
            dx, g_gain, g_bias = normalise_back(dh, unit, rstd, norm_s[4 * l + 2])
            add_to(grads, C_UP, dot_tn(h, du))
            gnorm[4 * l + 2] += g_gain
            gnorm[4 * l + 3] += g_bias
            dx = dx + dx2
            dx_s[at] = dx.reshape(chunk, res, D)
            g1 = dx.astype(BF)
            add_to(grads, C_OUT, dot_tn(o_s[l, at].reshape(rows, D), g1))
            do = dot_nt(g1, layer_table(l, C_OUT)).reshape(chunk, res, D)
            do0_s[at] = do[..., :HEAD].astype(BF)
            o1_s[at] = do[..., HEAD:]

        def window(i):
            b0 = i * batch
            at = pl.ds(b0, batch)
            kv = kv_s[l, pl.ds(b0, batch + 1)].reshape((batch + 1) * STRIDE, 2 * HEAD)
            probs = p0_s[l, at].reshape(batch * res, 2 * STRIDE)
            do = [do0_s[b0 + j] for j in range(batch)]
            keys = [kv[j * STRIDE : (j + 2) * STRIDE, :HEAD] for j in range(batch)]
            dp = jnp.concatenate(
                [dot_nt(do[j], kv[j * STRIDE : (j + 2) * STRIDE, HEAD:]) for j in range(batch)], 0
            )
            wide_p = probs.astype(F32)
            ds = (wide_p * (dp - jnp.sum(wide_p * dp, -1, keepdims=True)) * SCALE).astype(BF)
            carry = edge_s[...]
            for j in range(batch):
                cut = slice(j * res, (j + 1) * res)
                dq0_s[b0 + j] = dot(ds[cut], keys[j]).astype(BF)
                dkv = jnp.concatenate([dot_tn(ds[cut], q0_s[l, b0 + j]), dot_tn(probs[cut], do[j])], 1)
                done = (carry + dkv[:STRIDE]).reshape(group, res, 2 * HEAD)
                own_s[b0 + j] = done[0]
                for k in range(group - 1):
                    away_s[k, b0 + j] = done[k + 1].astype(BF)
                carry = dkv[STRIDE:]
            edge_s[...] = carry

        def strided(i):
            probs = p1_s[l, pl.ds(i * pack, pack)].reshape(pack * side, side)
            qkvs = [qkv1_s[l, i * pack + j] for j in range(pack)]
            ats = [pl.ds(pl.multiple_of(8 * (i * pack + j), 8), 8) for j in range(pack)]
            dos = [o1_s[:, at, :].reshape(side, HEAD).astype(BF) for at in ats]
            dp = jnp.concatenate([dot_nt(do, qkv[:, 2 * HEAD :]) for do, qkv in zip(dos, qkvs)], 0)
            wide_p = probs.astype(F32)
            ds = (wide_p * (dp - jnp.sum(wide_p * dp, -1, keepdims=True)) * SCALE).astype(BF)
            for j in range(pack):
                cut = slice(j * side, (j + 1) * side)
                dq = dot(ds[cut], qkvs[j][:, HEAD : 2 * HEAD])
                dk = dot_tn(ds[cut], qkvs[j][:, :HEAD])
                dv = dot_tn(probs[cut], dos[j])
                stage[:, ats[j], :] = jnp.concatenate([dq, dk, dv], 1).reshape(blocks, 8, 3 * HEAD)

        def mixed(i):
            at = pl.ds(i * chunk, chunk)
            dkv = own_s[pl.ds(i * chunk + 1, chunk)]
            for k in range(group - 1):
                dkv = dkv + back_s[l % 2, k, at].astype(F32)
            d1 = stage[at]
            return jnp.concatenate(
                [
                    dq0_s[at],
                    d1[..., :HEAD].astype(BF),
                    dkv[..., :HEAD].astype(BF),
                    d1[..., HEAD : 2 * HEAD].astype(BF),
                    dkv[..., HEAD:].astype(BF),
                    d1[..., 2 * HEAD :].astype(BF),
                ],
                -1,
            ).reshape(rows, 6 * HEAD)

        def mix_grad(i, dqkv=None, h=None):
            dqkv = mixed(i) if dqkv is None else dqkv
            if h is None:
                h, _, _ = kept(2 * l, pl.ds(i * chunk, chunk))
            add_to(grads, C_IN, dot_tn(h, dqkv))

        def mix_state(i, dqkv=None, both=None):
            at = pl.ds(i * chunk, chunk)
            dqkv = mixed(i) if dqkv is None else dqkv
            unit, rstd = kept(2 * l, at)[1:] if both is None else both
            dh = dot_nt(dqkv, layer_table(l, C_IN))
            dx, g_gain, g_bias = normalise_back(dh, unit, rstd, norm_s[4 * l])
            gnorm[4 * l] += g_gain
            gnorm[4 * l + 1] += g_bias
            dx_s[at] += dx.reshape(chunk, res, D)

        def mix(i):
            dqkv = mixed(i)
            h, unit, rstd = kept(2 * l, pl.ds(i * chunk, chunk))
            mix_grad(i, dqkv, h)
            mix_state(i, dqkv, (unit, rstd))

        def take(point):
            for step in points.get(point, ()):
                step()

        loop(chunks, feed, points.get("feed", ()))
        take("window")
        edge_s[...] = jnp.zeros_like(edge_s)
        loop(blocks // batch, window)
        last = edge_s[...].reshape(group, res, 2 * HEAD)
        own_s[blocks] = last[0]
        for k in range(group - 1):
            away_s[k, blocks] = last[k + 1].astype(BF)
        copies = [give(l, k) for k in range(group - 1)]
        for copy in copies:
            copy.start()
        take("strided")
        loop(n_groups // pack, strided)
        for copy in copies:
            copy.wait()
        take("mix")
        if l > 0:
            loop(chunks, mix)
            take("end")
        else:
            loop(chunks, mix_grad)
            take("end")
            loop(chunks, mix_state)

    def section(index, ref, cols, base, at_once=False):
        cut = slice(base + cols[0], base + cols[1])
        grad = ref.at[..., cols[0] : cols[1]]

        def way(k, src, dst, device):
            return push(src, dst, rs_send.at[index, k], rs_recv.at[index, k], device)

        one = way(0, s1.at[..., cut], r1.at[..., cut], sibling)
        def two():
            return way(1, s1.at[every, 0, :, cut], r2.at[every, :, cut], beside)

        def three(k):
            return way(1 + k, s1.at[lax.rem(z + k, depth), 1, :, cut], r2.at[depth + k - 1, :, cut], peers[k - 1])

        def direct(k):
            q = plane[k - 1]
            return way(k, s1.at[q // 2, q % 2, :, cut], r2.at[k - 1, :, cut], seq_id(q // 2, q % 2, core))

        def last(k):
            return way(columns + k - 1, r4.at[x_img, :, cut], r4.at[x_img, :, cut], across[k - 1])

        def go_core():
            s1[..., cut] = grad[every, pair, 1 - core].astype(BF)
            one.start()

        def go_y():
            one.wait()
            total = grad[every, 1 - y, core] + r1[every, 1 - y, :, cut].astype(F32)
            s1[every, 0, :, cut] = total.astype(BF)
            two().start()

        def go_z():
            two().wait()
            total = grad[every, y, core] + r1[every, y, :, cut].astype(F32) + r2[every, :, cut].astype(F32)
            s1[every, 1, :, cut] = total.astype(BF)
            for k in range(1, depth):
                three(k).start()

        def go_plane(start=True):
            one.wait()
            total = grad[every, pair, core] + r1[..., cut].astype(F32)
            s1[..., cut] = total.astype(BF)
            if start:
                for k in range(1, columns):
                    direct(k).start()

        def to_img(copy, number, mine, first):
            for k in range(1, number):
                copy(k).wait()
            total = mine.astype(F32)
            for k in range(1, number):
                total = total + r2[first + k - 1, :, cut].astype(F32)
            r4[x_img, :, cut] = total.astype(BF)
            for k in range(1, m):
                last(k).start()

        def go_img():
            to_img(three, depth, s1[z, 1, :, cut], depth)

        def from_plane():
            to_img(direct, columns, s1[z, y, :, cut], 0)

        def end():
            for k in range(1, m):
                last(k).wait()
            total = r4[0, :, cut].astype(F32)
            for k in range(1, m):
                total = total + r4[k, :, cut].astype(F32)
            sums[:, cut] = total
            square = jnp.sum(jnp.sum(total * total, 0, keepdims=True), 1, keepdims=True)
            squares[...] += jnp.broadcast_to(square, squares.shape)

        return (go_core, go_plane, from_plane, end) if at_once else (go_core, go_y, go_z, go_img, end)

    def crossed(index, ref, cols, base):
        tiles = (cols[1] - cols[0]) // 128
        cut = slice(base + cols[0], base + cols[1])
        grad = ref.at[..., cols[0] : cols[1]]
        ends = [128 * (tiles * p // m) for p in range(m + 1)]
        shares = [slice(cut.start + ends[p], cut.start + ends[p + 1]) for p in range(m)]
        widths = [ends[p + 1] - ends[p] for p in range(m)]
        one = push(s1.at[..., cut], r1.at[..., cut], rs_send.at[index, 0], rs_recv.at[index, 0], sibling)

        def over(p, group_at):
            there = r_cross.at[group_at, every, pair, :, 0 : widths[p]]
            return push(s1.at[..., shares[p]], there, c_send.at[p], c_recv.at[group_at], {"img": p})

        def direct(p, k):
            q = plane[k - 1]
            return push(
                s1.at[q // 2, q % 2, :, shares[p]],
                r2.at[k - 1, :, shares[p]],
                rs_send.at[index, k],
                rs_recv.at[index, k],
                seq_id(q // 2, q % 2, core),
            )

        def share(p, k):
            there = sums.at[:, shares[p]]
            return push(there, there, cb_send.at[k], cb_recv.at[p], across[k])

        def mine(p, step):
            if widths[p]:
                pl.when(x_img == p)(step)

        def not_mine(p, step):
            if widths[p]:
                pl.when(x_img != p)(step)

        def go_core():
            s1[..., cut] = grad[every, pair, 1 - core].astype(BF)
            one.start()

        def go_img():
            one.wait()
            total = grad[every, pair, core] + r1[..., cut].astype(F32)
            s1[..., cut] = total.astype(BF)
            for p in range(m):
                not_mine(p, lambda: over(p, x_img).start())

        def go_plane():
            for p in range(m):

                def step():
                    total = s1[..., shares[p]].astype(F32)
                    for group_at in range(m):
                        if group_at != p:
                            over(p, group_at).wait_recv()
                            total = total + r_cross[group_at, ..., 0 : widths[p]].astype(F32)
                    s1[..., shares[p]] = total.astype(BF)
                    for k in range(1, columns):
                        direct(p, k).start()

                mine(p, step)

        def end():
            for p in range(m):

                def step():
                    total = s1[z, y, :, shares[p]].astype(F32)
                    for k in range(1, columns):
                        direct(p, k).wait()
                        total = total + r2[k - 1, :, shares[p]].astype(F32)
                    sums[:, shares[p]] = total
                    for k in range(m - 1):
                        share(p, k).start()
                    square = jnp.sum(jnp.sum(total * total, 0, keepdims=True), 1, keepdims=True)
                    squares[...] += jnp.broadcast_to(square, squares.shape)

                mine(p, step)

        def drain():
            for p in range(m):

                def sent():
                    over(p, x_img).wait_send()
                    share(p, 0).wait_recv()

                def shared():
                    for k in range(m - 1):
                        share(p, k).wait_send()

                not_mine(p, sent)
                mine(p, shared)

        return go_core, go_img, go_plane, end, drain

    def of_layer(l):
        grads, base = g_layers.at[l % 2], l * C_LAYER
        kind = crossed if l == 0 else section
        return kind(2 * l, grads, (C_OUT[0], C_LAYER), base), section(2 * l + 1, grads, C_IN, base, l == 0)

    (feed_two, mix_two), (feed_one, mix_one), (feed_zero, mix_zero) = (of_layer(l) for l in (2, 1, 0))
    head_sum = section(6, g_rest, C_HEAD, LAYERS * C_LAYER)
    first_sum = section(7, g_rest, (C_TOK[0], C_POS[1]), LAYERS * C_LAYER, True)

    first_base = LAYERS * C_LAYER
    first_cuts = [slice(first_base + 128 * b, first_base + 128 * (b + 1)) for b in range(C_POS[1] // 128)]

    def first_send(b, k):
        own_place = k == columns - 1
        q = column if own_place else plane[k]
        device = {"img": b % m} if own_place else {**seq_id(q // 2, q % 2, core), "img": b % m}
        here = s1.at[q // 2, q % 2, :, first_cuts[b]]
        there = r_first.at[x_img, k, :, 128 * b : 128 * (b + 1)]
        return push(here, there, f_send.at[b, k], f_recv.at[b, x_img, k], device)

    def first_came(b, group_at, k):
        there = r_first.at[group_at, k, :, 128 * b : 128 * (b + 1)]
        return push(there, there, f_send.at[b, k], f_recv.at[b, group_at, k], sibling)

    def first_share(b, k):
        there = sums.at[:, first_cuts[b]]
        return push(there, there, b_send.at[b, k], b_recv.at[b], across[k])

    def first_start():
        first_sum[1](start=False)
        for b in range(len(first_cuts)):
            for k in range(columns - 1):
                first_send(b, k).start()

            @pl.when(x_img != b % m)
            def _():
                first_send(b, columns - 1).start()

    def first_end():
        for b in range(len(first_cuts)):

            @pl.when(x_img == b % m)
            def _():
                total = s1[z, y, :, first_cuts[b]].astype(F32)
                for group_at in range(m):
                    for k in range(columns - 1):
                        first_came(b, group_at, k).wait_recv()
                        total = total + r_first[group_at, k, :, 128 * b : 128 * (b + 1)].astype(F32)
                    if group_at != b % m:
                        first_came(b, group_at, columns - 1).wait_recv()
                        total = total + r_first[group_at, columns - 1, :, 128 * b : 128 * (b + 1)].astype(F32)
                sums[:, first_cuts[b]] = total
                for k in range(m - 1):
                    first_share(b, k).start()
                square = jnp.sum(jnp.sum(total * total, 0, keepdims=True), 1, keepdims=True)
                squares[...] += jnp.broadcast_to(square, squares.shape)

    def first_drain():
        for b in range(len(first_cuts)):
            for k in range(columns - 1):
                first_send(b, k).wait_send()

            @pl.when(x_img != b % m)
            def _():
                first_send(b, columns - 1).wait_send()
                first_share(b, 0).wait_recv()

            @pl.when(x_img == b % m)
            def _():
                for k in range(m - 1):
                    first_share(b, k).wait_send()

    squares[...] = jnp.zeros_like(squares)
    head_sum[0]()
    backward(
        2,
        {
            "window": [head_sum[1], feed_two[0]],
            "strided": [feed_two[1]],
            "mix": [head_sum[2]],
            "end": [mix_two[0]],
        },
    )
    backward(
        1,
        {
            "feed": [mix_two[1]],
            "window": [feed_two[2], feed_one[0]],
            "strided": [head_sum[3], feed_one[1]],
            "mix": [mix_two[2]],
            "end": [feed_two[3], head_sum[4], mix_one[0]],
        },
    )
    g_layers[0] = jnp.zeros(g_layers.shape[1:], F32)
    backward(
        0,
        {
            "feed": [mix_one[1]],
            "window": [feed_one[2], feed_zero[0], mix_two[3]],
            "strided": [feed_zero[1], feed_two[4]],
            "mix": [mix_one[2]],
            "end": [mix_zero[0], mix_two[4]],
        },
    )
    mix_zero[1]()

    def embed_back(i):
        b0 = i * chunk
        hot = jnp.concatenate([one_hot(ids_s, b0), place_hot(b0)], 1).astype(BF)
        dx = dx_s[pl.ds(b0, chunk)].reshape(rows, D)
        add_to(g_rest, (C_TOK[0], C_POS[1]), dot_tn(dx.astype(BF), hot))

    loop(chunks, embed_back)
    for i in range(2 * NORMS):
        wide[POS + i : POS + i + 1, :] = jnp.sum(gnorm[i], 0, keepdims=True)
    add_to(g_rest, C_POS, jnp.transpose(wide[...]))
    first_sum[0]()
    first_start()
    feed_zero[2]()
    feed_one[3]()
    mix_one[3]()
    mix_zero[2]()
    for part_sum in (feed_one, mix_one, mix_zero):
        part_sum[-1]()
    squares[...] = jnp.where(x_img == 0, squares[...], 0.0)
    first_end()
    feed_zero[3]()

    told = jnp.where(line == 2, squares[...], told)
    st_all[x_img, column] = told
    mine = st_all.at[x_img, column]
    plane_places = [(x_img, q) for q in plane]
    plane_places += [(lax.rem(x_img + k, m), lax.rem(column + j, columns)) for k in range(1, m) for j in range(columns)]
    copies = []
    for k, (group_at, q) in enumerate(plane_places, 1):
        spot = (k // columns, k % columns)
        device = {**seq_id(q // 2, q % 2, core), "img": group_at}
        copies.append(push(mine, mine, st_send.at[spot], st_recv.at[spot], device))
    for copy in copies:
        copy.start()
    for a in range(len(parts)):
        for k in range(depth - 1):
            gather_z(a, k).wait_send()
        gather_y(a).wait_send()
        gather_core(a).wait_send()
    for copy in copies:
        copy.wait()
    told = jnp.zeros((8, 128), F32)
    for group_at in range(m):
        for q in range(columns):
            told = told + st_all[group_at, q]
    st_core[core] = told
    copy = push(st_core.at[core], st_core.at[core], st_send.at[0, 0], st_recv.at[0, 0], sibling)
    copy.start()
    first_drain()
    feed_zero[4]()
    copy.wait()
    told = st_core[0] + st_core[1]
    count = told[1:2, :1]
    norm = jnp.sqrt(told[2:3, :1]) / count
    factor = jnp.minimum(1.0, CLIP_NORM / norm) / count
    totals[...] = jnp.where(line == 2, norm, jnp.where(line == 3, factor, told))


def adam(master, gradient, first, second):
    first = BETA_ONE * first + (1.0 - BETA_ONE) * gradient
    second = BETA_TWO * second + (1.0 - BETA_TWO) * gradient * gradient
    moved = first / (1.0 - BETA_ONE**STEP) / (jnp.sqrt(second / (1.0 - BETA_TWO**STEP)) + ADAM_EPS)
    return master - LEARN_RATE * (moved + WEIGHT_DECAY * master), first, second


def update_kernel(rows, *refs):
    sums, totals = refs[:2]
    masters, firsts, seconds = refs[2:10], refs[10:18], refs[18:26]
    outs = (refs[26:34], refs[34:42], refs[42:50])
    scalars, turned = refs[50:53], refs[53]
    factor = totals[3:4, :1]
    for k in range(3):
        scalars[k][0, 0] = totals[k, 0]

    def put(index, at, gradient):
        result = adam(masters[index][at], gradient * factor, firsts[index][at], seconds[index][at])
        for k in range(3):
            outs[k][index][at] = result[k]

    base = LAYERS * C_LAYER
    put(0, ..., sums[:, base + C_TOK[0] : base + C_TOK[1]])
    put(1, ..., sums[:, base + C_POS[0] : base + C_POS[0] + POS])
    put(6, ..., sums[:, base + C_HEAD[0] : base + C_HEAD[1]])
    turned[...] = jnp.transpose(sums[:, base + C_POS[0] : base + C_POS[1]])
    for i in range(NORMS):
        put(7, i, turned[POS + 2 * i : POS + 2 * i + 2, :])
    for l in range(LAYERS):
        for index, cols in ((2, C_IN), (3, C_OUT), (4, C_UP), (5, C_DOWN)):
            put(index, l, sums[:, l * C_LAYER + cols[0] : l * C_LAYER + cols[1]])


def turned(tok, pos, w_in, w_out, w_up, w_down, head, norms):
    return (tok.T, pos.T, w_in, w_out, w_up, jnp.swapaxes(w_down, 1, 2), head, norms)


def on_device(geo, pixels, loss_mask, *weights):
    masters, firsts, seconds = (turned(*weights[k : k + 8]) for k in (0, 8, 16))
    n_rows, depth, blocks, res, group = geo.rows, geo.depth, geo.blocks, geo.res, geo.group
    m = geo.m
    vmem = pl.BlockSpec(memory_space=pltpu.VMEM)
    chunk = 12
    batch = 24
    pack = 4
    n_groups = res // 8
    side = 8 * blocks
    sums, totals = pl.pallas_call(
        functools.partial(step_kernel, geo, chunk, batch, pack),
        out_shape=(
            jax.ShapeDtypeStruct((n_rows, C_ALL), F32),
            jax.ShapeDtypeStruct((8, 128), F32),
        ),
        in_specs=[vmem] * 10,
        out_specs=(vmem,) * 2,
        scratch_shapes=[
            pltpu.VMEM((depth, 2, 2, 2 * geo.own, geo.wide), BF),
            pltpu.VMEM((depth, 2, 2, n_rows, C_REST), BF),
            pltpu.VMEM((LAYERS, depth, 2, 2, n_rows, C_LAYER), BF),
            pltpu.VMEM((depth, 2, 2, n_rows, C_REST), F32),
            pltpu.VMEM((2, depth, 2, 2, n_rows, C_LAYER), F32),
            pltpu.VMEM((blocks, res, D), F32),
            pltpu.VMEM((2 * LAYERS, blocks, res, D), BF),
            pltpu.VMEM((blocks, res, 128), F32),
            pltpu.VMEM((blocks + 1, res, 2 * HEAD), F32),
            pltpu.VMEM((LAYERS, blocks, res, HEAD), BF),
            pltpu.VMEM((LAYERS, blocks + 1, group, res, 2 * HEAD), BF),
            pltpu.VMEM((LAYERS, n_groups, side, 3 * HEAD), BF),
            pltpu.VMEM((LAYERS, blocks, res, 2 * STRIDE), BF),
            pltpu.VMEM((LAYERS, n_groups, side, side), BF),
            pltpu.VMEM((LAYERS, blocks, res, D), BF),
            pltpu.VMEM((LAYERS, blocks, res, FF), BF),
            pltpu.VMEM((LAYERS, blocks, res, FF), BF),
            pltpu.VMEM((blocks, res, 3 * HEAD), F32),
            pltpu.VMEM((blocks, res, HEAD), F32),
            pltpu.VMEM((blocks, res, HEAD), BF),
            pltpu.VMEM((blocks, res, HEAD), BF),
            pltpu.VMEM((group - 1, blocks + 1, res, 2 * HEAD), BF),
            pltpu.VMEM((2, group - 1, blocks, res, 2 * HEAD), BF),
            pltpu.VMEM((STRIDE, 2 * HEAD), F32),
            pltpu.VMEM((res, 128), F32),
            pltpu.VMEM((res, 128), F32),
            pltpu.VMEM((res, 128), F32),
            pltpu.VMEM((8, 128), F32),
            pltpu.VMEM((geo.images, 2 * geo.own, 128), F32),
            pltpu.VMEM((2, res, 2 * STRIDE), F32),
            pltpu.VMEM((side, side), F32),
            pltpu.VMEM((16, 1, D), F32),
            pltpu.VMEM((2 * NORMS, 8, D), F32),
            pltpu.VMEM((128, D), F32),
            pltpu.VMEM((8, 128), F32),
            pltpu.VMEM((depth, 2, n_rows, C_ALL), BF),
            pltpu.VMEM((depth, 2, n_rows, C_ALL), BF),
            pltpu.VMEM((2 * depth - 1, n_rows, C_ALL), BF),
            pltpu.VMEM((m, n_rows, C_ALL), BF),
            pltpu.VMEM((m, depth, 2, n_rows, 128 * -(-(C_LAYER - C_OUT[0]) // 128 // m)), BF),
            pltpu.VMEM((m, 2 * depth, n_rows, C_POS[1]), BF),
            pltpu.VMEM((2, 8, 128), F32),
            pltpu.VMEM((m, 2 * depth, 8, 128), F32),
            pltpu.SemaphoreType.DMA((3 + 2 * LAYERS, depth + 1)),
            pltpu.SemaphoreType.DMA((3 + 2 * LAYERS, depth + 1)),
            pltpu.SemaphoreType.DMA((group - 1,)),
            pltpu.SemaphoreType.DMA((2 * LAYERS, group - 1)),
            pltpu.SemaphoreType.DMA((2 * LAYERS + 2, 2 * depth + m)),
            pltpu.SemaphoreType.DMA((2 * LAYERS + 2, 2 * depth + m)),
            pltpu.SemaphoreType.DMA((m,)),
            pltpu.SemaphoreType.DMA((m,)),
            pltpu.SemaphoreType.DMA((m,)),
            pltpu.SemaphoreType.DMA((m,)),
            pltpu.SemaphoreType.DMA((C_POS[1] // 128, 2 * depth)),
            pltpu.SemaphoreType.DMA((C_POS[1] // 128, m, 2 * depth)),
            pltpu.SemaphoreType.DMA((C_POS[1] // 128, m)),
            pltpu.SemaphoreType.DMA((C_POS[1] // 128,)),
            pltpu.SemaphoreType.DMA((m, 2 * depth)),
            pltpu.SemaphoreType.DMA((m, 2 * depth)),
        ],
        compiler_params=pltpu.CompilerParams(
            collective_id=0, has_side_effects=True, vmem_limit_bytes=VMEM_LIMIT
        ),
        name="step",
    )(jnp.swapaxes(pixels, 1, 2), jnp.swapaxes(loss_mask, 1, 2), *masters)

    shapes = [jax.ShapeDtypeStruct(item.shape, F32) for item in masters]
    outs = pl.pallas_call(
        functools.partial(update_kernel, n_rows),
        out_shape=shapes * 3 + [jax.ShapeDtypeStruct((1, 1), F32)] * 3,
        in_specs=[vmem] * 26,
        out_specs=[vmem] * 24 + [pl.BlockSpec(memory_space=pltpu.SMEM)] * 3,
        scratch_shapes=[pltpu.VMEM((128, n_rows), F32)],
        name="update",
    )(sums, totals, *masters, *firsts, *seconds)
    return (
        *(item.reshape(()) for item in outs[24:]),
        *turned(*outs[:8]),
        *turned(*outs[8:16]),
        *turned(*outs[16:24]),
    )


def solution(mesh):
    pixels = P("img", None, "seq")
    weights = (
        P(None, "seq"),
        P(None, "seq"),
        P(None, "seq", None),
        P(None, "seq", None),
        P(None, "seq", None),
        P(None, None, "seq"),
        P("seq", None),
        P(None, None, "seq"),
    )

    def body(pixels, loss_mask, *rest):
        geo = Geometry(mesh.shape["seq"], mesh.shape["img"], pixels.shape[0], pixels.shape[1])
        return on_device(geo, pixels, loss_mask, *rest)

    return jax.shard_map(
        body,
        mesh=mesh,
        in_specs=(pixels, pixels) + weights * 3,
        out_specs=(P(), P(), P()) + weights * 3,
        check_vma=False,
    )
```

```python
import functools
import math

import jax
import jax.numpy as jnp
from jax import lax
from jax.experimental import pallas as pl
from jax.experimental.pallas import tpu as pltpu
from jax.sharding import PartitionSpec as P

D = 256
HEAD = 128
FF = 512
V = 256
STRIDE = 128
LAYERS = 3
NORMS = 2 * LAYERS + 1
STEP = 10
SIDE = 32
POS = 2 * SIDE + 3
CLIP_NORM = 0.05
BETA_ONE = 0.9
BETA_TWO = 0.95
LEARN_RATE = 0.1
WEIGHT_DECAY = 0.1
ADAM_EPS = 1e-08
SMOOTHING = 0.1
NORM_EPS = 1e-05
SCALE = HEAD ** (-0.5)

C_IN, C_OUT, C_UP, C_DOWN = (0, 768), (768, 1024), (1024, 1536), (1536, 2048)
C_LAYER = 2048
C_TOK, C_POS, C_HEAD = (0, 256), (256, 384), (384, 640)
C_REST = 640
C_ALL = LAYERS * C_LAYER + C_REST

BF = jnp.bfloat16
F32 = jnp.float32
VMEM_LIMIT = 64 * 1024 * 1024


def dot(a, b):
    return lax.dot_general(a, b, (((1,), (0,)), ((), ())), preferred_element_type=F32)


def dot_nt(a, b):
    return lax.dot_general(a, b, (((1,), (1,)), ((), ())), preferred_element_type=F32)


def dot_tn(a, b):
    return lax.dot_general(a, b, (((0,), (0,)), ((), ())), preferred_element_type=F32)


class Geometry:
    def __init__(self, n, m, images, blocks):
        self.n, self.m, self.images, self.blocks = n, m, images, blocks
        self.depth = n // 4
        self.rows = D // n
        self.group = n // images
        self.res = STRIDE // self.group
        self.own = STRIDE // n
        self.wide = -(-images * blocks // 128) * 128

    def place(self):
        me = lax.axis_index("seq")
        return me // 4, me // 2 % 2, me % 2


def seq_id(z, y, core):
    return {"seq": z * 4 + y * 2 + core}


def greet(devices):
    barrier = pltpu.get_barrier_semaphore()
    for device in devices:
        pl.semaphore_signal(barrier, inc=1, device_id=device, device_id_type=pl.DeviceIdType.MESH)


def greeted(devices):
    pl.semaphore_wait(pltpu.get_barrier_semaphore(), len(devices))


def push(src, dst, send_sem, recv_sem, device):
    return pltpu.make_async_remote_copy(
        src_ref=src,
        dst_ref=dst,
        send_sem=send_sem,
        recv_sem=recv_sem,
        device_id=device,
        device_id_type=pl.DeviceIdType.MESH,
    )


def normalise(x):
    centre = x - jnp.mean(x, -1, keepdims=True)
    spread = jnp.mean(centre * centre, -1, keepdims=True)
    rstd = lax.rsqrt(spread + NORM_EPS)
    return centre * rstd, rstd


def fold(x):
    return jnp.sum(x.reshape(x.shape[0] // 8, 8, x.shape[1]), 0)


def normalise_back(dy, unit, rstd, gain):
    dxh = dy * (1.0 + gain)
    mean_one = jnp.mean(dxh, -1, keepdims=True)
    mean_two = jnp.mean(dxh * unit, -1, keepdims=True)
    return rstd * (dxh - mean_one - unit * mean_two), fold(dy * unit), fold(dy)


def gelu_both(u):
    c = math.sqrt(2.0 / math.pi)
    square = u * u
    half = 0.5 + 0.5 * jnp.tanh(u * (c + (0.044715 * c) * square))
    a = u * half
    return a, half + a * (1.0 - half) * (2.0 * c + (6.0 * 0.044715 * c) * square)


def softmax(raw):
    e = jnp.exp2((raw - jnp.max(raw, -1, keepdims=True)) * (SCALE * math.log2(math.e)))
    return e * (1.0 / jnp.sum(e, -1, keepdims=True))


def step_kernel(
    geo, chunk, batch, pack,
    pixels, mask, tok, pos, w_in, w_out, w_up, w_down, head, norms,
    sums, totals,
    px, rest, layers, g_rest, g_layers,
    x_s, unit_s, rstd_s, own_s, q0_s, kv_s, qkv1_s, p0_s, p1_s, o_s, a_s, slope_s, stage, o1_s, do0_s, dq0_s,
    away_s, back_s, edge_s, ids_s, tgt_s, msk_s, prev_s, pack_s, bias0, bias1, norm_s, gnorm, wide, squares,
    s1, r1, r2, r4, r_cross, r_first, st_core, st_all,
    g_send, g_recv, kv_send, kv_recv, rs_send, rs_recv, c_send, c_recv, cb_send, cb_recv, f_send, f_recv, b_send, b_recv, st_send, st_recv,
):
    z, y, core = geo.place()
    me, x_img = lax.axis_index("seq"), lax.axis_index("img")
    depth, group, res, blocks, own, m = geo.depth, geo.group, geo.res, geo.blocks, geo.own, geo.m
    image, part = me // group, me % group
    siblings = [{"seq": image * group + lax.rem(part + k, group)} for k in range(1, group)]
    peers = [seq_id(lax.rem(z + k, depth), y, core) for k in range(1, depth)]
    beside, sibling = seq_id(z, 1 - y, core), seq_id(z, y, 1 - core)
    columns = 2 * depth
    column = z * 2 + y
    plane = [lax.rem(column + k, columns) for k in range(1, columns)]
    across = [{"img": lax.rem(x_img + k, m)} for k in range(1, m)]
    off_plane = [{**seq_id(q // 2, q % 2, core), "img": lax.rem(x_img + k, m)} for k in range(1, m) for q in plane]
    others = [seq_id(q // 2, q % 2, core) for q in plane] + across + [sibling] + off_plane
    if group > 2:
        others.append(seq_id(z, 1 - y, 1 - core))
    greet(others)
    rows = chunk * res
    chunks = blocks // chunk
    n_groups = res // 8
    every, pair = pl.ds(0, depth), pl.ds(0, 2)

    pack_s[...] = jnp.zeros_like(pack_s)
    pack_s[:, :own, :blocks] = pixels[...].astype(F32)
    pack_s[:, own:, :blocks] = mask[...].astype(F32)
    at = lax.broadcasted_iota(jnp.int32, (128, geo.wide), 0)
    to = lax.broadcasted_iota(jnp.int32, (128, geo.wide), 1)
    packed = jnp.zeros((2 * own, geo.wide), F32)
    for i in range(geo.images):
        spot = ((to == at + i * blocks) & (at < blocks)).astype(F32).astype(BF)
        packed = packed + dot(pack_s[i].astype(BF), spot)
    px[z, y, core] = packed.astype(BF)
    rest[z, y, core, :, C_TOK[0] : C_TOK[1]] = tok[...].astype(BF)
    wide[...] = jnp.zeros_like(wide)
    for i in range(NORMS):
        wide[POS + 2 * i : POS + 2 * i + 2, : geo.rows] = norms[i]
    flipped = jnp.transpose(wide[:, :128])[: geo.rows]
    wide[: geo.rows, :128] = flipped
    wide[: geo.rows, :POS] = pos[...]
    rest[z, y, core, :, C_POS[0] : C_POS[1]] = wide[: geo.rows, :128].astype(BF)

    parts = [px, rest.at[..., 0 : C_POS[1]]]
    for l in range(LAYERS):
        parts += [layers.at[l, ..., 0 : C_IN[1]], layers.at[l, ..., C_OUT[0] : C_LAYER]]
    parts += [rest.at[..., C_HEAD[0] : C_HEAD[1]]]

    def gather_z(a, k):
        mine = parts[a].at[z, y, core]
        return push(mine, mine, g_send.at[a, k], g_recv.at[a, k], peers[k])

    def gather_y(a):
        column = parts[a].at[every, y, core]
        return push(column, column, g_send.at[a, depth - 1], g_recv.at[a, depth - 1], beside)

    def gather_core(a):
        half = parts[a].at[every, pair, core]
        return push(half, half, g_send.at[a, depth], g_recv.at[a, depth], sibling)

    def to_y(a):
        for k in range(depth - 1):
            gather_z(a, k).wait_recv()
        gather_y(a).start()

    def to_core(a):
        gather_y(a).wait_recv()
        gather_core(a).start()

    def arrived(a):
        gather_core(a).wait_recv()

    def to_z(a):
        for k in range(depth - 1):
            gather_z(a, k).start()

    greeted(others)
    to_z(0)
    to_z(1)
    for l in range(LAYERS):
        layers[l, z, y, core, :, C_IN[0] : C_IN[1]] = w_in[l].astype(BF)
        if l == 0:
            to_z(2)
        layers[l, z, y, core, :, C_OUT[0] : C_OUT[1]] = w_out[l].astype(BF)
        layers[l, z, y, core, :, C_UP[0] : C_UP[1]] = w_up[l].astype(BF)
        layers[l, z, y, core, :, C_DOWN[0] : C_DOWN[1]] = w_down[l].astype(BF)
    rest[z, y, core, :, C_HEAD[0] : C_HEAD[1]] = head[...].astype(BF)

    def table(ref, cols):
        piece = ref[..., cols[0] : cols[1]]
        width = cols[1] - cols[0]
        if geo.rows % 16:
            return piece.astype(F32).reshape(D, width).astype(BF)
        return piece.reshape(D, width)

    def layer_table(l, cols):
        return table(layers.at[l], cols)

    def add_to(ref, cols, value):
        shape = (depth, 2, 2, geo.rows, cols[1] - cols[0])
        ref[..., cols[0] : cols[1]] += value.reshape(shape)

    for ref in (ids_s, tgt_s, msk_s, prev_s, wide, g_rest, g_layers, gnorm):
        ref[...] = jnp.zeros_like(ref)
    for l in range(LAYERS):
        kv_s[l, 0] = jnp.zeros((group, res, 2 * HEAD), BF)

    qi = part * res + lax.broadcasted_iota(jnp.int32, (res, 2 * STRIDE), 0)
    kj = lax.broadcasted_iota(jnp.int32, (res, 2 * STRIDE), 1)
    kj = kj // STRIDE * STRIDE + (kj % STRIDE + part * res) % STRIDE
    seen = (kj > qi) & (kj <= qi + STRIDE)
    bias0[0] = jnp.where(seen & (kj >= STRIDE), 0.0, -1e30)
    bias0[1] = jnp.where(seen, 0.0, -1e30)
    side = 8 * blocks
    ri = lax.broadcasted_iota(jnp.int32, (side, side), 0)
    ci = lax.broadcasted_iota(jnp.int32, (side, side), 1)
    bias1[...] = jnp.where(((ri & 7) == (ci & 7)) & (ri >= ci), 0.0, -1e30)

    to_y(0)
    to_y(1)
    to_z(3)
    to_y(2)
    to_z(4)
    to_core(0)
    to_core(1)
    arrived(0)

    span = depth // group
    at = lax.broadcasted_iota(jnp.int32, (geo.wide, 128), 0)
    to = lax.broadcasted_iota(jnp.int32, (geo.wide, 128), 1)
    spot = ((at == to + image * blocks) & (to < blocks)).astype(F32).astype(BF)
    for j in range(geo.images):
        piece = dot(px[part * span + j // 4, j // 2 % 2, j % 2], spot)
        tgt_s[j * own : (j + 1) * own, :] = piece[:own]
        msk_s[j * own : (j + 1) * own, :] = piece[own:]
    prev = dot(px[lax.rem(part * span + depth - 1, depth), 1, 1], spot)[:own]
    lane = lax.broadcasted_iota(jnp.int32, prev.shape, 1)
    moved = jnp.where(lane == 0, -1.0, pltpu.roll(prev, 1, 1))
    prev = jnp.where(part == 0, moved, prev)
    ids_s[0:1, :] = prev[own - 1 : own, :]
    ids_s[1:res, :] = tgt_s[0 : res - 1, :]

    arrived(1)
    wide[...] = jnp.transpose(table(rest, C_POS).astype(F32))
    for i in range(2 * NORMS):
        norm_s[i] = wide[POS + i : POS + i + 1, :]
    wide[...] = jnp.zeros_like(wide)
    to_y(3)
    to_z(5)

    def spread(ref, b0):
        values = ref[...].astype(BF)
        at = lax.broadcasted_iota(jnp.int32, (128, 128), 0)
        return jnp.concatenate(
            [dot(values, (at == b0 + j).astype(F32).astype(BF)) for j in range(chunk)], 0
        )

    def one_hot(ref, b0, on=1.0, off=0.0):
        value = spread(ref, b0)
        lane = lax.broadcasted_iota(jnp.int32, (rows, 128), 1).astype(F32)
        return jnp.concatenate([jnp.where(value == lane, on, off), jnp.where(value == lane + 128.0, on, off)], 1)

    def place_hot(b0):
        r = lax.broadcasted_iota(jnp.int32, (rows, 128), 0)
        lane = lax.broadcasted_iota(jnp.int32, (rows, 128), 1).astype(F32)
        p = ((b0 + r // res) * STRIDE + part * res + r % res).astype(F32)
        third = jnp.floor((p + 0.5) * (1.0 / 3.0))
        line = jnp.floor((third + 0.5) * (1.0 / SIDE))
        hits = (lane == line) | (lane == SIDE + third - SIDE * line)
        return (hits | (lane == 2 * SIDE + p - 3.0 * third)).astype(F32)

    def loop(count, body, between=()):
        def inner(i, carry):
            if between:
                pl.when(i == count - 1)(lambda: [step() for step in between] and None)
            body(i)
            return carry

        if count == 1:
            inner(0, None)
        else:
            lax.fori_loop(0, count, inner, 0)

    def embed(i):
        b0 = i * chunk
        hot = jnp.concatenate([one_hot(ids_s, b0), place_hot(b0)], 1).astype(BF)
        x = dot_nt(hot, table(rest, (C_TOK[0], C_POS[1])))
        x_s[pl.ds(b0, chunk)] = x.reshape(chunk, res, D)

    loop(chunks, embed)
    to_core(2)
    to_y(4)
    to_z(6)

    def keep(k, at, x):
        unit, rstd = normalise(x)
        unit = unit.astype(BF)
        unit_s[k, at] = unit.reshape(x.shape[0] // res, res, D)
        rstd_s[at, :, k : k + 1] = rstd.reshape(x.shape[0] // res, res, 1)
        return (unit.astype(F32) * (1.0 + norm_s[2 * k]) + norm_s[2 * k + 1]).astype(BF)

    def kept(k, at):
        unit = unit_s[k, at].reshape(rows, D).astype(F32)
        h = (unit * (1.0 + norm_s[2 * k]) + norm_s[2 * k + 1]).astype(BF)
        return h, unit, rstd_s[at, :, k : k + 1].reshape(rows, 1)

    def exchange(l, k):
        mine = kv_s.at[l, pl.ds(1, blocks), 0]
        there = kv_s.at[l, pl.ds(1, blocks), group - 1 - k]
        return push(mine, there, kv_send.at[k], kv_recv.at[l, k], siblings[k])

    def forward(l):
        def mix(i):
            b0 = i * chunk
            at = pl.ds(b0, chunk)
            h = keep(2 * l, at, x_s[at].reshape(rows, D))
            qkv = dot(h, layer_table(l, C_IN)).reshape(chunk, res, 6 * HEAD)
            q0_s[l, at] = qkv[..., :HEAD].astype(BF)
            kv_s[l, pl.ds(b0 + 1, chunk), 0, :, :HEAD] = qkv[..., 2 * HEAD : 3 * HEAD].astype(BF)
            kv_s[l, pl.ds(b0 + 1, chunk), 0, :, HEAD:] = qkv[..., 4 * HEAD : 5 * HEAD].astype(BF)
            stage[at, :, :HEAD] = qkv[..., HEAD : 2 * HEAD]
            stage[at, :, HEAD : 2 * HEAD] = qkv[..., 3 * HEAD : 4 * HEAD]
            stage[at, :, 2 * HEAD :] = qkv[..., 5 * HEAD :]

        def strided(i):
            qkvs = []
            for j in range(pack):
                at = pl.ds(pl.multiple_of(8 * (i * pack + j), 8), 8)
                qkv = stage[:, at, :].reshape(side, 3 * HEAD).astype(BF)
                qkv1_s[l, i * pack + j] = qkv
                qkvs.append(qkv)
            raw = [dot_nt(qkv[:, :HEAD], qkv[:, HEAD : 2 * HEAD]) + bias1[...] for qkv in qkvs]
            probs = softmax(jnp.concatenate(raw, 0)).astype(BF)
            p1_s[l, pl.ds(i * pack, pack)] = probs.reshape(pack, side, side)
            for j in range(pack):
                at = pl.ds(pl.multiple_of(8 * (i * pack + j), 8), 8)
                value = dot(probs[j * side : (j + 1) * side], qkvs[j][:, 2 * HEAD :])
                o1_s[:, at, :] = value.reshape(blocks, 8, HEAD)

        def window(i):
            b0 = i * batch
            kv = kv_s[l, pl.ds(b0, batch + 1)].reshape((batch + 1) * STRIDE, 2 * HEAD)
            raw = [
                dot_nt(q0_s[l, b0 + j], kv[j * STRIDE : (j + 2) * STRIDE, :HEAD])
                + bias0[jnp.minimum(b0 + j, 1)]
                for j in range(batch)
            ]
            probs = softmax(jnp.concatenate(raw, 0)).astype(BF)
            p0_s[l, pl.ds(b0, batch)] = probs.reshape(batch, res, 2 * STRIDE)
            for j in range(batch):
                value = dot(probs[j * res : (j + 1) * res], kv[j * STRIDE : (j + 2) * STRIDE, HEAD:])
                o_s[l, b0 + j, :, :HEAD] = value.astype(BF)

        def feed(i):
            b0 = i * chunk
            at = pl.ds(b0, chunk)
            o_s[l, at, :, HEAD:] = o1_s[at].astype(BF)
            x1 = x_s[at].reshape(rows, D) + dot(o_s[l, at].reshape(rows, D), layer_table(l, C_OUT))
            h = keep(2 * l + 1, at, x1)
            a, slope = gelu_both(dot(h, layer_table(l, C_UP)).astype(BF))
            a_s[l, at] = a.reshape(chunk, res, FF)
            slope_s[l, at] = slope.reshape(chunk, res, FF)
            x2 = x1 + dot_nt(a, layer_table(l, C_DOWN))
            x_s[at] = x2.reshape(chunk, res, D)

        arrived(2 + 2 * l)
        loop(chunks, mix)
        copies = [exchange(l, k) for k in range(group - 1)]
        for copy in copies:
            copy.start()
        if l == 0:
            to_z(7)
        if l == 1:
            to_core(5)
            to_y(7)
        loop(n_groups // pack, strided)
        if l == 0:
            to_core(3)
            to_y(5)
            to_z(8)
        if l == 1:
            to_core(6)
        if l == 2:
            to_core(8)
        for copy in copies:
            copy.wait()
        loop(blocks // batch, window)
        if l == 0:
            to_core(4)
        if l == 1:
            to_y(8)
        arrived(3 + 2 * l)
        loop(chunks, feed, [lambda: to_y(6)] if l == 0 else [])
        if l == 1:
            to_core(7)

    for l in range(LAYERS):
        forward(l)
    arrived(8)

    dx_s = x_s

    def finish(i, loss):
        b0 = i * chunk
        at = pl.ds(b0, chunk)
        unit, rstd = normalise(x_s[at].reshape(rows, D))
        gain = norm_s[4 * LAYERS]
        h = (unit * (1.0 + gain) + norm_s[4 * LAYERS + 1]).astype(BF)
        table_head = table(rest, C_HEAD)
        logits = dot(h, table_head)
        shift = logits - jnp.max(logits, -1, keepdims=True)
        e = jnp.exp(shift)
        total = jnp.sum(e, -1, keepdims=True)
        weight = spread(msk_s, b0)
        goal = one_hot(tgt_s, b0, 1.0 - SMOOTHING + SMOOTHING / V, SMOOTHING / V)
        per = jnp.log(total) - jnp.sum(goal * shift, -1, keepdims=True)
        loss = loss + jnp.sum(weight[:, :1] * per, 0, keepdims=True)
        weight = jnp.concatenate([weight, weight], 1)
        d_logits = weight * (e * (1.0 / total) - goal)
        d_logits = d_logits.astype(BF)
        add_to(g_rest, C_HEAD, dot_tn(h, d_logits))
        dx, g_gain, g_bias = normalise_back(dot_nt(d_logits, table_head), unit, rstd, gain)
        gnorm[4 * LAYERS] += g_gain
        gnorm[4 * LAYERS + 1] += g_bias
        dx_s[at] = dx.reshape(chunk, res, D)
        return loss

    loss = lax.fori_loop(0, chunks, finish, jnp.zeros((1, 1), F32))
    count = jnp.sum(jnp.sum(msk_s[...], 0, keepdims=True), 1, keepdims=True)
    line = lax.broadcasted_iota(jnp.int32, (8, 128), 0)
    told = jnp.where(line == 0, loss, jnp.where(line == 1, count, 0.0))

    def give(l, k):
        return push(
            away_s.at[k, pl.ds(1, blocks)], back_s.at[l % 2, k], kv_send.at[k], kv_recv.at[LAYERS + l, k], siblings[k]
        )

    def backward(l, points):
        grads = g_layers.at[l % 2]

        def feed(i):
            b0 = i * chunk
            at = pl.ds(b0, chunk)
            dx2 = dx_s[at].reshape(rows, D)
            g2 = dx2.astype(BF)
            a = a_s[l, at].reshape(rows, FF)
            du = slope_s[l, at].reshape(rows, FF) * dot(g2, layer_table(l, C_DOWN)).astype(BF)
            h, unit, rstd = kept(2 * l + 1, at)
            dh = dot_nt(du, layer_table(l, C_UP))
            add_to(grads, C_DOWN, dot_tn(g2, a))
            dx, g_gain, g_bias = normalise_back(dh, unit, rstd, norm_s[4 * l + 2])
            add_to(grads, C_UP, dot_tn(h, du))
            gnorm[4 * l + 2] += g_gain
            gnorm[4 * l + 3] += g_bias
            dx = dx + dx2
            dx_s[at] = dx.reshape(chunk, res, D)
            g1 = dx.astype(BF)
            add_to(grads, C_OUT, dot_tn(o_s[l, at].reshape(rows, D), g1))
            do = dot_nt(g1, layer_table(l, C_OUT)).reshape(chunk, res, D)
            do0_s[at] = do[..., :HEAD].astype(BF)
            o1_s[at] = do[..., HEAD:]

        def window(i):
            b0 = i * batch
            at = pl.ds(b0, batch)
            kv = kv_s[l, pl.ds(b0, batch + 1)].reshape((batch + 1) * STRIDE, 2 * HEAD)
            probs = p0_s[l, at].reshape(batch * res, 2 * STRIDE)
            do = [do0_s[b0 + j] for j in range(batch)]
            keys = [kv[j * STRIDE : (j + 2) * STRIDE, :HEAD] for j in range(batch)]
            dp = jnp.concatenate(
                [dot_nt(do[j], kv[j * STRIDE : (j + 2) * STRIDE, HEAD:]) for j in range(batch)], 0
            )
            wide_p = probs.astype(F32)
            ds = (wide_p * (dp - jnp.sum(wide_p * dp, -1, keepdims=True)) * SCALE).astype(BF)
            carry = edge_s[...]
            for j in range(batch):
                cut = slice(j * res, (j + 1) * res)
                dq0_s[b0 + j] = dot(ds[cut], keys[j]).astype(BF)
                dkv = jnp.concatenate([dot_tn(ds[cut], q0_s[l, b0 + j]), dot_tn(probs[cut], do[j])], 1)
                done = (carry + dkv[:STRIDE]).reshape(group, res, 2 * HEAD)
                own_s[b0 + j] = done[0]
                for k in range(group - 1):
                    away_s[k, b0 + j] = done[k + 1].astype(BF)
                carry = dkv[STRIDE:]
            edge_s[...] = carry

        def strided(i):
            probs = p1_s[l, pl.ds(i * pack, pack)].reshape(pack * side, side)
            qkvs = [qkv1_s[l, i * pack + j] for j in range(pack)]
            ats = [pl.ds(pl.multiple_of(8 * (i * pack + j), 8), 8) for j in range(pack)]
            dos = [o1_s[:, at, :].reshape(side, HEAD).astype(BF) for at in ats]
            dp = jnp.concatenate([dot_nt(do, qkv[:, 2 * HEAD :]) for do, qkv in zip(dos, qkvs)], 0)
            wide_p = probs.astype(F32)
            ds = (wide_p * (dp - jnp.sum(wide_p * dp, -1, keepdims=True)) * SCALE).astype(BF)
            for j in range(pack):
                cut = slice(j * side, (j + 1) * side)
                dq = dot(ds[cut], qkvs[j][:, HEAD : 2 * HEAD])
                dk = dot_tn(ds[cut], qkvs[j][:, :HEAD])
                dv = dot_tn(probs[cut], dos[j])
                stage[:, ats[j], :] = jnp.concatenate([dq, dk, dv], 1).reshape(blocks, 8, 3 * HEAD)

        def mixed(i):
            at = pl.ds(i * chunk, chunk)
            dkv = own_s[pl.ds(i * chunk + 1, chunk)]
            for k in range(group - 1):
                dkv = dkv + back_s[l % 2, k, at].astype(F32)
            d1 = stage[at]
            return jnp.concatenate(
                [
                    dq0_s[at],
                    d1[..., :HEAD].astype(BF),
                    dkv[..., :HEAD].astype(BF),
                    d1[..., HEAD : 2 * HEAD].astype(BF),
                    dkv[..., HEAD:].astype(BF),
                    d1[..., 2 * HEAD :].astype(BF),
                ],
                -1,
            ).reshape(rows, 6 * HEAD)

        def mix_grad(i, dqkv=None, h=None):
            dqkv = mixed(i) if dqkv is None else dqkv
            if h is None:
                h, _, _ = kept(2 * l, pl.ds(i * chunk, chunk))
            add_to(grads, C_IN, dot_tn(h, dqkv))

        def mix_state(i, dqkv=None, both=None):
            at = pl.ds(i * chunk, chunk)
            dqkv = mixed(i) if dqkv is None else dqkv
            unit, rstd = kept(2 * l, at)[1:] if both is None else both
            dh = dot_nt(dqkv, layer_table(l, C_IN))
            dx, g_gain, g_bias = normalise_back(dh, unit, rstd, norm_s[4 * l])
            gnorm[4 * l] += g_gain
            gnorm[4 * l + 1] += g_bias
            dx_s[at] += dx.reshape(chunk, res, D)

        def mix(i):
            dqkv = mixed(i)
            h, unit, rstd = kept(2 * l, pl.ds(i * chunk, chunk))
            mix_grad(i, dqkv, h)
            mix_state(i, dqkv, (unit, rstd))

        def take(point):
            for step in points.get(point, ()):
                step()

        loop(chunks, feed, points.get("feed", ()))
        take("window")
        edge_s[...] = jnp.zeros_like(edge_s)
        loop(blocks // batch, window)
        last = edge_s[...].reshape(group, res, 2 * HEAD)
        own_s[blocks] = last[0]
        for k in range(group - 1):
            away_s[k, blocks] = last[k + 1].astype(BF)
        copies = [give(l, k) for k in range(group - 1)]
        for copy in copies:
            copy.start()
        take("strided")
        loop(n_groups // pack, strided)
        for copy in copies:
            copy.wait()
        take("mix")
        if l > 0:
            loop(chunks, mix)
            take("end")
        else:
            loop(chunks, mix_grad)
            take("end")
            loop(chunks, mix_state)

    def section(index, ref, cols, base, at_once=False):
        cut = slice(base + cols[0], base + cols[1])
        grad = ref.at[..., cols[0] : cols[1]]

        def way(k, src, dst, device):
            return push(src, dst, rs_send.at[index, k], rs_recv.at[index, k], device)

        one = way(0, s1.at[..., cut], r1.at[..., cut], sibling)
        def two():
            return way(1, s1.at[every, 0, :, cut], r2.at[every, :, cut], beside)

        def three(k):
            return way(1 + k, s1.at[lax.rem(z + k, depth), 1, :, cut], r2.at[depth + k - 1, :, cut], peers[k - 1])

        def direct(k):
            q = plane[k - 1]
            return way(k, s1.at[q // 2, q % 2, :, cut], r2.at[k - 1, :, cut], seq_id(q // 2, q % 2, core))

        def last(k):
            return way(columns + k - 1, r4.at[x_img, :, cut], r4.at[x_img, :, cut], across[k - 1])

        def go_core():
            s1[..., cut] = grad[every, pair, 1 - core].astype(BF)
            one.start()

        def go_y():
            one.wait()
            total = grad[every, 1 - y, core] + r1[every, 1 - y, :, cut].astype(F32)
            s1[every, 0, :, cut] = total.astype(BF)
            two().start()

        def go_z():
            two().wait()
            total = grad[every, y, core] + r1[every, y, :, cut].astype(F32) + r2[every, :, cut].astype(F32)
            s1[every, 1, :, cut] = total.astype(BF)
            for k in range(1, depth):
                three(k).start()

        def go_plane(start=True):
            one.wait()
            total = grad[every, pair, core] + r1[..., cut].astype(F32)
            s1[..., cut] = total.astype(BF)
            if start:
                for k in range(1, columns):
                    direct(k).start()

        def to_img(copy, number, mine, first):
            for k in range(1, number):
                copy(k).wait()
            total = mine.astype(F32)
            for k in range(1, number):
                total = total + r2[first + k - 1, :, cut].astype(F32)
            r4[x_img, :, cut] = total.astype(BF)
            for k in range(1, m):
                last(k).start()

        def go_img():
            to_img(three, depth, s1[z, 1, :, cut], depth)

        def from_plane():
            to_img(direct, columns, s1[z, y, :, cut], 0)

        def end():
            for k in range(1, m):
                last(k).wait()
            total = r4[0, :, cut].astype(F32)
            for k in range(1, m):
                total = total + r4[k, :, cut].astype(F32)
            sums[:, cut] = total
            square = jnp.sum(jnp.sum(total * total, 0, keepdims=True), 1, keepdims=True)
            squares[...] += jnp.broadcast_to(square, squares.shape)

        return (go_core, go_plane, from_plane, end) if at_once else (go_core, go_y, go_z, go_img, end)

    def crossed(index, ref, cols, base):
        tiles = (cols[1] - cols[0]) // 128
        cut = slice(base + cols[0], base + cols[1])
        grad = ref.at[..., cols[0] : cols[1]]
        ends = [128 * (tiles * p // m) for p in range(m + 1)]
        shares = [slice(cut.start + ends[p], cut.start + ends[p + 1]) for p in range(m)]
        widths = [ends[p + 1] - ends[p] for p in range(m)]
        one = push(s1.at[..., cut], r1.at[..., cut], rs_send.at[index, 0], rs_recv.at[index, 0], sibling)

        def over(p, group_at):
            there = r_cross.at[group_at, every, pair, :, 0 : widths[p]]
            return push(s1.at[..., shares[p]], there, c_send.at[p], c_recv.at[group_at], {"img": p})

        def direct(p, k):
            q = plane[k - 1]
            return push(
                s1.at[q // 2, q % 2, :, shares[p]],
                r2.at[k - 1, :, shares[p]],
                rs_send.at[index, k],
                rs_recv.at[index, k],
                seq_id(q // 2, q % 2, core),
            )

        def share(p, k):
            there = sums.at[:, shares[p]]
            return push(there, there, cb_send.at[k], cb_recv.at[p], across[k])

        def mine(p, step):
            if widths[p]:
                pl.when(x_img == p)(step)

        def not_mine(p, step):
            if widths[p]:
                pl.when(x_img != p)(step)

        def go_core():
            s1[..., cut] = grad[every, pair, 1 - core].astype(BF)
            one.start()

        def go_img():
            one.wait()
            total = grad[every, pair, core] + r1[..., cut].astype(F32)
            s1[..., cut] = total.astype(BF)
            for p in range(m):
                not_mine(p, lambda: over(p, x_img).start())

        def go_plane():
            for p in range(m):

                def step():
                    total = s1[..., shares[p]].astype(F32)
                    for group_at in range(m):
                        if group_at != p:
                            over(p, group_at).wait_recv()
                            total = total + r_cross[group_at, ..., 0 : widths[p]].astype(F32)
                    s1[..., shares[p]] = total.astype(BF)
                    for k in range(1, columns):
                        direct(p, k).start()

                mine(p, step)

        def end():
            for p in range(m):

                def step():
                    total = s1[z, y, :, shares[p]].astype(F32)
                    for k in range(1, columns):
                        direct(p, k).wait()
                        total = total + r2[k - 1, :, shares[p]].astype(F32)
                    sums[:, shares[p]] = total
                    for k in range(m - 1):
                        share(p, k).start()
                    square = jnp.sum(jnp.sum(total * total, 0, keepdims=True), 1, keepdims=True)
                    squares[...] += jnp.broadcast_to(square, squares.shape)

                mine(p, step)

        def drain():
            for p in range(m):

                def sent():
                    over(p, x_img).wait_send()
                    share(p, 0).wait_recv()

                def shared():
                    for k in range(m - 1):
                        share(p, k).wait_send()

                not_mine(p, sent)
                mine(p, shared)

        return go_core, go_img, go_plane, end, drain

    def of_layer(l):
        grads, base = g_layers.at[l % 2], l * C_LAYER
        kind = crossed if l == 0 else section
        return kind(2 * l, grads, (C_OUT[0], C_LAYER), base), section(2 * l + 1, grads, C_IN, base, l == 0)

    (feed_two, mix_two), (feed_one, mix_one), (feed_zero, mix_zero) = (of_layer(l) for l in (2, 1, 0))
    head_sum = section(6, g_rest, C_HEAD, LAYERS * C_LAYER)
    first_sum = section(7, g_rest, (C_TOK[0], C_POS[1]), LAYERS * C_LAYER, True)

    first_base = LAYERS * C_LAYER
    first_cuts = [slice(first_base + 128 * b, first_base + 128 * (b + 1)) for b in range(C_POS[1] // 128)]

    def first_send(b, k):
        own_place = k == columns - 1
        q = column if own_place else plane[k]
        device = {"img": b % m} if own_place else {**seq_id(q // 2, q % 2, core), "img": b % m}
        here = s1.at[q // 2, q % 2, :, first_cuts[b]]
        there = r_first.at[x_img, k, :, 128 * b : 128 * (b + 1)]
        return push(here, there, f_send.at[b, k], f_recv.at[b, x_img, k], device)

    def first_came(b, group_at, k):
        there = r_first.at[group_at, k, :, 128 * b : 128 * (b + 1)]
        return push(there, there, f_send.at[b, k], f_recv.at[b, group_at, k], sibling)

    def first_share(b, k):
        there = sums.at[:, first_cuts[b]]
        return push(there, there, b_send.at[b, k], b_recv.at[b], across[k])

    def first_start():
        first_sum[1](start=False)
        for b in range(len(first_cuts)):
            for k in range(columns - 1):
                first_send(b, k).start()

            @pl.when(x_img != b % m)
            def _():
                first_send(b, columns - 1).start()

    def first_end():
        for b in range(len(first_cuts)):

            @pl.when(x_img == b % m)
            def _():
                total = s1[z, y, :, first_cuts[b]].astype(F32)
                for group_at in range(m):
                    for k in range(columns - 1):
                        first_came(b, group_at, k).wait_recv()
                        total = total + r_first[group_at, k, :, 128 * b : 128 * (b + 1)].astype(F32)
                    if group_at != b % m:
                        first_came(b, group_at, columns - 1).wait_recv()
                        total = total + r_first[group_at, columns - 1, :, 128 * b : 128 * (b + 1)].astype(F32)
                sums[:, first_cuts[b]] = total
                for k in range(m - 1):
                    first_share(b, k).start()
                square = jnp.sum(jnp.sum(total * total, 0, keepdims=True), 1, keepdims=True)
                squares[...] += jnp.broadcast_to(square, squares.shape)

    def first_drain():
        for b in range(len(first_cuts)):
            for k in range(columns - 1):
                first_send(b, k).wait_send()

            @pl.when(x_img != b % m)
            def _():
                first_send(b, columns - 1).wait_send()
                first_share(b, 0).wait_recv()

            @pl.when(x_img == b % m)
            def _():
                for k in range(m - 1):
                    first_share(b, k).wait_send()

    squares[...] = jnp.zeros_like(squares)
    head_sum[0]()
    backward(
        2,
        {
            "window": [head_sum[1], feed_two[0]],
            "strided": [feed_two[1]],
            "mix": [head_sum[2]],
            "end": [mix_two[0]],
        },
    )
    backward(
        1,
        {
            "feed": [mix_two[1]],
            "window": [feed_two[2], feed_one[0]],
            "strided": [head_sum[3], feed_one[1]],
            "mix": [mix_two[2]],
            "end": [feed_two[3], head_sum[4], mix_one[0]],
        },
    )
    g_layers[0] = jnp.zeros(g_layers.shape[1:], F32)
    backward(
        0,
        {
            "feed": [mix_one[1]],
            "window": [feed_one[2], feed_zero[0], mix_two[3]],
            "strided": [feed_zero[1], feed_two[4]],
            "mix": [mix_one[2]],
            "end": [mix_zero[0], mix_two[4]],
        },
    )
    mix_zero[1]()

    def embed_back(i):
        b0 = i * chunk
        hot = jnp.concatenate([one_hot(ids_s, b0), place_hot(b0)], 1).astype(BF)
        dx = dx_s[pl.ds(b0, chunk)].reshape(rows, D)
        add_to(g_rest, (C_TOK[0], C_POS[1]), dot_tn(dx.astype(BF), hot))

    loop(chunks, embed_back)
    for i in range(2 * NORMS):
        wide[POS + i : POS + i + 1, :] = jnp.sum(gnorm[i], 0, keepdims=True)
    add_to(g_rest, C_POS, jnp.transpose(wide[...]))
    first_sum[0]()
    first_start()
    feed_zero[2]()
    feed_one[3]()
    mix_one[3]()
    mix_zero[2]()
    for part_sum in (feed_one, mix_one, mix_zero):
        part_sum[-1]()
    squares[...] = jnp.where(x_img == 0, squares[...], 0.0)
    first_end()
    feed_zero[3]()

    told = jnp.where(line == 2, squares[...], told)
    st_all[x_img, column] = told
    mine = st_all.at[x_img, column]
    plane_places = [(x_img, q) for q in plane]
    plane_places += [(lax.rem(x_img + k, m), lax.rem(column + j, columns)) for k in range(1, m) for j in range(columns)]
    copies = []
    for k, (group_at, q) in enumerate(plane_places, 1):
        spot = (k // columns, k % columns)
        device = {**seq_id(q // 2, q % 2, core), "img": group_at}
        copies.append(push(mine, mine, st_send.at[spot], st_recv.at[spot], device))
    for copy in copies:
        copy.start()
    for a in range(len(parts)):
        for k in range(depth - 1):
            gather_z(a, k).wait_send()
        gather_y(a).wait_send()
        gather_core(a).wait_send()
    for copy in copies:
        copy.wait()
    told = jnp.zeros((8, 128), F32)
    for group_at in range(m):
        for q in range(columns):
            told = told + st_all[group_at, q]
    st_core[core] = told
    copy = push(st_core.at[core], st_core.at[core], st_send.at[0, 0], st_recv.at[0, 0], sibling)
    copy.start()
    first_drain()
    feed_zero[4]()
    copy.wait()
    told = st_core[0] + st_core[1]
    count = told[1:2, :1]
    norm = jnp.sqrt(told[2:3, :1]) / count
    factor = jnp.minimum(1.0, CLIP_NORM / norm) / count
    totals[...] = jnp.where(line == 2, norm, jnp.where(line == 3, factor, told))


def adam(master, gradient, first, second):
    first = BETA_ONE * first + (1.0 - BETA_ONE) * gradient
    second = BETA_TWO * second + (1.0 - BETA_TWO) * gradient * gradient
    moved = first / (1.0 - BETA_ONE**STEP) / (jnp.sqrt(second / (1.0 - BETA_TWO**STEP)) + ADAM_EPS)
    return master - LEARN_RATE * (moved + WEIGHT_DECAY * master), first, second


def update_kernel(rows, *refs):
    sums, totals = refs[:2]
    masters, firsts, seconds = refs[2:10], refs[10:18], refs[18:26]
    outs = (refs[26:34], refs[34:42], refs[42:50])
    scalars, turned = refs[50:53], refs[53]
    factor = totals[3:4, :1]
    for k in range(3):
        scalars[k][0, 0] = totals[k, 0]

    def put(index, at, gradient):
        result = adam(masters[index][at], gradient * factor, firsts[index][at], seconds[index][at])
        for k in range(3):
            outs[k][index][at] = result[k]

    base = LAYERS * C_LAYER
    put(0, ..., sums[:, base + C_TOK[0] : base + C_TOK[1]])
    put(1, ..., sums[:, base + C_POS[0] : base + C_POS[0] + POS])
    put(6, ..., sums[:, base + C_HEAD[0] : base + C_HEAD[1]])
    turned[...] = jnp.transpose(sums[:, base + C_POS[0] : base + C_POS[1]])
    for i in range(NORMS):
        put(7, i, turned[POS + 2 * i : POS + 2 * i + 2, :])
    for l in range(LAYERS):
        for index, cols in ((2, C_IN), (3, C_OUT), (4, C_UP), (5, C_DOWN)):
            put(index, l, sums[:, l * C_LAYER + cols[0] : l * C_LAYER + cols[1]])


def turned(tok, pos, w_in, w_out, w_up, w_down, head, norms):
    return (tok.T, pos.T, w_in, w_out, w_up, jnp.swapaxes(w_down, 1, 2), head, norms)


def on_device(geo, pixels, loss_mask, *weights):
    masters, firsts, seconds = (turned(*weights[k : k + 8]) for k in (0, 8, 16))
    n_rows, depth, blocks, res, group = geo.rows, geo.depth, geo.blocks, geo.res, geo.group
    m = geo.m
    vmem = pl.BlockSpec(memory_space=pltpu.VMEM)
    chunk = 12
    batch = 24
    pack = 4
    n_groups = res // 8
    side = 8 * blocks
    sums, totals = pl.pallas_call(
        functools.partial(step_kernel, geo, chunk, batch, pack),
        out_shape=(
            jax.ShapeDtypeStruct((n_rows, C_ALL), F32),
            jax.ShapeDtypeStruct((8, 128), F32),
        ),
        in_specs=[vmem] * 10,
        out_specs=(vmem,) * 2,
        scratch_shapes=[
            pltpu.VMEM((depth, 2, 2, 2 * geo.own, geo.wide), BF),
            pltpu.VMEM((depth, 2, 2, n_rows, C_REST), BF),
            pltpu.VMEM((LAYERS, depth, 2, 2, n_rows, C_LAYER), BF),
            pltpu.VMEM((depth, 2, 2, n_rows, C_REST), F32),
            pltpu.VMEM((2, depth, 2, 2, n_rows, C_LAYER), F32),
            pltpu.VMEM((blocks, res, D), F32),
            pltpu.VMEM((2 * LAYERS, blocks, res, D), BF),
            pltpu.VMEM((blocks, res, 128), F32),
            pltpu.VMEM((blocks + 1, res, 2 * HEAD), F32),
            pltpu.VMEM((LAYERS, blocks, res, HEAD), BF),
            pltpu.VMEM((LAYERS, blocks + 1, group, res, 2 * HEAD), BF),
            pltpu.VMEM((LAYERS, n_groups, side, 3 * HEAD), BF),
            pltpu.VMEM((LAYERS, blocks, res, 2 * STRIDE), BF),
            pltpu.VMEM((LAYERS, n_groups, side, side), BF),
            pltpu.VMEM((LAYERS, blocks, res, D), BF),
            pltpu.VMEM((LAYERS, blocks, res, FF), BF),
            pltpu.VMEM((LAYERS, blocks, res, FF), BF),
            pltpu.VMEM((blocks, res, 3 * HEAD), F32),
            pltpu.VMEM((blocks, res, HEAD), F32),
            pltpu.VMEM((blocks, res, HEAD), BF),
            pltpu.VMEM((blocks, res, HEAD), BF),
            pltpu.VMEM((group - 1, blocks + 1, res, 2 * HEAD), BF),
            pltpu.VMEM((2, group - 1, blocks, res, 2 * HEAD), BF),
            pltpu.VMEM((STRIDE, 2 * HEAD), F32),
            pltpu.VMEM((res, 128), F32),
            pltpu.VMEM((res, 128), F32),
            pltpu.VMEM((res, 128), F32),
            pltpu.VMEM((8, 128), F32),
            pltpu.VMEM((geo.images, 2 * geo.own, 128), F32),
            pltpu.VMEM((2, res, 2 * STRIDE), F32),
            pltpu.VMEM((side, side), F32),
            pltpu.VMEM((16, 1, D), F32),
            pltpu.VMEM((2 * NORMS, 8, D), F32),
            pltpu.VMEM((128, D), F32),
            pltpu.VMEM((8, 128), F32),
            pltpu.VMEM((depth, 2, n_rows, C_ALL), BF),
            pltpu.VMEM((depth, 2, n_rows, C_ALL), BF),
            pltpu.VMEM((2 * depth - 1, n_rows, C_ALL), BF),
            pltpu.VMEM((m, n_rows, C_ALL), BF),
            pltpu.VMEM((m, depth, 2, n_rows, 128 * -(-(C_LAYER - C_OUT[0]) // 128 // m)), BF),
            pltpu.VMEM((m, 2 * depth, n_rows, C_POS[1]), BF),
            pltpu.VMEM((2, 8, 128), F32),
            pltpu.VMEM((m, 2 * depth, 8, 128), F32),
            pltpu.SemaphoreType.DMA((3 + 2 * LAYERS, depth + 1)),
            pltpu.SemaphoreType.DMA((3 + 2 * LAYERS, depth + 1)),
            pltpu.SemaphoreType.DMA((group - 1,)),
            pltpu.SemaphoreType.DMA((2 * LAYERS, group - 1)),
            pltpu.SemaphoreType.DMA((2 * LAYERS + 2, 2 * depth + m)),
            pltpu.SemaphoreType.DMA((2 * LAYERS + 2, 2 * depth + m)),
            pltpu.SemaphoreType.DMA((m,)),
            pltpu.SemaphoreType.DMA((m,)),
            pltpu.SemaphoreType.DMA((m,)),
            pltpu.SemaphoreType.DMA((m,)),
            pltpu.SemaphoreType.DMA((C_POS[1] // 128, 2 * depth)),
            pltpu.SemaphoreType.DMA((C_POS[1] // 128, m, 2 * depth)),
            pltpu.SemaphoreType.DMA((C_POS[1] // 128, m)),
            pltpu.SemaphoreType.DMA((C_POS[1] // 128,)),
            pltpu.SemaphoreType.DMA((m, 2 * depth)),
            pltpu.SemaphoreType.DMA((m, 2 * depth)),
        ],
        compiler_params=pltpu.CompilerParams(
            collective_id=0, has_side_effects=True, vmem_limit_bytes=VMEM_LIMIT
        ),
        name="step",
    )(jnp.swapaxes(pixels, 1, 2), jnp.swapaxes(loss_mask, 1, 2), *masters)

    shapes = [jax.ShapeDtypeStruct(item.shape, F32) for item in masters]
    outs = pl.pallas_call(
        functools.partial(update_kernel, n_rows),
        out_shape=shapes * 3 + [jax.ShapeDtypeStruct((1, 1), F32)] * 3,
        in_specs=[vmem] * 26,
        out_specs=[vmem] * 24 + [pl.BlockSpec(memory_space=pltpu.SMEM)] * 3,
        scratch_shapes=[pltpu.VMEM((128, n_rows), F32)],
        name="update",
    )(sums, totals, *masters, *firsts, *seconds)
    return (
        *(item.reshape(()) for item in outs[24:]),
        *turned(*outs[:8]),
        *turned(*outs[8:16]),
        *turned(*outs[16:24]),
    )


def solution(mesh):
    pixels = P("img", None, "seq")
    weights = (
        P(None, "seq"),
        P(None, "seq"),
        P(None, "seq", None),
        P(None, "seq", None),
        P(None, "seq", None),
        P(None, None, "seq"),
        P("seq", None),
        P(None, None, "seq"),
    )

    def body(pixels, loss_mask, *rest):
        geo = Geometry(mesh.shape["seq"], mesh.shape["img"], pixels.shape[0], pixels.shape[1])
        return on_device(geo, pixels, loss_mask, *rest)

    return jax.shard_map(
        body,
        mesh=mesh,
        in_specs=(pixels, pixels) + weights * 3,
        out_specs=(P(), P(), P()) + weights * 3,
        check_vma=False,
    )
```
